32 devices in a mesh: seg: 16 (over z, x, core), mlp: 2 (over y).
Axes of the slice: x: 2, y: 2, z: 4, core: 2. Of those that a mesh axis runs over, the one named last changes fastest.
Arguments:
- tokens: bfloat16 [32, 1024, 1024], P(('seg', 'mlp')), may hold values from -6 to 6
- initial_state: bfloat16 [32, 512, 1024], P(('seg', 'mlp')), may hold values from -6 to 6
- valid: int32 [32], P(('seg', 'mlp')), may hold values from 513 to 1024, as said below
- token_query_weight: bfloat16 [1024, 1024], P('seg'), may hold values from -0.1875 to 0.1875
- token_key_weight: bfloat16 [1024, 1024], P('seg'), may hold values from -0.1875 to 0.1875
- token_value_weight: bfloat16 [1024, 1024], P('seg'), may hold values from -0.1875 to 0.1875
- token_output_weight: bfloat16 [1024, 1024], P('seg'), may hold values from -3.5 to 3.5
- state_query_weight: bfloat16 [1024, 1024], P('seg'), may hold values from -0.1875 to 0.1875
- state_key_weight: bfloat16 [1024, 1024], P('seg'), may hold values from -0.1875 to 0.1875
- state_value_weight: bfloat16 [1024, 1024], P('seg'), may hold values from -0.1875 to 0.1875
- state_update_weight: bfloat16 [1024, 1024], P('seg'), may hold values from -2.5 to 2.5
- up_projection_weight: bfloat16 [1024, 4096], P('seg', 'mlp'), may hold values from -0.1875 to 0.1875
- down_projection_weight: bfloat16 [1024, 4096], P('seg', 'mlp'), may hold values from -0.09375 to 0.09375
- token_norm_gain: bfloat16 [1024], P('seg'), may hold values from 0.099609375 to 1.8984375
- state_norm_gain: bfloat16 [1024], P('seg'), may hold values from 0.099609375 to 1.8984375
- feedforward_norm_gain: bfloat16 [1024], P('seg'), may hold values from 0.099609375 to 1.8984375
- state_gate_bias: bfloat16 [1024], P('seg'), may hold values from -3 to 3
- output_cotangent: bfloat16 [32, 1024, 1024], P(('seg', 'mlp')), may hold values from -6 to 6
- final_state_cotangent: bfloat16 [32, 512, 1024], P(('seg', 'mlp')), may hold values from -6 to 6
Outputs:
- out: bfloat16 [32, 1024, 1024], P(('seg', 'mlp'))
- final_state: bfloat16 [32, 512, 1024], P(('seg', 'mlp'))
- grad_tokens: float32 [32, 1024, 1024], P(('seg', 'mlp'))
- grad_state: float32 [32, 512, 1024], P(('seg', 'mlp'))
- grad_w_query: float32 [1024, 1024], P('seg')
- grad_w_key: float32 [1024, 1024], P('seg')
- grad_w_value: float32 [1024, 1024], P('seg')
- grad_w_out: float32 [1024, 1024], P('seg')
- grad_w_squery: float32 [1024, 1024], P('seg')
- grad_w_skey: float32 [1024, 1024], P('seg')
- grad_w_svalue: float32 [1024, 1024], P('seg')
- grad_w_sout: float32 [1024, 1024], P('seg')
- grad_w_up: float32 [1024, 4096], P('seg', 'mlp')
- grad_w_down: float32 [1024, 4096], P('seg', 'mlp')
- grad_gain_attn: float32 [1024], P('seg')
- grad_gain_state: float32 [1024], P('seg')
- grad_gain_mlp: float32 [1024], P('seg')
- grad_gate_bias: float32 [1024], P('seg')
The draws below stay inside these ranges and needn't reach their ends.
Inputs may be any that keep to these rules, and one draw needn't show every extreme that they name: More than 512 valid tokens in each segment, so only its last block has masked positions; in every draw some segment has all 1024 tokens valid.
All inputs are finite; a program needn't handle non-finite values.
Results may differ from the reference program's by a relative error of at most 0.022.
Values may be sent and summed in bfloat16 or wider, within the bound.
A program may use at most 448 MiB of HBM per device.

```python
import jax
import jax.numpy as jnp
from jax import lax

MODEL_WIDTH = 1024
HEADS = 8
HEAD = 128
FF = 4096
BLOCK = 512
NSTATE = 512
NBLK = 2
SEG_LEN = 1024
SEGS = 32


def draw_valid(key, part):
    key = jax.random.fold_in(key, 11)
    key_counts, key_full = jax.random.split(key)
    counts = jax.random.randint(key_counts, (SEGS,), SEG_LEN - BLOCK + 1, SEG_LEN + 1)
    full_index = jax.random.randint(key_full, (), 0, SEGS)
    return jnp.where(jnp.arange(SEGS) == full_index, SEG_LEN, counts).astype(jnp.int32)


def block_levels(rng, shape, shards, smallest, top_value):
    def one(position, blocks):
        draws = jax.random.uniform(jax.random.fold_in(jax.random.fold_in(rng, 6), position), (blocks,), jnp.float32, smallest / len(shards), top_value / len(shards))
        return jnp.repeat(jnp.exp(draws), shape[position] // blocks).reshape((-1,) + (1,) * (len(shape) - position - 1))

    factor_of = one(*shards[0])
    for cut in shards[1:]:
        factor_of = factor_of * one(*cut)
    return factor_of


def normal_values(rng, dims, scale, reach, cuts=(), kind=jnp.bfloat16):
    loudness = block_levels(rng, dims, cuts, -0.22, 0.18) if cuts else 1.0
    values = jax.random.normal(rng, dims, jnp.float32) * scale * loudness
    return jnp.minimum(jnp.maximum(values, -reach), reach).astype(kind)


def setup_inputs(seed: int = 0) -> dict:
    splits = jax.random.split(jax.random.key(seed), 20)
    tokens = normal_values(splits[0], (SEGS, SEG_LEN, MODEL_WIDTH), 1.0, 6.0, ((0, 32),))
    initial_state = normal_values(splits[1], (SEGS, NSTATE, MODEL_WIDTH), 1.0, 6.0, ((0, 32),))
    valid = draw_valid(jax.random.fold_in(splits[19], 71), 0)
    token_query_weight = normal_values(splits[3], (MODEL_WIDTH, MODEL_WIDTH), MODEL_WIDTH ** -0.5, 0.1875, ((0, 16),))
    token_key_weight = normal_values(splits[4], (MODEL_WIDTH, MODEL_WIDTH), MODEL_WIDTH ** -0.5, 0.1875, ((0, 16),))
    token_value_weight = normal_values(splits[5], (MODEL_WIDTH, MODEL_WIDTH), MODEL_WIDTH ** -0.5, 0.1875, ((0, 16),))
    token_output_weight = normal_values(splits[6], (MODEL_WIDTH, MODEL_WIDTH), (MODEL_WIDTH * 3 // (BLOCK + NSTATE)) ** -0.5, 3.5, ((0, 16),))
    state_query_weight = normal_values(splits[7], (MODEL_WIDTH, MODEL_WIDTH), MODEL_WIDTH ** -0.5, 0.1875, ((0, 16),))
    state_key_weight = normal_values(splits[8], (MODEL_WIDTH, MODEL_WIDTH), MODEL_WIDTH ** -0.5, 0.1875, ((0, 16),))
    state_value_weight = normal_values(splits[9], (MODEL_WIDTH, MODEL_WIDTH), MODEL_WIDTH ** -0.5, 0.1875, ((0, 16),))
    state_update_weight = normal_values(splits[10], (MODEL_WIDTH, MODEL_WIDTH), (MODEL_WIDTH * 3 // BLOCK) ** -0.5, 2.5, ((0, 16),))
    up_projection_weight = normal_values(splits[11], (MODEL_WIDTH, FF), MODEL_WIDTH ** -0.5, 0.1875, ((0, 16), (1, 2)))
    down_projection_weight = normal_values(splits[12], (MODEL_WIDTH, FF), FF ** -0.5, 0.09375, ((0, 16), (1, 2)))
    token_norm_gain = jnp.clip(1.0 + 0.18 * jax.random.normal(splits[13], (MODEL_WIDTH,), jnp.float32), 0.099609375, 1.8984375).astype(jnp.bfloat16)
    state_norm_gain = jnp.clip(1.0 + 0.18 * jax.random.normal(splits[14], (MODEL_WIDTH,), jnp.float32), 0.099609375, 1.8984375).astype(jnp.bfloat16)
    feedforward_norm_gain = jnp.clip(1.0 + 0.18 * jax.random.normal(splits[15], (MODEL_WIDTH,), jnp.float32), 0.099609375, 1.8984375).astype(jnp.bfloat16)
    state_gate_bias = jnp.clip(jax.random.uniform(splits[16], (MODEL_WIDTH,), jnp.float32, -3.0, 3.0) * block_levels(splits[16], (MODEL_WIDTH,), ((0, 16),), -0.4, 0.0), -3.0, 3.0).astype(jnp.bfloat16)
    output_cotangent = normal_values(splits[17], (SEGS, SEG_LEN, MODEL_WIDTH), 1.0, 6.0, ((0, 32),))
    final_state_cotangent = normal_values(splits[18], (SEGS, NSTATE, MODEL_WIDTH), 1.0, 6.0, ((0, 32),))
    return dict(tokens=tokens, initial_state=initial_state, valid=valid, token_query_weight=token_query_weight, token_key_weight=token_key_weight, token_value_weight=token_value_weight, token_output_weight=token_output_weight, state_query_weight=state_query_weight, state_key_weight=state_key_weight, state_value_weight=state_value_weight, state_update_weight=state_update_weight, up_projection_weight=up_projection_weight, down_projection_weight=down_projection_weight, token_norm_gain=token_norm_gain, state_norm_gain=state_norm_gain, feedforward_norm_gain=feedforward_norm_gain, state_gate_bias=state_gate_bias, output_cotangent=output_cotangent, final_state_cotangent=final_state_cotangent)


EPS = 1e-06
NEGATIVE = -1e+30
GELU_C = 0.7978845608
GELU_K = 0.044715

@jax.custom_vjp
def low(v):
    return lax.optimization_barrier(v.astype(jnp.bfloat16)).astype(jnp.float32)

@jax.custom_vjp
def low_back(v):
    return v

def low_keep(v):
    return (low(v), None)

def low_pass(kept, grad):
    return (grad,)

def back_keep(v):
    return (v, None)

def back_low(kept, grad):
    return (low(grad),)
low.defvjp(low_keep, low_pass)
low_back.defvjp(back_keep, back_low)

def rms_norm(values, gain):
    return values * lax.rsqrt(lax.optimization_barrier(jnp.mean(values * values, axis=-1, keepdims=True)) + EPS) * gain

def round_operands(values):
    return low(low_back(values))

def precise_product(left, right):
    return jnp.dot(left, right, precision=lax.Precision.HIGHEST)

def gelu_tanh(values):
    return 0.5 * values * (1.0 + jnp.tanh(GELU_C * (values + GELU_K * values * values * values)))

def split_heads(values):
    return values.reshape(values.shape[0], HEADS, HEAD)

def attend(query_rows, key_rows, value_rows, allowed):
    scores = jnp.einsum('qhd,khd->hqk', split_heads(query_rows), split_heads(key_rows), precision=lax.Precision.HIGHEST) * HEAD ** (-0.5)
    scores = jnp.where(allowed[None], low_back(scores), NEGATIVE)
    shifted = scores - lax.optimization_barrier(jnp.max(scores, axis=-1, keepdims=True))
    weights = jnp.exp(shifted)
    probs = low(weights / lax.optimization_barrier(jnp.sum(weights, axis=-1, keepdims=True)))
    mixed_out = jnp.einsum('hqk,khd->qhd', probs, split_heads(value_rows), precision=lax.Precision.HIGHEST)
    return round_operands(mixed_out.reshape(query_rows.shape[0], MODEL_WIDTH))

def segment_forward(layer_parameters, seg_tokens, seg_state, valid_count):
    token_query_weight, token_key_weight, token_value_weight, token_output_weight, state_query_weight, state_key_weight, state_value_weight, state_update_weight, up_projection_weight, down_projection_weight, token_norm_gain, state_norm_gain, feedforward_norm_gain, state_gate_bias = layer_parameters
    gate_open = 1.0 / (1.0 + jnp.exp(-state_gate_bias))

    def block_step(state_carry, inputs):
        state_now, key_prev, value_prev = state_carry
        block_x, block_index = inputs
        row_ids = block_index * BLOCK + jnp.arange(BLOCK, dtype=jnp.int32)
        col_ids = jnp.concatenate([row_ids - BLOCK, row_ids])
        near_ok = (col_ids[None, :] <= row_ids[:, None]) & (col_ids[None, :] > row_ids[:, None] - BLOCK) & (col_ids[None, :] >= 0) & (col_ids[None, :] < valid_count)
        allowed = jnp.concatenate([near_ok, jnp.ones((BLOCK, NSTATE), dtype=jnp.bool_)], axis=1)
        normed = low(rms_norm(block_x, token_norm_gain))
        query_tok = round_operands(precise_product(normed, token_query_weight))
        key_tok = round_operands(precise_product(normed, token_key_weight))
        value_tok = round_operands(precise_product(normed, token_value_weight))
        normalized_state = low(rms_norm(state_now, state_norm_gain))
        state_query = round_operands(precise_product(normalized_state, state_query_weight))
        state_key_rows = round_operands(precise_product(normalized_state, state_key_weight))
        state_value = round_operands(precise_product(normalized_state, state_value_weight))
        key_all = jnp.concatenate([key_prev, key_tok, state_key_rows], axis=0)
        value_all = jnp.concatenate([value_prev, value_tok, state_value], axis=0)
        mixed_out = attend(query_tok, key_all, value_all, allowed)
        resid = block_x + low_back(precise_product(mixed_out, token_output_weight))
        ynorm = low(rms_norm(resid, feedforward_norm_gain))
        up_act = low_back(precise_product(ynorm, up_projection_weight))
        hidden = low(gelu_tanh(up_act))
        out_block = resid + low_back(precise_product(hidden, down_projection_weight.T))
        seen = jnp.broadcast_to((row_ids < valid_count)[None, :], (NSTATE, BLOCK))
        state_read = attend(state_query, key_tok, value_tok, seen)
        update = low_back(precise_product(state_read, state_update_weight))
        next_state = gate_open * state_now + (1.0 - gate_open) * update
        return ((next_state, key_tok, value_tok), out_block)
    blocks = seg_tokens.reshape(NBLK, BLOCK, MODEL_WIDTH)
    zero_block = jnp.zeros((BLOCK, MODEL_WIDTH), seg_tokens.dtype)
    (last_state, key_last, value_last), out_rows = lax.scan(jax.checkpoint(block_step), (seg_state, zero_block, zero_block), (blocks, jnp.arange(NBLK, dtype=jnp.int32)))
    return (out_rows.reshape(SEG_LEN, MODEL_WIDTH), last_state)

def reference(tokens, initial_state, valid, token_query_weight, token_key_weight, token_value_weight, token_output_weight, state_query_weight, state_key_weight, state_value_weight, state_update_weight, up_projection_weight, down_projection_weight, token_norm_gain, state_norm_gain, feedforward_norm_gain, state_gate_bias, output_cotangent, final_state_cotangent):
    layer_parameters = tuple((weight_matrix.astype(jnp.float32) for weight_matrix in (token_query_weight, token_key_weight, token_value_weight, token_output_weight, state_query_weight, state_key_weight, state_value_weight, state_update_weight, up_projection_weight, down_projection_weight, token_norm_gain, state_norm_gain, feedforward_norm_gain, state_gate_bias)))

    def per_segment(totals, inputs):
        seg_tokens, seg_state, valid_count, seg_cot, seg_scot = inputs

        def forward_fn(params_in, tokens_in, state_in):
            return segment_forward(params_in, tokens_in, state_in, valid_count)
        (out_rows, last_state), pullback = jax.vjp(forward_fn, layer_parameters, seg_tokens.astype(jnp.float32), seg_state.astype(jnp.float32))
        keep_rows = (jnp.arange(SEG_LEN, dtype=jnp.int32) < valid_count).astype(jnp.float32)[:, None]
        grad_params, grad_tok, grad_st = pullback((seg_cot.astype(jnp.float32) * keep_rows, seg_scot.astype(jnp.float32)))
        totals = tuple((total_one + grad_one for total_one, grad_one in zip(totals, grad_params)))
        return (totals, (out_rows.astype(jnp.bfloat16), last_state.astype(jnp.bfloat16), grad_tok, grad_st))
    start_totals = tuple((jnp.zeros_like(param_one) for param_one in layer_parameters))
    totals, (out_all, final_all, grad_tok_all, grad_st_all) = lax.scan(per_segment, start_totals, (tokens, initial_state, valid, output_cotangent, final_state_cotangent))
    return (out_all, final_all, grad_tok_all, grad_st_all, totals[0], totals[1], totals[2], totals[3], totals[4], totals[5], totals[6], totals[7], totals[8], totals[9], totals[10], totals[11], totals[12], totals[13])
```

```python
import functools
import jax
import jax.numpy as jnp
from jax import lax
from jax.experimental import pallas as pl
from jax.experimental.pallas import tpu as pltpu
from jax.sharding import PartitionSpec as P

MESH = pl.DeviceIdType.MESH


class Place:
    def __init__(self, seg_size, mlp_size):
        seg = lax.axis_index("seg")
        self.sizes = {"z": seg_size // 4, "x": 2, "c": 2, "m": mlp_size}
        self.at = {
            "z": lax.div(seg, 4),
            "x": lax.rem(lax.div(seg, 2), 2),
            "c": lax.rem(seg, 2),
            "m": lax.axis_index("mlp"),
        }

    def device(self, **moved):
        at = {**self.at, **moved}
        return (at["z"] * 4 + at["x"] * 2 + at["c"], at["m"])

    def ahead(self, axis, step):
        return lax.rem(self.at[axis] + step, self.sizes[axis])

    def behind(self, axis, step):
        return lax.rem(self.at[axis] + self.sizes[axis] - step, self.sizes[axis])

    def greet(self):
        barrier = pltpu.get_barrier_semaphore()

        def signal(**moved):
            pl.semaphore_signal(
                barrier, inc=1, device_id=self.device(**moved), device_id_type=MESH
            )

        z, last = self.at["z"], self.sizes["z"] - 1
        count = 0
        for axis in "xcm":
            for step in range(1, self.sizes[axis]):
                signal(**{axis: self.ahead(axis, step)})
                count += 1

        @pl.when(z > 0)
        def _():
            signal(z=z - 1)

        @pl.when(z < last)
        def _():
            signal(z=z + 1)

        count = count + lax.min(z, 1) + lax.min(last - z, 1)
        pl.semaphore_wait(barrier, count)


class Wires:
    def __init__(self, place, send, recv):
        self.place, self.send, self.recv, self.used = place, send, recv, 0

    def copy(self, src, dst, pair, moved):
        return pltpu.make_async_remote_copy(
            src_ref=src,
            dst_ref=dst,
            send_sem=self.send.at[pair],
            recv_sem=self.recv.at[pair],
            device_id=self.place.device(**moved),
            device_id_type=MESH,
        )


def guarded(condition, action):
    if condition is None:
        action()
    else:
        pl.when(condition)(action)


class Flow:
    def __init__(self, wires):
        self.wires, self.arriving, self.sent = wires, [], []

    def move(self, src, dst, moved, landing, goes=None, comes=None):
        pair = self.wires.used
        self.wires.used += 1
        out = lambda: self.wires.copy(src, dst, pair, moved)
        guarded(goes, lambda: out().start())
        self.sent.append((goes, lambda: out().wait_send()))
        self.arriving.append(
            (comes, lambda: self.wires.copy(landing, landing, pair, moved).wait_recv())
        )

    def arrive(self):
        for condition, wait in self.arriving:
            guarded(condition, wait)
        self.arriving.clear()

    def finish(self):
        self.arrive()
        for condition, wait in self.sent:
            guarded(condition, wait)
        self.sent.clear()


def gather(wires, source, target, order, local_sem):
    place, flow = wires.place, Flow(wires)
    axes = ("m" if len(target.shape) == 6 else "") + "zxc"
    at, sizes, done = place.at, place.sizes, set()

    def view(**moved):
        index = [
            moved[a] if a in moved else pl.ds(0, sizes[a]) if a in done else at[a] for a in axes
        ]
        return target.at[tuple(index)]

    own = pltpu.make_async_copy(source, view(), local_sem)
    own.start()
    first = True
    z, last = at["z"], sizes["z"] - 1
    for axis in order + "c":
        if axis == "z":
            for t in range(last):
                flow.arrive()
                below, above = lax.max(z - t, 0), lax.min(z + t, last)
                flow.move(
                    source if first and t == 0 else view(z=below),
                    view(z=below),
                    dict(z=z + 1),
                    view(z=lax.max(z - 1 - t, 0)),
                    (z >= t) & (z < last),
                    z >= t + 1,
                )
                flow.move(
                    source if first and t == 0 else view(z=above),
                    view(z=above),
                    dict(z=z - 1),
                    view(z=lax.min(z + 1 + t, last)),
                    (z + t <= last) & (z > 0),
                    z + 1 + t <= last,
                )
                yield
        else:
            flow.arrive()
            for step in range(1, sizes[axis]):
                flow.move(
                    source if first else view(),
                    view(),
                    {axis: place.ahead(axis, step)},
                    view(**{axis: place.behind(axis, step)}),
                )
            yield
        done.add(axis)
        if first:
            own.wait()
            first = False
    flow.finish()


def add_into(total, term, chunks):
    def body(i, carry):
        total[i] = (total[i].astype(jnp.float32) + term[i].astype(jnp.float32)).astype(total.dtype)
        return carry

    lax.fori_loop(0, chunks, body, 0)


def flat_add(total, term):
    lead = total.shape[:-2]
    n = 1
    for d in lead:
        n *= d
    def body(i, carry):
        idx, rest = [], i
        for d in reversed(lead):
            idx.append(lax.rem(rest, d)); rest = lax.div(rest, d)
        idx = tuple(reversed(idx))
        total[idx] = (total[idx].astype(jnp.float32) + term[idx].astype(jnp.float32)).astype(total.dtype)
        return carry
    lax.fori_loop(0, n, body, 0)


def scatter(wires, grad, result, own, core_in, m_in, x_in, up_in, down_in, order, local_sem):
    place, flow = wires.place, Flow(wires)
    split_m = len(grad.shape) == 6
    axes = ("m" if split_m else "") + "zx"
    at, sizes, done = place.at, place.sizes, set()
    z, last = at["z"], sizes["z"] - 1
    lead = (slice(None),) * len(axes)
    full = tuple(pl.ds(0, sizes[a]) for a in axes)

    def view(ref, **moved):
        index = [
            moved[a] if a in moved else at[a] if a in done else pl.ds(0, sizes[a]) for a in axes
        ]
        return ref.at[tuple(index)]

    load = pltpu.make_async_copy(grad.at[full + (at["c"],)], own, local_sem)
    load.start()
    flow.move(grad.at[full + (1 - at["c"],)], core_in, dict(c=1 - at["c"]), core_in)
    yield
    load.wait()
    flow.arrive()
    flat_add(own, core_in)
    for axis in order:
        if axis == "x":
            flow.move(view(own, x=1 - at["x"]), x_in, dict(x=1 - at["x"]), x_in)
            yield
            flow.arrive()
            done.add("x")
            flat_add(view(own), x_in)
        elif axis == "m":
            for step in range(1, sizes["m"]):
                flow.move(
                    view(own, m=place.ahead("m", step)), m_in.at[step - 1],
                    dict(m=place.ahead("m", step)), m_in.at[step - 1],
                )
            yield
            flow.arrive()
            done.add("m")
            for step in range(1, sizes["m"]):
                flat_add(view(own), m_in.at[step - 1])
        else:
            for t in range(last):
                up, down = lax.min(last - t + z, last), lax.max(z - last + t, 0)
                flow.move(view(own, z=up), up_in.at[t], dict(z=z + 1), up_in.at[t],
                          (z <= t) & (z < last), (z >= 1) & (z - 1 <= t))
                flow.move(view(own, z=down), down_in.at[t], dict(z=z - 1), down_in.at[t],
                          (last - z <= t) & (z > 0), (z < last) & (last - z - 1 <= t))
                yield
                flow.arrive()
                up, down = lax.min(last - 1 - t + z, last), lax.max(z - last + t + 1, 0)
                pl.when((z >= 1) & (z - 1 <= t))(lambda: flat_add(view(own, z=up), up_in.at[t]))
                pl.when((z < last) & (last - z - 1 <= t))(lambda: flat_add(view(own, z=down), down_in.at[t]))
            done.add("z")
    if split_m:
        result[...] = view(own)[...].astype(jnp.float32)
    else:
        slot = m_in.at[at["m"]]
        slot[...] = view(own)[...]
        for step in range(1, sizes["m"]):
            flow.move(slot, slot, dict(m=place.ahead("m", step)), m_in.at[place.behind("m", step)])
        yield
        flow.arrive()
        total = m_in[0].astype(jnp.float32)
        for i in range(1, sizes["m"]):
            total = total + m_in[i].astype(jnp.float32)
        result[...] = total
    flow.finish()


def run_rounds(flows):
    live, waiting = [], list(flows)
    while live or waiting:
        if waiting:
            live.append(waiting.pop(0))
        live = [f for f in live if next(f, StopIteration) is not StopIteration]


def lead_shape(order, split_m, done, sizes):
    axes = ("m" if split_m else "") + "zx"
    return tuple(sizes[a] for a in axes if a not in done)


def gather_call(sources, orders, seg_size, mlp_size, name, collective_id):
    count = len(sources)
    sizes = {"z": seg_size // 4, "x": 2, "c": 2, "m": mlp_size}

    def kernel(*refs):
        ins, outs = refs[:count], refs[count : 2 * count]
        send, recv, local = refs[2 * count :]
        place = Place(seg_size, mlp_size)
        place.greet()
        wires = Wires(place, send, recv)
        run_rounds(
            [gather(wires, ins[i], outs[i], orders[i], local.at[i]) for i in range(count)]
        )

    shapes = [
        jax.ShapeDtypeStruct(
            ((mlp_size,) if "m" in order else ()) + (sizes["z"], 2, 2) + source.shape, source.dtype
        )
        for source, order in zip(sources, orders)
    ]
    pairs = sum(2 * (sizes["z"] - 1) + 2 + ("m" in order) * (mlp_size - 1) for order in orders)
    anywhere = pl.BlockSpec(memory_space=pl.ANY)
    return pl.pallas_call(
        kernel,
        out_shape=shapes,
        in_specs=[anywhere] * count,
        out_specs=[anywhere] * count,
        scratch_shapes=[
            pltpu.SemaphoreType.DMA((pairs,)),
            pltpu.SemaphoreType.DMA((pairs,)),
            pltpu.SemaphoreType.DMA((count,)),
        ],
        compiler_params=pltpu.CompilerParams(collective_id=collective_id, has_side_effects=True),
        name=name,
    )(*sources)


def scatter_buffers(grad, order, sizes):
    split_m = grad.ndim == 6
    rows = grad.shape[-2:]

    def left(axis):
        done = order[: order.index(axis) + 1]
        return lead_shape(order, split_m, done, sizes) + rows

    return [
        pltpu.VMEM(shape, grad.dtype)
        for shape in (
            lead_shape(order, split_m, "", sizes) + rows,
            lead_shape(order, split_m, "", sizes) + rows,
            (sizes["m"] - 1,) + left("m") if split_m else (sizes["m"],) + rows,
            left("x"),
            (sizes["z"] - 1,) + left("z"),
            (sizes["z"] - 1,) + left("z"),
        )
    ]


def scatter_call(grads, orders, seg_size, mlp_size, name, collective_id):
    count = len(grads)
    sizes = {"z": seg_size // 4, "x": 2, "c": 2, "m": mlp_size}

    def kernel(*refs):
        ins, outs = refs[:count], refs[count : 2 * count]
        buffers = refs[2 * count : -3]
        send, recv, local = refs[-3:]
        place = Place(seg_size, mlp_size)
        place.greet()
        wires = Wires(place, send, recv)
        run_rounds(
            [
                scatter(
                    wires, ins[i], outs[i], *buffers[6 * i : 6 * i + 6], orders[i], local.at[i]
                )
                for i in range(count)
            ]
        )

    buffers = []
    for grad, order in zip(grads, orders):
        buffers += scatter_buffers(grad, order, sizes)
    pairs = sum(2 * (sizes["z"] - 1) + 2 + (mlp_size - 1) for order in orders)
    return pl.pallas_call(
        kernel,
        out_shape=[jax.ShapeDtypeStruct(grad.shape[-2:], jnp.float32) for grad in grads],
        in_specs=[pl.BlockSpec(memory_space=pl.ANY)] * count,
        out_specs=[pl.BlockSpec(memory_space=pltpu.VMEM)] * count,
        scratch_shapes=buffers
        + [
            pltpu.SemaphoreType.DMA((pairs,)),
            pltpu.SemaphoreType.DMA((pairs,)),
            pltpu.SemaphoreType.DMA((count,)),
        ],
        compiler_params=pltpu.CompilerParams(
            collective_id=collective_id, has_side_effects=True, vmem_limit_bytes=56 << 20
        ),
        name=name,
    )(*grads)


HEADS = 8
HEAD = 128
BLOCK = 512


EPS = 1e-06
NEGATIVE = -1e30
GELU_C = 0.7978845608
GELU_K = 0.044715


def rms_norm(values, gain):
    return values * lax.rsqrt(jnp.mean(values * values, axis=-1, keepdims=True) + EPS) * gain


def gelu_tanh(values):
    return 0.5 * values * (1.0 + jnp.tanh(GELU_C * (values + GELU_K * values * values * values)))


def matmul(left, right):
    return jnp.dot(left, right, preferred_element_type=jnp.float32)


def matmul_tn(left, right):
    return lax.dot_general(
        left, right, (((0,), (0,)), ((), ())), preferred_element_type=jnp.float32
    )


def matmul_nt(left, right):
    return lax.dot_general(
        left, right, (((1,), (1,)), ((), ())), preferred_element_type=jnp.float32
    )


def split_heads(values):
    return values.reshape(values.shape[0], HEADS, HEAD)


def score_block(query_rows, key_rows, allowed):
    scores = jnp.einsum(
        "qhd,khd->hqk",
        split_heads(query_rows),
        split_heads(key_rows),
        preferred_element_type=jnp.float32,
    ) * HEAD ** (-0.5)
    return jnp.where(allowed[None], scores, NEGATIVE)


def attend_forward(query_rows, key_rows, value_rows, allowed):
    scores = score_block(query_rows, key_rows, allowed)
    row_max = jnp.max(scores, axis=-1, keepdims=True)
    weights = jnp.exp(scores - row_max)
    row_total = jnp.sum(weights, axis=-1, keepdims=True)
    probs = (weights / row_total).astype(jnp.bfloat16)
    mixed_out = jnp.einsum(
        "hqk,khd->qhd", probs, split_heads(value_rows), preferred_element_type=jnp.float32
    )
    log_total = (row_max + jnp.log(row_total))[..., 0]
    return (mixed_out.reshape(query_rows.shape[0], -1).astype(jnp.bfloat16), log_total)


def attend_backward(query_rows, key_rows, value_rows, allowed, log_total, grad_mixed):
    score_scale = HEAD ** (-0.5)
    scores = score_block(query_rows, key_rows, allowed)
    probs = jnp.exp(scores - log_total[..., None])
    grad_heads = split_heads(grad_mixed)
    grad_values = jnp.einsum(
        "hqk,qhd->khd", probs.astype(jnp.bfloat16), grad_heads, preferred_element_type=jnp.float32
    )
    grad_probs = jnp.einsum(
        "qhd,khd->hqk", grad_heads, split_heads(value_rows), preferred_element_type=jnp.float32
    )
    grad_scores = (
        probs * (grad_probs - jnp.sum(grad_probs * probs, axis=-1, keepdims=True))
    ).astype(jnp.bfloat16)
    grad_query = (
        jnp.einsum(
            "hqk,khd->qhd", grad_scores, split_heads(key_rows), preferred_element_type=jnp.float32
        )
        * score_scale
    )
    grad_keys = (
        jnp.einsum(
            "hqk,qhd->khd", grad_scores, split_heads(query_rows), preferred_element_type=jnp.float32
        )
        * score_scale
    )
    query_count = query_rows.shape[0]
    key_count = key_rows.shape[0]
    return (
        grad_query.reshape(query_count, -1),
        grad_keys.reshape(key_count, -1),
        grad_values.reshape(key_count, -1),
    )


def shards(
    mlp_size,
    tokens,
    initial_state,
    valid,
    token_query_weight,
    token_key_weight,
    token_value_weight,
    token_output_weight,
    state_query_weight,
    state_key_weight,
    state_value_weight,
    state_update_weight,
    up_projection_weight,
    down_projection_weight,
    token_norm_gain,
    state_norm_gain,
    feedforward_norm_gain,
    state_gate_bias,
    output_cotangent,
    final_state_cotangent,
):
    rows = token_query_weight.shape[0]
    width = tokens.shape[2]
    seg_size = width // rows
    part = up_projection_weight.shape[1]
    half = part // 2
    small = jnp.concatenate(
        [token_norm_gain, state_norm_gain, feedforward_norm_gain, state_gate_bias]
    ).reshape(-1, 128)
    small = jnp.pad(small, ((0, 16 - small.shape[0]), (0, 0)))
    sources = [
        token_query_weight,
        token_key_weight,
        token_value_weight,
        small,
        state_query_weight,
        state_key_weight,
        state_value_weight,
        token_output_weight,
        state_update_weight,
        up_projection_weight[:, :half],
        down_projection_weight[:, :half],
        up_projection_weight[:, half:],
        down_projection_weight[:, half:],
    ]
    gathered = gather_call(
        sources, ["zx"] * 9 + ["zxm"] * 4, seg_size, mlp_size, "gather_weights", 1
    )
    (
        query_full,
        key_full,
        value_full,
        small_all,
        state_query_matrix,
        state_key_matrix,
        state_value_matrix,
        out_full,
        sout_full,
    ) = gathered[:9]
    query_full, key_full, value_full, out_full, sout_full = [
        w.reshape(width, width) for w in (query_full, key_full, value_full, out_full, sout_full)
    ]
    state_query_matrix, state_key_matrix, state_value_matrix = [
        w.reshape(width, width) for w in (state_query_matrix, state_key_matrix, state_value_matrix)
    ]
    ups, downs = [
        [pair[m].reshape(width, half) for pair in pairs for m in range(mlp_size)]
        for pairs in ((gathered[9], gathered[11]), (gathered[10], gathered[12]))
    ]
    small_rows = small_all.reshape(seg_size, -1)[:, : 4 * rows].reshape(seg_size, 4, rows)
    small_rows = small_rows.transpose(1, 0, 2).reshape(4, width).astype(jnp.float32)
    attn_gain, state_gain, mlp_gain, gate_bias = small_rows
    gate_open = 1.0 / (1.0 + jnp.exp(-gate_bias))
    token_proj = jnp.concatenate([query_full, key_full, value_full], axis=1)
    state_projection = jnp.concatenate(
        [state_query_matrix, state_key_matrix, state_value_matrix], axis=1
    )
    seg_tokens = tokens[0].astype(jnp.float32)
    seq_len = seg_tokens.shape[0]
    feature_width = seg_tokens.shape[1]
    block_count = seq_len // BLOCK
    state_rows = initial_state.shape[1]
    valid_count = valid[0]
    block_ids = jnp.arange(block_count, dtype=jnp.int32)
    zero_block = jnp.zeros((BLOCK, feature_width), jnp.bfloat16)

    def masks_for(block_index):
        row_ids = block_index * BLOCK + jnp.arange(BLOCK, dtype=jnp.int32)
        col_ids = jnp.concatenate([row_ids - BLOCK, row_ids])
        near_ok = (
            (col_ids[None, :] <= row_ids[:, None])
            & (col_ids[None, :] > row_ids[:, None] - BLOCK)
            & (col_ids[None, :] >= 0)
            & (col_ids[None, :] < valid_count)
        )
        allowed = jnp.concatenate([near_ok, jnp.ones((BLOCK, state_rows), dtype=jnp.bool_)], axis=1)
        seen = jnp.broadcast_to((row_ids < valid_count)[None, :], (state_rows, BLOCK))
        return (allowed, seen)

    def forward_step(state_carry, inputs):
        state_now, key_prev, value_prev = state_carry
        block_x, block_index = inputs
        allowed, seen = masks_for(block_index)
        normed = rms_norm(block_x, attn_gain).astype(jnp.bfloat16)
        token_qkv = matmul(normed, token_proj).astype(jnp.bfloat16)
        query_tok = token_qkv[:, :feature_width]
        key_tok = token_qkv[:, feature_width : 2 * feature_width]
        value_tok = token_qkv[:, 2 * feature_width :]
        normalized_state = rms_norm(state_now, state_gain).astype(jnp.bfloat16)
        state_qkv = matmul(normalized_state, state_projection).astype(jnp.bfloat16)
        key_all = jnp.concatenate(
            [key_prev, key_tok, state_qkv[:, feature_width : 2 * feature_width]], axis=0
        )
        value_all = jnp.concatenate(
            [value_prev, value_tok, state_qkv[:, 2 * feature_width :]], axis=0
        )
        mixed_out, log_total = attend_forward(query_tok, key_all, value_all, allowed)
        resid = block_x + matmul(mixed_out, out_full)
        state_read, state_log = attend_forward(
            state_qkv[:, :feature_width], key_tok, value_tok, seen
        )
        update = matmul(state_read, sout_full)
        next_state = gate_open * state_now + (1.0 - gate_open) * update
        kept_block = (
            normed,
            token_qkv,
            normalized_state,
            state_qkv,
            mixed_out,
            log_total,
            state_read,
            state_log,
            update,
            resid,
            state_now,
        )
        return ((next_state, key_tok, value_tok), kept_block)

    state_start = initial_state[0].astype(jnp.float32)
    (last_state, key_last, value_last), kept_all = lax.scan(
        forward_step,
        (state_start, zero_block, zero_block),
        (seg_tokens.reshape(block_count, BLOCK, feature_width), block_ids),
    )
    (
        normed_all,
        token_qkv_all,
        state_normed_all,
        state_qkv_all,
        mixed_all,
        log_all,
        read_all,
        read_log_all,
        update_all,
        resid_all,
        states_all,
    ) = kept_all
    resid_rows = resid_all.reshape(seq_len, feature_width)
    ynorm = rms_norm(resid_rows, mlp_gain).astype(jnp.bfloat16)
    keep_rows = (jnp.arange(seq_len, dtype=jnp.int32) < valid_count).astype(jnp.float32)[:, None]
    grad_out = output_cotangent[0].astype(jnp.float32) * keep_rows
    grad_branch = grad_out.astype(jnp.bfloat16)
    out_rows = resid_rows
    grad_ynorm = jnp.zeros_like(resid_rows)
    up_grads, down_grads = [], []
    for up_part, down_part in zip(ups, downs):
        up_act = matmul(ynorm, up_part)
        hidden = gelu_tanh(up_act).astype(jnp.bfloat16)
        out_rows = out_rows + matmul_nt(hidden, down_part)
        grad_hidden = matmul(grad_branch, down_part)
        grad_up = jax.vjp(gelu_tanh, up_act)[1](grad_hidden)[0].astype(jnp.bfloat16)
        down_grads.append(matmul_tn(grad_branch, hidden).astype(jnp.bfloat16))
        up_grads.append(matmul_tn(ynorm, grad_up).astype(jnp.bfloat16))
        grad_ynorm = grad_ynorm + matmul_nt(grad_up, up_part)
    depth = seg_size // 4
    forward_grads = [
        jnp.stack(grads[start : start + mlp_size]).reshape(mlp_size, depth, 2, 2, rows, half)
        for start in (0, mlp_size)
        for grads in (up_grads, down_grads)
    ]
    up_left, down_left, up_right, down_right = scatter_call(
        forward_grads, ["mxz"] * 4, seg_size, mlp_size, "scatter_forward", 2
    )
    up_grad_part = jnp.concatenate([up_left, up_right], axis=1)
    down_grad_part = jnp.concatenate([down_left, down_right], axis=1)
    grad_resid_norm, mlp_gain_grad = jax.vjp(rms_norm, resid_rows, mlp_gain)[1](grad_ynorm)
    grad_resid = grad_out + grad_resid_norm

    def backward_step(grad_carry, inputs):
        grad_state_next, grad_key_next, grad_value_next = grad_carry
        (
            block_index,
            prev_qkv,
            token_qkv,
            state_qkv,
            mixed_out,
            log_total,
            state_read,
            state_log,
            update,
            state_now,
            grad_block,
        ) = inputs
        allowed, seen = masks_for(block_index)
        query_tok = token_qkv[:, :feature_width]
        key_tok = token_qkv[:, feature_width : 2 * feature_width]
        value_tok = token_qkv[:, 2 * feature_width :]
        key_all = jnp.concatenate(
            [
                prev_qkv[:, feature_width : 2 * feature_width],
                key_tok,
                state_qkv[:, feature_width : 2 * feature_width],
            ],
            axis=0,
        )
        value_all = jnp.concatenate(
            [prev_qkv[:, 2 * feature_width :], value_tok, state_qkv[:, 2 * feature_width :]], axis=0
        )
        grad_update = (grad_state_next * (1.0 - gate_open)).astype(jnp.bfloat16)
        bias_term = (
            jnp.sum(grad_state_next * (state_now - update), axis=0) * gate_open * (1.0 - gate_open)
        )
        grad_read = matmul_nt(grad_update, sout_full).astype(jnp.bfloat16)
        grad_squery, grad_key_read, grad_value_read = attend_backward(
            state_qkv[:, :feature_width], key_tok, value_tok, seen, state_log, grad_read
        )
        grad_mix_in = grad_block.astype(jnp.bfloat16)
        grad_mixed = matmul_nt(grad_mix_in, out_full).astype(jnp.bfloat16)
        grad_query, grad_keys, grad_values = attend_backward(
            query_tok, key_all, value_all, allowed, log_total, grad_mixed
        )
        grad_key_tok = (grad_keys[BLOCK : 2 * BLOCK] + grad_key_read + grad_key_next).astype(
            jnp.bfloat16
        )
        grad_value_tok = (
            grad_values[BLOCK : 2 * BLOCK] + grad_value_read + grad_value_next
        ).astype(jnp.bfloat16)
        grad_token_qkv = jnp.concatenate(
            [grad_query.astype(jnp.bfloat16), grad_key_tok, grad_value_tok], axis=1
        )
        grad_state_qkv = jnp.concatenate(
            [grad_squery, grad_keys[2 * BLOCK :], grad_values[2 * BLOCK :]], axis=1
        ).astype(jnp.bfloat16)
        grad_state_normed = matmul_nt(grad_state_qkv, state_projection)
        grad_state_norm, state_gain_term = jax.vjp(rms_norm, state_now, state_gain)[1](
            grad_state_normed
        )
        grad_state_now = grad_state_next * gate_open + grad_state_norm
        carry_out = (grad_state_now, grad_keys[:BLOCK], grad_values[:BLOCK])
        return (
            carry_out,
            (grad_token_qkv, grad_state_qkv, grad_mix_in, grad_update, bias_term, state_gain_term),
        )

    prev_qkv_all = jnp.concatenate(
        [jnp.zeros((1, BLOCK, 3 * feature_width), jnp.bfloat16), token_qkv_all[:-1]], axis=0
    )
    zero_grad = jnp.zeros((BLOCK, feature_width), jnp.float32)
    (grad_state_start, unused_key, unused_value), grads_block = lax.scan(
        backward_step,
        (final_state_cotangent[0].astype(jnp.float32), zero_grad, zero_grad),
        (
            block_ids,
            prev_qkv_all,
            token_qkv_all,
            state_qkv_all,
            mixed_all,
            log_all,
            read_all,
            read_log_all,
            update_all,
            states_all,
            grad_resid.reshape(block_count, BLOCK, feature_width),
        ),
        reverse=True,
    )
    (
        grad_token_qkv_all,
        grad_state_qkv_all,
        grad_mix_all,
        grad_update_all,
        bias_terms,
        state_gain_terms,
    ) = grads_block
    grad_qkv_rows = grad_token_qkv_all.reshape(seq_len, 3 * feature_width)
    token_proj_grad = matmul_tn(normed_all.reshape(seq_len, feature_width), grad_qkv_rows)
    grad_normed = matmul_nt(grad_qkv_rows, token_proj)
    grad_tok_norm, attn_gain_grad = jax.vjp(rms_norm, seg_tokens, attn_gain)[1](grad_normed)
    grad_tokens = grad_resid + grad_tok_norm
    out_grad = matmul_tn(
        mixed_all.reshape(seq_len, feature_width), grad_mix_all.reshape(seq_len, feature_width)
    )
    state_total = block_count * state_rows
    state_projection_gradient = matmul_tn(
        state_normed_all.reshape(state_total, feature_width),
        grad_state_qkv_all.reshape(state_total, 3 * feature_width),
    )
    sout_grad = matmul_tn(
        read_all.reshape(state_total, feature_width),
        grad_update_all.reshape(state_total, feature_width),
    )
    bias_grad = jnp.sum(bias_terms, axis=0)
    state_gain_grad = jnp.sum(state_gain_terms, axis=0)
    query_grad = token_proj_grad[:, :feature_width]
    key_grad = token_proj_grad[:, feature_width : 2 * feature_width]
    value_grad = token_proj_grad[:, 2 * feature_width :]
    squery_grad = state_projection_gradient[:, :feature_width]
    state_key_gradient = state_projection_gradient[:, feature_width : 2 * feature_width]
    svalue_grad = state_projection_gradient[:, 2 * feature_width :]
    small_grads = jnp.stack([attn_gain_grad, state_gain_grad, mlp_gain_grad, bias_grad])
    small_grads = small_grads.reshape(4, seg_size, rows).transpose(1, 0, 2)
    small_grads = small_grads.reshape(seg_size, -1, 128)
    small_lines = small_grads.shape[1]
    small_grads = jnp.pad(small_grads, ((0, 0), (0, 8 - small_lines), (0, 0)))
    summed = scatter_call(
        [small_grads.reshape(depth, 2, 2, 8, 128)]
        + [
            grad.astype(jnp.bfloat16).reshape(depth, 2, 2, rows, width)
            for grad in (
                out_grad,
                sout_grad,
                squery_grad,
                state_key_gradient,
                svalue_grad,
                query_grad,
                key_grad,
                value_grad,
            )
        ],
        ["xz"] * 9,
        seg_size,
        mlp_size,
        "scatter_rest",
        3,
    )
    (
        small_sum,
        out_grad,
        sout_grad,
        squery_grad,
        state_key_gradient,
        svalue_grad,
        query_grad,
        key_grad,
        value_grad,
    ) = summed
    attn_gain_grad, state_gain_grad, mlp_gain_grad, bias_grad = small_sum[:small_lines].reshape(
        4, rows
    )
    return (
        out_rows.astype(jnp.bfloat16)[None],
        last_state.astype(jnp.bfloat16)[None],
        grad_tokens[None],
        grad_state_start[None],
        query_grad,
        key_grad,
        value_grad,
        out_grad,
        squery_grad,
        state_key_gradient,
        svalue_grad,
        sout_grad,
        up_grad_part,
        down_grad_part,
        attn_gain_grad,
        state_gain_grad,
        mlp_gain_grad,
        bias_grad,
    )


def solution(mesh):
    return jax.shard_map(
        functools.partial(shards, mesh.shape["mlp"]),
        mesh=mesh,
        in_specs=(
            P(("seg", "mlp"), None, None),
            P(("seg", "mlp"), None, None),
            P(("seg", "mlp")),
            P("seg", None),
            P("seg", None),
            P("seg", None),
            P("seg", None),
            P("seg", None),
            P("seg", None),
            P("seg", None),
            P("seg", None),
            P("seg", "mlp"),
            P("seg", "mlp"),
            P("seg"),
            P("seg"),
            P("seg"),
            P("seg"),
            P(("seg", "mlp"), None, None),
            P(("seg", "mlp"), None, None),
        ),
        out_specs=(
            P(("seg", "mlp"), None, None),
            P(("seg", "mlp"), None, None),
            P(("seg", "mlp"), None, None),
            P(("seg", "mlp"), None, None),
            P("seg", None),
            P("seg", None),
            P("seg", None),
            P("seg", None),
            P("seg", None),
            P("seg", None),
            P("seg", None),
            P("seg", None),
            P("seg", "mlp"),
            P("seg", "mlp"),
            P("seg"),
            P("seg"),
            P("seg"),
            P("seg"),
        ),
        check_vma=False,
    )
```

```python
import functools
import jax
import jax.numpy as jnp
from jax import lax
from jax.experimental import pallas as pl
from jax.experimental.pallas import tpu as pltpu
from jax.sharding import PartitionSpec as P

MESH = pl.DeviceIdType.MESH


class Place:
    def __init__(self, seg_size, mlp_size):
        seg = lax.axis_index("seg")
        self.sizes = {"z": seg_size // 4, "x": 2, "c": 2, "m": mlp_size}
        self.at = {
            "z": lax.div(seg, 4),
            "x": lax.rem(lax.div(seg, 2), 2),
            "c": lax.rem(seg, 2),
            "m": lax.axis_index("mlp"),
        }

    def device(self, **moved):
        at = {**self.at, **moved}
        return (at["z"] * 4 + at["x"] * 2 + at["c"], at["m"])

    def ahead(self, axis, step):
        return lax.rem(self.at[axis] + step, self.sizes[axis])

    def behind(self, axis, step):
        return lax.rem(self.at[axis] + self.sizes[axis] - step, self.sizes[axis])

    def greet(self):
        barrier = pltpu.get_barrier_semaphore()

        def signal(**moved):
            pl.semaphore_signal(
                barrier, inc=1, device_id=self.device(**moved), device_id_type=MESH
            )

        z, last = self.at["z"], self.sizes["z"] - 1
        count = 0
        for axis in "xcm":
            for step in range(1, self.sizes[axis]):
                signal(**{axis: self.ahead(axis, step)})
                count += 1

        @pl.when(z > 0)
        def _():
            signal(z=z - 1)

        @pl.when(z < last)
        def _():
            signal(z=z + 1)

        count = count + lax.min(z, 1) + lax.min(last - z, 1)
        pl.semaphore_wait(barrier, count)


class Wires:
    def __init__(self, place, send, recv):
        self.place, self.send, self.recv, self.used = place, send, recv, 0

    def copy(self, src, dst, pair, moved):
        return pltpu.make_async_remote_copy(
            src_ref=src,
            dst_ref=dst,
            send_sem=self.send.at[pair],
            recv_sem=self.recv.at[pair],
            device_id=self.place.device(**moved),
            device_id_type=MESH,
        )


def guarded(condition, action):
    if condition is None:
        action()
    else:
        pl.when(condition)(action)


class Flow:
    def __init__(self, wires):
        self.wires, self.arriving, self.sent = wires, [], []

    def move(self, src, dst, moved, landing, goes=None, comes=None):
        pair = self.wires.used
        self.wires.used += 1
        out = lambda: self.wires.copy(src, dst, pair, moved)
        guarded(goes, lambda: out().start())
        self.sent.append((goes, lambda: out().wait_send()))
        self.arriving.append(
            (comes, lambda: self.wires.copy(landing, landing, pair, moved).wait_recv())
        )

    def arrive(self):
        for condition, wait in self.arriving:
            guarded(condition, wait)
        self.arriving.clear()

    def finish(self):
        self.arrive()
        for condition, wait in self.sent:
            guarded(condition, wait)
        self.sent.clear()


def gather(wires, source, target, order, columns, local_sem):
    place, flow = wires.place, Flow(wires)
    axes = ("m" if len(target.shape) == 6 else "") + "zxc"
    at, sizes, done = place.at, place.sizes, set()

    def view(**moved):
        index = [
            moved[a] if a in moved else pl.ds(0, sizes[a]) if a in done else at[a] for a in axes
        ]
        return target.at[tuple(index) + block]

    block = (pl.ds(0, source.shape[0]), pl.ds(*columns))
    source = source.at[block]
    own = pltpu.make_async_copy(source, view(), local_sem)
    own.start()
    first = True
    z, last = at["z"], sizes["z"] - 1
    for axis in order + "c":
        if axis == "z":
            for t in range(last):
                flow.arrive()
                below, above = lax.max(z - t, 0), lax.min(z + t, last)
                flow.move(
                    source if first and t == 0 else view(z=below),
                    view(z=below),
                    dict(z=z + 1),
                    view(z=lax.max(z - 1 - t, 0)),
                    (z >= t) & (z < last),
                    z >= t + 1,
                )
                flow.move(
                    source if first and t == 0 else view(z=above),
                    view(z=above),
                    dict(z=z - 1),
                    view(z=lax.min(z + 1 + t, last)),
                    (z + t <= last) & (z > 0),
                    z + 1 + t <= last,
                )
                yield
        else:
            flow.arrive()
            for step in range(1, sizes[axis]):
                flow.move(
                    source if first else view(),
                    view(),
                    {axis: place.ahead(axis, step)},
                    view(**{axis: place.behind(axis, step)}),
                )
            yield
        done.add(axis)
        if first:
            own.wait()
            first = False
    flow.finish()


def add_into(total, term):
    lead = total.shape[:-2]

    def body(i, carry):
        index, rest = [], i
        for size in reversed(lead):
            index.append(lax.rem(rest, size))
            rest = lax.div(rest, size)
        there = tuple(reversed(index))
        summed = total[there].astype(jnp.float32) + term[there].astype(jnp.float32)
        total[there] = summed.astype(total.dtype)
        return carry

    lax.fori_loop(0, functools.reduce(lambda a, b: a * b, lead, 1), body, 0)


def scatter(wires, grad, result, own, core_in, m_in, x_in, up_in, down_in, order, columns, local_sem):
    place, flow = wires.place, Flow(wires)
    split_m = len(grad.shape) == 6
    axes = ("m" if split_m else "") + "zx"
    at, sizes, done = place.at, place.sizes, set()
    z, last = at["z"], sizes["z"] - 1
    full = tuple(pl.ds(0, sizes[a]) for a in axes)
    block = (pl.ds(0, grad.shape[-2]), pl.ds(*columns))

    def view(ref, **moved):
        index = [
            moved[a] if a in moved else at[a] if a in done else pl.ds(0, sizes[a]) for a in axes
        ]
        return ref.at[tuple(index)]

    load = pltpu.make_async_copy(grad.at[full + (at["c"],) + block], own, local_sem)
    load.start()
    flow.move(grad.at[full + (1 - at["c"],) + block], core_in, dict(c=1 - at["c"]), core_in)
    yield
    load.wait()
    flow.arrive()
    add_into(own, core_in)
    for axis in order:
        if axis == "x":
            flow.move(view(own, x=1 - at["x"]), x_in, dict(x=1 - at["x"]), x_in)
            yield
            flow.arrive()
            done.add("x")
            add_into(view(own), x_in)
        elif axis == "m":
            for step in range(1, sizes["m"]):
                flow.move(
                    view(own, m=place.ahead("m", step)), m_in.at[step - 1],
                    dict(m=place.ahead("m", step)), m_in.at[step - 1],
                )
            yield
            flow.arrive()
            done.add("m")
            for step in range(1, sizes["m"]):
                add_into(view(own), m_in.at[step - 1])
        else:
            for t in range(last):
                up, down = lax.min(last - t + z, last), lax.max(z - last + t, 0)
                flow.move(view(own, z=up), up_in.at[t], dict(z=z + 1), up_in.at[t],
                          (z <= t) & (z < last), (z >= 1) & (z - 1 <= t))
                flow.move(view(own, z=down), down_in.at[t], dict(z=z - 1), down_in.at[t],
                          (last - z <= t) & (z > 0), (z < last) & (last - z - 1 <= t))
                yield
                flow.arrive()
                up, down = lax.min(last - 1 - t + z, last), lax.max(z - last + t + 1, 0)
                pl.when((z >= 1) & (z - 1 <= t))(lambda: add_into(view(own, z=up), up_in.at[t]))
                pl.when((z < last) & (last - z - 1 <= t))(lambda: add_into(view(own, z=down), down_in.at[t]))
            done.add("z")
    if split_m:
        result[block] = view(own)[...].astype(jnp.float32)
    else:
        slot = m_in.at[at["m"]]
        slot[...] = view(own)[...]
        for step in range(1, sizes["m"]):
            flow.move(slot, slot, dict(m=place.ahead("m", step)), m_in.at[place.behind("m", step)])
        yield
        flow.arrive()
        total = m_in[0].astype(jnp.float32)
        for i in range(1, sizes["m"]):
            total = total + m_in[i].astype(jnp.float32)
        result[block] = total
    flow.finish()


def run_rounds(flows):
    live, waiting = [], list(flows)
    while live or waiting:
        if waiting:
            live.append(waiting.pop(0))
        live = [f for f in live if next(f, StopIteration) is not StopIteration]


def lead_shape(order, split_m, done, sizes):
    axes = ("m" if split_m else "") + "zx"
    return tuple(sizes[a] for a in axes if a not in done)


def gather_call(sources, units, seg_size, mlp_size, name, collective_id):
    count = len(sources)
    sizes = {"z": seg_size // 4, "x": 2, "c": 2, "m": mlp_size}

    def kernel(*refs):
        ins, outs = refs[:count], refs[count : 2 * count]
        send, recv, local = refs[2 * count :]
        place = Place(seg_size, mlp_size)
        place.greet()
        wires = Wires(place, send, recv)
        run_rounds(
            [
                gather(wires, ins[i], outs[i], order, columns, local.at[unit])
                for unit, (i, order, columns) in enumerate(units)
            ]
        )

    kinds = {i: order for i, order, _ in units}
    shapes = [
        jax.ShapeDtypeStruct(
            ((mlp_size,) if "m" in kinds[i] else ()) + (sizes["z"], 2, 2) + source.shape,
            source.dtype,
        )
        for i, source in enumerate(sources)
    ]
    pairs = sum(2 * (sizes["z"] - 1) + 2 + ("m" in order) * (mlp_size - 1) for _, order, _ in units)
    anywhere = pl.BlockSpec(memory_space=pl.ANY)
    return pl.pallas_call(
        kernel,
        out_shape=shapes,
        in_specs=[anywhere] * count,
        out_specs=[anywhere] * count,
        scratch_shapes=[
            pltpu.SemaphoreType.DMA((pairs,)),
            pltpu.SemaphoreType.DMA((pairs,)),
            pltpu.SemaphoreType.DMA((len(units),)),
        ],
        compiler_params=pltpu.CompilerParams(collective_id=collective_id, has_side_effects=True),
        name=name,
    )(*sources)


def scatter_buffers(grad, order, columns, sizes):
    split_m = grad.ndim == 6
    rows = (grad.shape[-2], columns[1])

    def left(axis):
        done = order[: order.index(axis) + 1]
        return lead_shape(order, split_m, done, sizes) + rows

    return [
        pltpu.VMEM(shape, grad.dtype)
        for shape in (
            lead_shape(order, split_m, "", sizes) + rows,
            lead_shape(order, split_m, "", sizes) + rows,
            (sizes["m"] - 1,) + left("m") if split_m else (sizes["m"],) + rows,
            left("x"),
            (sizes["z"] - 1,) + left("z"),
            (sizes["z"] - 1,) + left("z"),
        )
    ]


def scatter_call(grads, units, seg_size, mlp_size, name, collective_id):
    count = len(grads)
    sizes = {"z": seg_size // 4, "x": 2, "c": 2, "m": mlp_size}

    def kernel(*refs):
        ins, outs = refs[:count], refs[count : 2 * count]
        buffers = refs[2 * count : -3]
        send, recv, local = refs[-3:]
        place = Place(seg_size, mlp_size)
        place.greet()
        wires = Wires(place, send, recv)
        run_rounds(
            [
                scatter(
                    wires, ins[i], outs[i], *buffers[6 * unit : 6 * unit + 6], order, columns,
                    local.at[unit],
                )
                for unit, (i, order, columns) in enumerate(units)
            ]
        )

    buffers = []
    for i, order, columns in units:
        buffers += scatter_buffers(grads[i], order, columns, sizes)
    pairs = sum(2 * (sizes["z"] - 1) + 2 + (mlp_size - 1) for _, order, _ in units)
    return pl.pallas_call(
        kernel,
        out_shape=[jax.ShapeDtypeStruct(grad.shape[-2:], jnp.float32) for grad in grads],
        in_specs=[pl.BlockSpec(memory_space=pl.ANY)] * count,
        out_specs=[pl.BlockSpec(memory_space=pltpu.VMEM)] * count,
        scratch_shapes=buffers
        + [
            pltpu.SemaphoreType.DMA((pairs,)),
            pltpu.SemaphoreType.DMA((pairs,)),
            pltpu.SemaphoreType.DMA((len(units),)),
        ],
        compiler_params=pltpu.CompilerParams(
            collective_id=collective_id, has_side_effects=True, vmem_limit_bytes=56 << 20
        ),
        name=name,
    )(*grads)


HEAD = 128
BLOCK = 512
EPS = 1e-06
NEGATIVE = -1e30
GELU_C = 0.7978845608
GELU_K = 0.044715
SCALE = HEAD**-0.5
LOG2E = 1.4426950408889634
PAIR = 2 * HEAD
TILE = 256
BF16 = jnp.bfloat16
F32 = jnp.float32
VMEM_LIMIT = 60 << 20


def matmul(left, right):
    return jnp.dot(left, right, preferred_element_type=F32)


def matmul_nt(left, right):
    return lax.dot_general(left, right, (((1,), (1,)), ((), ())), preferred_element_type=F32)


def inverse_rms(values):
    return lax.rsqrt(jnp.mean(values * values, axis=-1, keepdims=True) + EPS)


def rms_backward(values, gain, grad):
    inverse = inverse_rms(values)
    unit = values * inverse
    weighted = grad * gain
    inner = jnp.mean(weighted * unit, axis=-1, keepdims=True)
    return inverse * (weighted - unit * inner), grad * unit


def params(**more):
    return pltpu.CompilerParams(vmem_limit_bytes=VMEM_LIMIT, **more)


def whole(shape):
    return pl.BlockSpec(shape, lambda *_: (0,) * len(shape))


def project_kernel(x_ref, gain_ref, wq, wk, wv, normed, q, k, v):
    @pl.when(pl.program_id(0) == 0)
    def _():
        x = x_ref[...].astype(F32)
        normed[...] = (x * inverse_rms(x) * gain_ref[...]).astype(BF16)

    rows = normed[...]
    for weight, out in ((wq, q), (wk, k), (wv, v)):
        out[...] = matmul(rows, weight[...]).astype(BF16)


def project(x, gain, weights):
    rows, width = x.shape
    tile = pl.BlockSpec((width, TILE), lambda j: (0, j))
    out = pl.BlockSpec((rows, TILE), lambda j: (0, j))
    return pl.pallas_call(
        project_kernel,
        grid=(width // TILE,),
        in_specs=[whole((rows, width)), whole((1, width)), tile, tile, tile],
        out_specs=[whole((rows, width)), out, out, out],
        out_shape=[jax.ShapeDtypeStruct((rows, width), BF16)] * 4,
        compiler_params=params(),
        name="project_tokens",
    )(x, gain, *weights)


def attend(query, pieces):
    scores = []
    for keys, _, mask in pieces:
        score = matmul_nt(keys, query) * (SCALE * LOG2E)
        scores.append(score if mask is None else jnp.where(mask, score, NEGATIVE))
    top = functools.reduce(jnp.maximum, [jnp.max(s, axis=0, keepdims=True) for s in scores])
    total, mixed = 0.0, 0.0
    for score, (_, values, _) in zip(scores, pieces):
        weights = jnp.exp2(score - top)
        total = total + jnp.sum(weights, axis=0, keepdims=True)
        mixed = mixed + matmul(values.T, weights.astype(BF16))
    return (mixed / total).T.astype(BF16), top + jnp.log2(total)


def attend_backward(query, log_total, grad, centre, pieces):
    grad_query = 0.0
    for keys, values, mask, add_keys, add_values in pieces:
        score = matmul_nt(keys, query) * (SCALE * LOG2E)
        if mask is not None:
            score = jnp.where(mask, score, NEGATIVE)
        probs = jnp.exp2(score - log_total)
        add_values(matmul(probs.astype(BF16), grad))
        grad_probs = matmul_nt(values, grad)
        grad_scores = (probs * (grad_probs - centre)).astype(BF16)
        add_keys(matmul(grad_scores, query) * SCALE)
        grad_query = grad_query + matmul(keys.T, grad_scores)
    return (grad_query * SCALE).T


def centre_of(grad, mixed):
    return jnp.sum((grad.astype(F32) * mixed.astype(F32)).T, axis=0, keepdims=True)


def position(shape, axis):
    return lax.broadcasted_iota(jnp.int32, shape, axis)


def token_pieces(block, half, valid):
    key = position((TILE, TILE), 0)
    query = position((TILE, TILE), 1)
    causal, recent = key <= query, key > query
    pieces = []
    if block:
        start = (block - 1) * BLOCK
        pieces.append(("near", start + half * TILE, TILE, recent))
        if half == 0:
            pieces.append(("near", start + TILE, TILE, None))
    start = block * BLOCK
    for piece in range(half + 1):
        first = start + piece * TILE
        seen = first + key < valid
        mask = causal if piece == half else None
        if block:
            mask = seen if mask is None else mask & seen
        pieces.append(("near", first, TILE, mask))
    pieces.append(("state", block * BLOCK, BLOCK, None))
    return pieces


def state_forward_kernel(
    valid, s0, gain, gate_bias, wq, wk, wv, wu, k, v,
    normed_out, sq, sk, sv, read, log_out, update_out, states, last,
    state, normed, total,
):
    block, pair = pl.program_id(0), pl.program_id(1)

    @pl.when((block == 0) & (pair == 0))
    def _():
        state[...] = s0[...].astype(F32)

    @pl.when(pair == 0)
    def _():
        now = state[...]
        rows = (now * inverse_rms(now) * gain[...]).astype(BF16)
        normed[...] = rows
        normed_out[...] = rows
        states[...] = now
        total[...] = jnp.zeros_like(total)

    rows = normed[...]
    for weight, out in ((wq, sq), (wk, sk), (wv, sv)):
        out[...] = matmul(rows, weight[...]).astype(BF16)
    seen = block * BLOCK + position((BLOCK, BLOCK), 0) < valid[0]
    for head in range(2):
        lanes = pl.ds(head * HEAD, HEAD)
        read[:, lanes], log_out[0, 0, pl.ds(head, 1), :] = attend(
            sq[:, lanes], [(k[:, lanes], v[:, lanes], seen)]
        )
    total[...] += matmul(read[...], wu[...])

    @pl.when(pair == pl.num_programs(1) - 1)
    def _():
        update = total[...]
        gate = 1.0 / (1.0 + jnp.exp(-gate_bias[...]))
        later = gate * state[...] + (1.0 - gate) * update
        update_out[...] = update
        state[...] = later
        last[...] = later.astype(BF16)


def state_forward(valid, s0, gain, gate_bias, weights, update_weight, k, v):
    rows, width = s0.shape
    blocks, pairs = k.shape[0] // BLOCK, width // PAIR
    columns = pl.BlockSpec((width, PAIR), lambda b, p: (0, p))
    tile = pl.BlockSpec((rows, PAIR), lambda b, p: (b, p))
    band = pl.BlockSpec((rows, width), lambda b, p: (b, 0))
    small = whole((1, width))

    def stack(kind):
        return jax.ShapeDtypeStruct((blocks * rows, width), kind)

    return pl.pallas_call(
        state_forward_kernel,
        grid=(blocks, pairs),
        in_specs=[
            pl.BlockSpec(memory_space=pltpu.SMEM), whole((rows, width)), small, small,
            columns, columns, columns, pl.BlockSpec((PAIR, width), lambda b, p: (p, 0)),
            pl.BlockSpec((BLOCK, PAIR), lambda b, p: (b, p)),
            pl.BlockSpec((BLOCK, PAIR), lambda b, p: (b, p)),
        ],
        out_specs=[
            band, tile, tile, tile, tile,
            pl.BlockSpec((1, 1, 2, rows), lambda b, p: (b, p, 0, 0)),
            band, band, whole((rows, width)),
        ],
        out_shape=[
            stack(BF16), stack(BF16), stack(BF16), stack(BF16), stack(BF16),
            jax.ShapeDtypeStruct((blocks, pairs, 2, rows), F32),
            stack(F32), stack(F32), jax.ShapeDtypeStruct((rows, width), BF16),
        ],
        scratch_shapes=[
            pltpu.VMEM((rows, width), F32), pltpu.VMEM((rows, width), BF16),
            pltpu.VMEM((rows, width), F32),
        ],
        compiler_params=params(),
        name="state_forward",
    )(valid, s0, gain, gate_bias, *weights, update_weight, k, v)


def token_forward_kernel(
    valid, x, gain, q, k, v, sk, sv, wo, mixed, log_out, resid, ynorm
):
    pair = pl.program_id(0)

    @pl.when(pair == 0)
    def _():
        resid[...] = x[...].astype(F32)

    count = valid[0]
    for head in range(2):
        lanes = pl.ds(head * HEAD, HEAD)
        for block in range(q.shape[0] // BLOCK):
            for half in range(BLOCK // TILE):
                rows = pl.ds(block * BLOCK + half * TILE, TILE)
                pieces = []
                for kind, first, size, mask in token_pieces(block, half, count):
                    keys, values = (k, v) if kind == "near" else (sk, sv)
                    there = pl.ds(first, size)
                    pieces.append((keys[there, lanes], values[there, lanes], mask))
                mixed[rows, lanes], log_out[0, pl.ds(head, 1), rows] = attend(
                    q[rows, lanes], pieces
                )
    resid[...] += matmul(mixed[...], wo[...])

    @pl.when(pair == pl.num_programs(0) - 1)
    def _():
        rows = resid[...]
        ynorm[...] = (rows * inverse_rms(rows) * gain[...]).astype(BF16)


def token_forward(valid, x, gain, q, k, v, sk, sv, wo):
    rows, width = x.shape
    pairs = width // PAIR
    tile = pl.BlockSpec((rows, PAIR), lambda p: (0, p))
    states = pl.BlockSpec((sk.shape[0], PAIR), lambda p: (0, p))
    return pl.pallas_call(
        token_forward_kernel,
        grid=(pairs,),
        in_specs=[
            pl.BlockSpec(memory_space=pltpu.SMEM), whole((rows, width)), whole((1, width)),
            tile, tile, tile, states, states, pl.BlockSpec((PAIR, width), lambda p: (p, 0)),
        ],
        out_specs=[
            tile, pl.BlockSpec((1, 2, rows), lambda p: (p, 0, 0)),
            whole((rows, width)), whole((rows, width)),
        ],
        out_shape=[
            jax.ShapeDtypeStruct((rows, width), BF16),
            jax.ShapeDtypeStruct((pairs, 2, rows), F32),
            jax.ShapeDtypeStruct((rows, width), F32),
            jax.ShapeDtypeStruct((rows, width), BF16),
        ],
        compiler_params=params(),
        name="token_forward",
    )(valid, x, gain, q, k, v, sk, sv, wo)


def feed_forward_kernel(
    valid, resid, ynorm, gain, cot, up_w, down_w,
    out, grad_resid, grad_rounded, gain_grad, up_grad, down_grad,
    ynorm_t, masked, masked_t, total, grad_total,
):
    step, last = pl.program_id(0), pl.num_programs(0) - 1

    @pl.when(step == 0)
    def _():
        keep = position(cot.shape, 0) < valid[0]
        grad = jnp.where(keep, cot[...], jnp.zeros_like(cot))
        masked[...] = grad
        masked_t[...] = grad.T
        ynorm_t[...] = ynorm[...].T
        total[...] = resid[...]
        grad_total[...] = jnp.zeros_like(grad_total)

    up_part, down_part = up_w[0], down_w[0]
    up = matmul(ynorm[...], up_part)
    grad_hidden = matmul(masked[...], down_part)
    square = up * up
    bent = jnp.tanh(GELU_C * (up + GELU_K * square * up))
    hidden = (0.5 * up * (1.0 + bent)).astype(BF16)
    slope = 0.5 * (1.0 + bent) + 0.5 * up * (1.0 - bent * bent) * (
        GELU_C * (1.0 + 3.0 * GELU_K * square)
    )
    grad_up = (grad_hidden * slope).astype(BF16)
    total[...] += matmul_nt(hidden, down_part)
    grad_total[...] += matmul_nt(grad_up, up_part)
    down_grad[0] = matmul(masked_t[...], hidden).astype(BF16)
    up_grad[0] = matmul(ynorm_t[...], grad_up).astype(BF16)

    @pl.when(step == last)
    def _():
        out[...] = total[...].astype(BF16)
        grad, gain_rows = rms_backward(resid[...], gain[...], grad_total[...])
        grad = masked[...].astype(F32) + grad
        grad_resid[...] = grad
        grad_rounded[...] = grad.astype(BF16)
        gain_grad[...] = jnp.sum(gain_rows, axis=0, keepdims=True)


def feed_forward(valid, resid, ynorm, gain, cot, up_w, down_w, chunk=512):
    rows, width = resid.shape
    parts, _, part = up_w.shape
    chunk = min(chunk, part)
    each = part // chunk
    weight = pl.BlockSpec((1, width, chunk), lambda j: (j // each, 0, j % each))
    full = whole((rows, width))
    once = pl.BlockSpec((rows, width), lambda j: (0, 0), pipeline_mode=pl.Buffered(1))
    return pl.pallas_call(
        feed_forward_kernel,
        grid=(parts * each,),
        in_specs=[pl.BlockSpec(memory_space=pltpu.SMEM), once, once, whole((1, width)), once, weight, weight],
        out_specs=[once, once, once, whole((1, width)), weight, weight],
        out_shape=[
            jax.ShapeDtypeStruct((rows, width), BF16),
            jax.ShapeDtypeStruct((rows, width), F32),
            jax.ShapeDtypeStruct((rows, width), BF16),
            jax.ShapeDtypeStruct((1, width), F32),
            jax.ShapeDtypeStruct(up_w.shape, BF16),
            jax.ShapeDtypeStruct(down_w.shape, BF16),
        ],
        scratch_shapes=[
            pltpu.VMEM((width, rows), BF16), pltpu.VMEM((rows, width), BF16),
            pltpu.VMEM((width, rows), BF16), pltpu.VMEM((rows, width), F32),
            pltpu.VMEM((rows, width), F32),
        ],
        compiler_params=params(),
        name="feed_forward",
    )(valid, resid, ynorm, gain, cot, up_w, down_w)


def token_backward_kernel(
    valid, grad, q, k, v, sk, sv, wo, mixed, log_total,
    dq, dk, dv, dsk, dsv, wo_grad,
    grad_mixed, near_k, near_v, state_k, state_v,
):
    grad_rows = grad[...]
    grad_mixed[...] = matmul_nt(grad_rows, wo[...]).astype(BF16)
    wo_grad[...] = matmul(mixed[...].T, grad_rows).astype(BF16)
    for ref in (near_k, near_v, state_k, state_v):
        ref[...] = jnp.zeros_like(ref)
    count = valid[0]
    for head in range(2):
        lanes = pl.ds(head * HEAD, HEAD)

        def adder(ref, there):
            def add(term):
                ref[there, lanes] += term

            return add

        for block in range(q.shape[0] // BLOCK):
            for half in range(BLOCK // TILE):
                rows = pl.ds(block * BLOCK + half * TILE, TILE)
                pieces = []
                for kind, first, size, mask in token_pieces(block, half, count):
                    keys, values = (k, v) if kind == "near" else (sk, sv)
                    sums = (near_k, near_v) if kind == "near" else (state_k, state_v)
                    there = pl.ds(first, size)
                    pieces.append(
                        (keys[there, lanes], values[there, lanes], mask)
                        + tuple(adder(ref, there) for ref in sums)
                    )
                out_grad = grad_mixed[rows, lanes]
                dq[rows, lanes] = attend_backward(
                    q[rows, lanes],
                    log_total[0, pl.ds(head, 1), rows],
                    out_grad,
                    centre_of(out_grad, mixed[rows, lanes]),
                    pieces,
                ).astype(BF16)
    dk[...] = near_k[...]
    dv[...] = near_v[...]
    dsk[...] = state_k[...].astype(BF16)
    dsv[...] = state_v[...].astype(BF16)


def token_backward(valid, grad, q, k, v, sk, sv, wo, mixed, log_total):
    rows, width = grad.shape
    pairs = width // PAIR
    tile = pl.BlockSpec((rows, PAIR), lambda p: (0, p))
    states = pl.BlockSpec((sk.shape[0], PAIR), lambda p: (0, p))
    band = pl.BlockSpec((PAIR, width), lambda p: (p, 0))
    return pl.pallas_call(
        token_backward_kernel,
        grid=(pairs,),
        in_specs=[
            pl.BlockSpec(memory_space=pltpu.SMEM), whole((rows, width)),
            tile, tile, tile, states, states, band, tile,
            pl.BlockSpec((1, 2, rows), lambda p: (p, 0, 0)),
        ],
        out_specs=[tile, tile, tile, states, states, band],
        out_shape=[
            jax.ShapeDtypeStruct((rows, width), BF16),
            jax.ShapeDtypeStruct((rows, width), F32),
            jax.ShapeDtypeStruct((rows, width), F32),
            jax.ShapeDtypeStruct(sk.shape, BF16),
            jax.ShapeDtypeStruct(sk.shape, BF16),
            jax.ShapeDtypeStruct((width, width), BF16),
        ],
        scratch_shapes=[
            pltpu.VMEM((rows, PAIR), BF16), pltpu.VMEM((rows, PAIR), F32),
            pltpu.VMEM((rows, PAIR), F32), pltpu.VMEM((sk.shape[0], PAIR), F32),
            pltpu.VMEM((sk.shape[0], PAIR), F32),
        ],
        compiler_params=params(),
        name="token_backward",
    )(valid, grad, q, k, v, sk, sv, wo, mixed, log_total)


def state_backward_kernel(
    valid, cot, gain, gate_bias, wq, wk, wv, wu, states, updates,
    sq, k, v, read, log_total, near_k, near_v, dsk, dsv,
    dsq, dk, dv, dz_out, grad_state, gain_grad, bias_grad,
    later, dz, total, grad_read, sum_q, sum_k, sum_v,
):
    step, pair = pl.program_id(0), pl.program_id(1)
    block = pl.num_programs(0) - 1 - step
    gate = 1.0 / (1.0 + jnp.exp(-gate_bias[...]))

    @pl.when((step == 0) & (pair == 0))
    def _():
        later[...] = cot[...].astype(F32)
        gain_grad[...] = jnp.zeros_like(gain_grad)
        bias_grad[...] = jnp.zeros_like(bias_grad)

    @pl.when(pair == 0)
    def _():
        grad = later[...]
        rounded = (grad * (1.0 - gate)).astype(BF16)
        dz[...] = rounded
        dz_out[...] = rounded
        bias_grad[...] += (
            jnp.sum(grad * (states[...] - updates[...]), axis=0, keepdims=True) * gate * (1.0 - gate)
        )
        total[...] = jnp.zeros_like(total)

    grad_read[...] = matmul_nt(dz[...], wu[...]).astype(BF16)
    seen = block * BLOCK + position((BLOCK, BLOCK), 0) < valid[0]
    sum_k[...] = near_k[...]
    sum_v[...] = near_v[...]
    for head in range(2):
        lanes = pl.ds(head * HEAD, HEAD)

        def adder(ref):
            def add(term):
                ref[:, lanes] += term

            return add

        out_grad = grad_read[:, lanes]
        dsq[:, lanes] = attend_backward(
            sq[:, lanes],
            log_total[0, 0, pl.ds(head, 1), :],
            out_grad,
            centre_of(out_grad, read[:, lanes]),
            [(k[:, lanes], v[:, lanes], seen, adder(sum_k), adder(sum_v))],
        ).astype(BF16)
    dk[...] = sum_k[...].astype(BF16)
    dv[...] = sum_v[...].astype(BF16)
    total[...] += (
        matmul_nt(dsq[...], wq[...]) + matmul_nt(dsk[...], wk[...]) + matmul_nt(dsv[...], wv[...])
    )

    @pl.when(pair == pl.num_programs(1) - 1)
    def _():
        grad, gain_rows = rms_backward(states[...], gain[...], total[...])
        grad = later[...] * gate + grad
        later[...] = grad
        grad_state[...] = grad
        gain_grad[...] += jnp.sum(gain_rows, axis=0, keepdims=True)


def state_backward(
    valid, cot, gain, gate_bias, weights, update_weight, states, updates,
    sq, k, v, read, log_total, near_k, near_v, dsk, dsv,
):
    rows, width = cot.shape
    blocks, pairs = k.shape[0] // BLOCK, width // PAIR
    columns = pl.BlockSpec((width, PAIR), lambda s, p: (0, p))
    tile = pl.BlockSpec((rows, PAIR), lambda s, p: (blocks - 1 - s, p))
    token = pl.BlockSpec((BLOCK, PAIR), lambda s, p: (blocks - 1 - s, p))
    band = pl.BlockSpec((rows, width), lambda s, p: (blocks - 1 - s, 0))
    small = whole((1, width))
    return pl.pallas_call(
        state_backward_kernel,
        grid=(blocks, pairs),
        in_specs=[
            pl.BlockSpec(memory_space=pltpu.SMEM), whole((rows, width)), small, small,
            columns, columns, columns, pl.BlockSpec((PAIR, width), lambda s, p: (p, 0)),
            band, band, tile, token, token, tile,
            pl.BlockSpec((1, 1, 2, rows), lambda s, p: (blocks - 1 - s, p, 0, 0)),
            token, token, tile, tile,
        ],
        out_specs=[tile, token, token, band, whole((rows, width)), small, small],
        out_shape=[
            jax.ShapeDtypeStruct((blocks * rows, width), BF16),
            jax.ShapeDtypeStruct(k.shape, BF16),
            jax.ShapeDtypeStruct(k.shape, BF16),
            jax.ShapeDtypeStruct((blocks * rows, width), BF16),
            jax.ShapeDtypeStruct((rows, width), F32),
            jax.ShapeDtypeStruct((1, width), F32),
            jax.ShapeDtypeStruct((1, width), F32),
        ],
        scratch_shapes=[
            pltpu.VMEM((rows, width), F32), pltpu.VMEM((rows, width), BF16),
            pltpu.VMEM((rows, width), F32), pltpu.VMEM((rows, PAIR), BF16),
            pltpu.VMEM((rows, PAIR), F32), pltpu.VMEM((BLOCK, PAIR), F32),
            pltpu.VMEM((BLOCK, PAIR), F32),
        ],
        compiler_params=params(),
        name="state_backward",
    )(
        valid, cot, gain, gate_bias, *weights, update_weight, states, updates,
        sq, k, v, read, log_total, near_k, near_v, dsk, dsv,
    )


def token_grad_kernel(x, gain, grad_resid, dq, dk, dv, wq, wk, wv, grad_x, gain_grad):
    @pl.when(pl.program_id(0) == 0)
    def _():
        gain_grad[...] = jnp.zeros_like(gain_grad)

    grad_normed = (
        matmul_nt(dq[...], wq[...]) + matmul_nt(dk[...], wk[...]) + matmul_nt(dv[...], wv[...])
    )
    grad, gain_rows = rms_backward(x[...].astype(F32), gain[...], grad_normed)
    grad_x[...] = grad_resid[...] + grad
    gain_grad[...] += jnp.sum(gain_rows, axis=0, keepdims=True)


def token_grad(x, gain, grad_resid, grads, weights):
    rows, width = x.shape
    band = pl.BlockSpec((TILE, width), lambda i: (i, 0))
    weight = whole((width, width))
    return pl.pallas_call(
        token_grad_kernel,
        grid=(rows // TILE,),
        in_specs=[band, whole((1, width)), band, band, band, band, weight, weight, weight],
        out_specs=[band, whole((1, width))],
        out_shape=[
            jax.ShapeDtypeStruct((rows, width), F32), jax.ShapeDtypeStruct((1, width), F32)
        ],
        compiler_params=params(),
        name="token_grad",
    )(x, gain, grad_resid, *grads, *weights)


def weight_grad_kernel(count, left, *refs):
    rights, outs, left_t = refs[:count], refs[count : 2 * count], refs[-1]

    @pl.when(pl.program_id(0) == 0)
    def _():
        left_t[...] = left[...].T

    for right, out in zip(rights, outs):
        out[...] = matmul(left_t[...], right[...]).astype(BF16)


def weight_grad(left, rights, name):
    rows, width = left.shape
    count = len(rights)
    tile = pl.BlockSpec((rows, TILE), lambda j: (0, j))
    out = pl.BlockSpec((width, TILE), lambda j: (0, j))
    return pl.pallas_call(
        functools.partial(weight_grad_kernel, count),
        grid=(rights[0].shape[1] // TILE,),
        in_specs=[whole((rows, width))] + [tile] * count,
        out_specs=[out] * count,
        out_shape=[jax.ShapeDtypeStruct((width, right.shape[1]), BF16) for right in rights],
        scratch_shapes=[pltpu.VMEM((width, rows), BF16)],
        compiler_params=params(),
        name=name,
    )(left, *rights)


def shards(
    mlp_size,
    tokens,
    initial_state,
    valid,
    token_query_weight,
    token_key_weight,
    token_value_weight,
    token_output_weight,
    state_query_weight,
    state_key_weight,
    state_value_weight,
    state_update_weight,
    up_projection_weight,
    down_projection_weight,
    token_norm_gain,
    state_norm_gain,
    feedforward_norm_gain,
    state_gate_bias,
    output_cotangent,
    final_state_cotangent,
):
    rows = token_query_weight.shape[0]
    width = tokens.shape[2]
    seg_size = width // rows
    depth = seg_size // 4
    part = up_projection_weight.shape[1]
    small = jnp.concatenate(
        [token_norm_gain, state_norm_gain, feedforward_norm_gain, state_gate_bias]
    ).reshape(-1, 128)
    small = jnp.pad(small, ((0, 16 - small.shape[0]), (0, 0)))
    square = [
        token_query_weight,
        token_key_weight,
        token_value_weight,
        state_query_weight,
        state_key_weight,
        state_value_weight,
        token_output_weight,
        state_update_weight,
    ]
    half = part // 2
    gathered = gather_call(
        [small] + square + [up_projection_weight, down_projection_weight],
        [(0, "zx", (0, small.shape[1]))]
        + [(1 + i, "zx", (0, width)) for i in range(8)]
        + [(9 + i, "zxm", (h * half, half)) for h in range(2) for i in range(2)],
        seg_size,
        mlp_size,
        "gather_weights",
        1,
    )
    wq, wk, wv, sqw, skw, svw, wo, wu = [w.reshape(width, width) for w in gathered[1:9]]
    up_w, down_w = [w.reshape(mlp_size, width, part) for w in gathered[9:]]
    gains = gathered[0].reshape(seg_size, -1)[:, : 4 * rows].reshape(seg_size, 4, rows)
    gains = gains.transpose(1, 0, 2).reshape(4, 1, width).astype(F32)
    token_gain, state_gain, mlp_gain, gate_bias = [gains[i] for i in range(4)]

    x, s0 = tokens[0], initial_state[0]
    normed, q, k, v = project(x, token_gain, [wq, wk, wv])
    snormed, sq, sk, sv, read, read_log, updates, states, last = state_forward(
        valid, s0, state_gain, gate_bias, [sqw, skw, svw], wu, k, v
    )
    mixed, token_log, resid, ynorm = token_forward(valid, x, mlp_gain, q, k, v, sk, sv, wo)
    out, grad_resid, grad_rounded, mlp_gain_grad, up_grad, down_grad = feed_forward(
        valid, resid, ynorm, mlp_gain, output_cotangent[0], up_w, down_w
    )
    forward_grads = [
        g.reshape(mlp_size, depth, 2, 2, rows, part) for g in (up_grad, down_grad)
    ]
    up_sum, down_sum = scatter_call(
        forward_grads,
        [(i, "mxz", (h * half, half)) for h in range(2) for i in range(2)],
        seg_size,
        mlp_size,
        "scatter_forward",
        2,
    )
    dq, near_k, near_v, dsk, dsv, wo_grad = token_backward(
        valid, grad_rounded, q, k, v, sk, sv, wo, mixed, token_log
    )
    dsq, dk, dv, dz, grad_state, state_gain_grad, bias_grad = state_backward(
        valid, final_state_cotangent[0], state_gain, gate_bias, [sqw, skw, svw], wu,
        states, updates, sq, k, v, read, read_log, near_k, near_v, dsk, dsv,
    )
    grad_tokens, token_gain_grad = token_grad(
        x, token_gain, grad_resid, [dq, dk, dv], [wq, wk, wv]
    )
    square_grads = (
        [wo_grad]
        + list(weight_grad(read, [dz], "weight_grad_update"))
        + list(weight_grad(snormed, [dsq, dsk, dsv], "weight_grad_state"))
        + list(weight_grad(normed, [dq, dk, dv], "weight_grad_tokens"))
    )
    small_grads = jnp.concatenate([token_gain_grad, state_gain_grad, mlp_gain_grad, bias_grad])
    small_grads = small_grads.reshape(4, seg_size, rows).transpose(1, 0, 2)
    small_grads = small_grads.reshape(seg_size, -1, 128)
    lines = small_grads.shape[1]
    small_grads = jnp.pad(small_grads, ((0, 0), (0, 8 - lines), (0, 0)))
    summed = scatter_call(
        [small_grads.reshape(depth, 2, 2, 8, 128)]
        + [grad.reshape(depth, 2, 2, rows, width) for grad in square_grads],
        [(0, "xz", (0, 128))] + [(1 + i, "xz", (0, width)) for i in range(8)],
        seg_size,
        mlp_size,
        "scatter_rest",
        3,
    )
    small_sum, go, gu, gsq, gsk, gsv, gq, gk, gv = summed
    small_sum = small_sum[:lines].reshape(4, rows)
    return (
        out[None],
        last[None],
        grad_tokens[None],
        grad_state[None],
        gq,
        gk,
        gv,
        go,
        gsq,
        gsk,
        gsv,
        gu,
        up_sum,
        down_sum,
        small_sum[0],
        small_sum[1],
        small_sum[2],
        small_sum[3],
    )


def solution(mesh):
    own = P(("seg", "mlp"), None, None)
    square, forward, small = P("seg", None), P("seg", "mlp"), P("seg")
    return jax.shard_map(
        functools.partial(shards, mesh.shape["mlp"]),
        mesh=mesh,
        in_specs=(own, own, P(("seg", "mlp")))
        + (square,) * 8
        + (forward,) * 2
        + (small,) * 4
        + (own, own),
        out_specs=(own,) * 4 + (square,) * 8 + (forward,) * 2 + (small,) * 4,
        check_vma=False,
    )
```

```python
import functools
import jax
import jax.numpy as jnp
from jax import lax
from jax.experimental import pallas as pl
from jax.experimental.pallas import tpu as pltpu
from jax.sharding import PartitionSpec as P

BF16 = jnp.bfloat16
F32 = jnp.float32
VMEM_LIMIT = 60 << 20
SQUARE_PIECES = 4
FORWARD_PIECES = 2


class Place:
    def __init__(self, sizes):
        seg = lax.axis_index("seg")
        self.sizes = sizes
        self.at = {
            "z": lax.div(seg, 4),
            "x": lax.rem(lax.div(seg, 2), 2),
            "c": lax.rem(seg, 2),
            "m": lax.axis_index("mlp"),
        }

    def device(self, moved):
        at = {**self.at, **moved}
        return (at["z"] * 4 + at["x"] * 2 + at["c"], at["m"])

    def ahead(self, axis, step):
        return lax.rem(self.at[axis] + step, self.sizes[axis])

    def behind(self, axis, step):
        return lax.rem(self.at[axis] + self.sizes[axis] - step, self.sizes[axis])

    def greet(self):
        barrier = pltpu.get_barrier_semaphore()
        count = 0
        for axis in "zxcm":
            for step in range(1, self.sizes[axis]):
                pl.semaphore_signal(
                    barrier,
                    inc=1,
                    device_id=self.device({axis: self.ahead(axis, step)}),
                    device_id_type=pl.DeviceIdType.MESH,
                )
                count += 1
        pl.semaphore_wait(barrier, count)


class Flow:
    def __init__(self, place, send, recv, taken):
        self.place, self.send, self.recv, self.taken = place, send, recv, taken
        self.steps, self.arriving, self.sent = [], [], []

    def move(self, actions, make):
        pair = self.taken[0]
        self.taken[0] += 1

        def copy(source, target, moved):
            return pltpu.make_async_remote_copy(
                src_ref=source,
                dst_ref=target,
                send_sem=self.send.at[pair],
                recv_sem=self.recv.at[pair],
                device_id=self.place.device(moved),
                device_id_type=pl.DeviceIdType.MESH,
            )

        def outgoing():
            source, target, moved, _ = make()
            return copy(source, target, moved)

        def incoming():
            _, _, moved, landing = make()
            return copy(landing, landing, moved)

        actions.append(lambda: outgoing().start())
        self.sent.append(lambda: outgoing().wait_send())
        self.arriving.append(lambda: incoming().wait_recv())

    def arrived(self):
        waits, self.arriving = self.arriving, []
        return waits


def gather_steps(flow, source, target, order, split, columns, local_sem, begin, end):
    place = flow.place
    at, sizes = place.at, place.sizes
    lead = ("m" if len(target.shape) == 6 else "") + "zxc"
    first_column, width = columns
    share = width // sizes["m"] if split else width

    def block(done, moved):
        if not split or "m" in done:
            lanes = pl.ds(first_column, width)
        else:
            lanes = pl.ds(pl.multiple_of(first_column + moved.get("m", at["m"]) * share, 128), share)
        return (pl.ds(0, source.shape[0]), lanes)

    def view(done, **moved):
        index = tuple(
            moved[a] if a in moved else pl.ds(0, sizes[a]) if a in done else at[a] for a in lead
        )
        return target.at[index + block(done, moved)]

    def own_source():
        return source.at[block("", {})]

    def own():
        return pltpu.make_async_copy(own_source(), view(""), local_sem)

    waits = []
    for i, axis in enumerate(order + "c"):
        done = order[:i]
        if not begin <= i < end:
            continue
        actions = flow.arrived() + waits
        waits = []
        if i == 0:
            actions.append(lambda: own().start())
            waits.append(lambda: own().wait())
        for step in range(1, sizes[axis]):

            def make(axis=axis, step=step, done=done):
                return (
                    view(done) if done else own_source(),
                    view(done),
                    {axis: place.ahead(axis, step)},
                    view(done, **{axis: place.behind(axis, step)}),
                )

            flow.move(actions, make)
        flow.steps.append(actions)
    flow.last = flow.arrived() + waits + flow.sent


def add_into(total, term):
    lead = total.shape[:-2]

    def body(i, carry):
        index, rest = [], i
        for size in reversed(lead):
            index.append(lax.rem(rest, size))
            rest = lax.div(rest, size)
        there = tuple(reversed(index)) + (Ellipsis,)
        total[there] = total[there] + term[there]
        return carry

    lax.fori_loop(0, functools.reduce(lambda a, b: a * b, lead, 1), body, 0)


def scatter_shapes(grad_shape, order, split, columns, sizes):
    lead = ("m" if len(grad_shape) == 6 else "") + "zx"
    rows, width = grad_shape[-2], columns[1]

    def left(done):
        share = width // sizes["m"] if split and "m" in done else width
        return tuple(sizes[a] for a in lead if a not in done) + (rows, share)

    shapes = [left(""), left("")]
    for i, axis in enumerate(order):
        shapes.append((sizes[axis] - 1,) + left(order[: i + 1]))
    if "m" not in lead:
        shapes.append((rows, width) if split else (sizes["m"], rows, width))
    return shapes


def scatter_steps(flow, grad, result, buffers, order, split, columns, local_sem):
    place = flow.place
    at, sizes = place.at, place.sizes
    whole_m = len(grad.shape) == 6
    lead = ("m" if whole_m else "") + "zx"
    own, core_in = buffers[:2]
    landing = dict(zip(order, buffers[2:]))
    last = buffers[-1]
    rows, width = grad.shape[-2], columns[1]
    share = width // sizes["m"] if split else width

    def lanes_of(place_m):
        return pl.ds(pl.multiple_of(place_m * share, 128), share)

    def grad_half(core):
        return grad.at[
            tuple(pl.ds(0, sizes[a]) for a in lead) + (core, pl.ds(0, rows), pl.ds(*columns))
        ]

    def view(done, **moved):
        index = tuple(
            moved[a] if a in moved else at[a] if a in done else pl.ds(0, sizes[a]) for a in lead
        )
        lanes = pl.ds(0, width)
        if split and ("m" in done or "m" in moved):
            lanes = lanes_of(moved.get("m", at["m"]))
        return own.at[index + (pl.ds(0, rows), lanes)]

    def load():
        return pltpu.make_async_copy(grad_half(at["c"]), own, local_sem)

    actions = [lambda: load().start()]
    flow.move(actions, lambda: (grad_half(1 - at["c"]), core_in, {"c": 1 - at["c"]}, core_in))
    flow.steps.append(actions)
    actions = [lambda: load().wait()] + flow.arrived() + [lambda: add_into(own, core_in)]
    done = ""
    for axis in order:
        for step in range(1, sizes[axis]):

            def make(axis=axis, step=step, done=done):
                there = place.ahead(axis, step)
                slot = landing[axis].at[step - 1]
                return (view(done, **{axis: there}), slot, {axis: there}, slot)

            flow.move(actions, make)
        flow.steps.append(actions)
        done += axis
        actions = flow.arrived()
        for step in range(1, sizes[axis]):
            actions.append(
                lambda axis=axis, step=step, done=done: add_into(
                    view(done), landing[axis].at[step - 1]
                )
            )
    block = (pl.ds(0, rows), pl.ds(*columns))
    if whole_m:

        def store():
            result[block] = view(done)[...].astype(F32)

        actions.append(store)
    elif split:

        def part(place_m):
            return last.at[pl.ds(0, rows), lanes_of(place_m)]

        def keep():
            part(at["m"])[...] = view(done)[...]

        actions.append(keep)
        for step in range(1, sizes["m"]):
            flow.move(
                actions,
                lambda step=step: (
                    part(at["m"]),
                    part(at["m"]),
                    {"m": place.ahead("m", step)},
                    part(place.behind("m", step)),
                ),
            )
        flow.steps.append(actions)
        actions = flow.arrived()

        def store():
            result[block] = last[...].astype(F32)

        actions.append(store)
    else:

        def keep():
            last[at["m"]] = view(done)[...]

        actions.append(keep)
        for step in range(1, sizes["m"]):
            flow.move(
                actions,
                lambda step=step: (
                    last.at[at["m"]],
                    last.at[at["m"]],
                    {"m": place.ahead("m", step)},
                    last.at[place.behind("m", step)],
                ),
            )
        flow.steps.append(actions)
        actions = flow.arrived()

        def store():
            total = last[0].astype(F32)
            for i in range(1, sizes["m"]):
                total = total + last[i].astype(F32)
            result[block] = total

        actions.append(store)
    flow.last = actions + flow.sent


class Gather:
    def __init__(self, sizes, arrays, units, together):
        self.sizes, self.arrays, self.units = sizes, arrays, units
        self.targets = [None] * len(arrays)
        self.starts, self.round = [], 0
        for start, count in enumerate(together):
            self.starts += [start] * count
        assert len(self.starts) == len(units)

    def ready(self, names):
        return max(
            start + len(unit[1]) + 1 for start, unit in zip(self.starts, self.units) if unit[0] in names
        )

    def until(self, end, collective_id):
        begin, self.round = self.round, max(end, self.round)
        return GatherPart(self, begin, end, collective_id) if begin < end else None


class GatherPart:
    def __init__(self, plan, begin, end, collective_id):
        self.plan, self.begin, self.end, self.collective_id = plan, begin, end, collective_id
        self.units = [
            (start, unit)
            for start, unit in zip(plan.starts, plan.units)
            if start < end and start + len(unit[1]) + 1 > begin
        ]
        self.names = sorted({unit[0] for _, unit in self.units})
        split = {unit[0]: unit[2] for _, unit in self.units}
        order = {unit[0]: unit[1] for _, unit in self.units}
        sizes = plan.sizes
        anywhere = pl.BlockSpec(memory_space=pl.ANY)
        old = [n for n in self.names if plan.targets[n] is not None]
        self.arrays = [plan.arrays[n] for n in self.names] + [plan.targets[n] for n in old]
        self.specs = [anywhere] * len(self.arrays)
        self.out_shape = [
            jax.ShapeDtypeStruct(
                ((sizes["m"],) if "m" in order[n] and not split[n] else ())
                + (sizes["z"], 2, 2)
                + plan.arrays[n].shape,
                plan.arrays[n].dtype,
            )
            for n in self.names
        ]
        self.out_specs = [anywhere] * len(self.names)
        self.aliases = {len(self.names) + i: self.names.index(n) for i, n in enumerate(old)}
        pairs = len(self.units) * (sum(sizes.values()) - 4)
        self.scratch = [
            pltpu.SemaphoreType.DMA((pairs,)),
            pltpu.SemaphoreType.DMA((pairs,)),
            pltpu.SemaphoreType.DMA((len(self.units),)),
        ]

    def rounds(self, ins, outs, scratch):
        place = Place(self.plan.sizes)
        send, recv, local = scratch
        taken = [0]
        rounds = [[] for _ in range(self.end - self.begin)]
        last = []
        for i, (start, (n, order, split, columns)) in enumerate(self.units):
            flow = Flow(place, send, recv, taken)
            begin = max(self.begin - start, 0)
            slot = self.names.index(n)
            gather_steps(
                flow, ins[slot], outs[slot], order, split, columns, local.at[i], begin, self.end - start
            )
            for step, actions in enumerate(flow.steps):
                rounds[start + begin + step - self.begin] += actions
            last += flow.last
        rounds[0].insert(0, place.greet)
        return rounds, last

    def received(self, outs):
        for n, out in zip(self.names, outs):
            self.plan.targets[n] = out


class Scatter:
    aliases = {}

    def __init__(self, sizes, arrays, units, together, collective_id):
        self.sizes, self.arrays, self.units = sizes, arrays, units
        self.collective_id = collective_id
        self.starts = []
        for start, count in enumerate(together):
            self.starts += [start] * count
        assert len(self.starts) == len(units)
        self.specs = [pl.BlockSpec(memory_space=pl.ANY)] * len(arrays)
        self.out_shape = [jax.ShapeDtypeStruct(a.shape[-2:], F32) for a in arrays]
        self.out_specs = [
            pl.BlockSpec(a.shape[-2:], lambda *_: (0, 0), pipeline_mode=pl.Buffered(1)) for a in arrays
        ]
        buffers = []
        for i, order, split, columns in units:
            buffers += [
                pltpu.VMEM(shape, arrays[i].dtype)
                for shape in scatter_shapes(arrays[i].shape, order, split, columns, sizes)
            ]
        pairs = len(units) * (sum(sizes.values()) - 4 + sizes["m"] - 1)
        self.scratch = buffers + [
            pltpu.SemaphoreType.DMA((pairs,)),
            pltpu.SemaphoreType.DMA((pairs,)),
            pltpu.SemaphoreType.DMA((len(units),)),
        ]

    def rounds(self, ins, outs, scratch):
        place = Place(self.sizes)
        send, recv, local = scratch[-3:]
        buffers = list(scratch[:-3])
        taken, flows, last = [0], [], []
        for unit, (i, order, split, columns) in enumerate(self.units):
            flow = Flow(place, send, recv, taken)
            count = len(scatter_shapes(ins[i].shape, order, split, columns, self.sizes))
            mine, buffers = buffers[:count], buffers[count:]
            scatter_steps(flow, ins[i], outs[i], mine, order, split, columns, local.at[unit])
            flows.append(flow)
        rounds = [[] for _ in range(max(s + len(f.steps) for s, f in zip(self.starts, flows)) + 1)]
        for start, flow in zip(self.starts, flows):
            for i, actions in enumerate(flow.steps + [flow.last]):
                rounds[start + i] += actions
        rounds[0].insert(0, place.greet)
        return rounds[:-1], rounds[-1]

    def received(self, outs):
        self.sums = outs


def run_all(actions):
    for action in actions:
        action()


def run_kernel(
    body, args, *, grid, in_specs, out_specs, out_shape, name, scratch_shapes=(), exchange=None, polls=1
):
    if exchange is None:
        return pl.pallas_call(
            functools.partial(body, lambda: None),
            grid=grid,
            in_specs=in_specs,
            out_specs=out_specs,
            out_shape=out_shape,
            scratch_shapes=scratch_shapes,
            compiler_params=pltpu.CompilerParams(vmem_limit_bytes=VMEM_LIMIT),
            name=name,
        )(*args)
    counts = (len(args), len(exchange.arrays), len(out_shape), len(exchange.out_shape))
    total = functools.reduce(lambda a, b: a * b, grid, 1)

    def kernel(*refs):
        refs = list(refs)
        ins, sent, outs, received = [[refs.pop(0) for _ in range(n)] for n in counts]
        own = [refs.pop(0) for _ in range(len(scratch_shapes))]
        step = 0
        for i, size in enumerate(grid):
            step = step * size + pl.program_id(i)
        rounds, last = exchange.rounds(sent, received, refs)
        slots = {}
        for i, actions in enumerate(rounds):
            slot = i * total * polls // len(rounds)
            slots.setdefault((slot % polls, slot // polls), []).extend(actions)
        called = [0]

        def poll():
            for at_step in range(total):
                actions = slots.get((called[0], at_step))
                if actions:
                    pl.when(step == at_step)(functools.partial(run_all, actions))
            called[0] += 1

        body(poll, *ins, *outs, *own)
        assert called[0] == polls
        pl.when(step == total - 1)(functools.partial(run_all, last))

    outs = pl.pallas_call(
        kernel,
        grid=grid,
        in_specs=list(in_specs) + exchange.specs,
        out_specs=list(out_specs) + exchange.out_specs,
        out_shape=list(out_shape) + exchange.out_shape,
        scratch_shapes=list(scratch_shapes) + exchange.scratch,
        input_output_aliases={counts[0] + i: counts[2] + o for i, o in exchange.aliases.items()},
        compiler_params=pltpu.CompilerParams(
            vmem_limit_bytes=VMEM_LIMIT,
            collective_id=exchange.collective_id,
            has_side_effects=True,
        ),
        name=name,
    )(*args, *exchange.arrays)
    exchange.received(outs[counts[2] :])
    return outs[: counts[2]]


def exchange_alone(exchange, name):
    run_kernel(
        lambda poll: poll(), [], grid=(1,), in_specs=[], out_specs=[], out_shape=[], name=name,
        exchange=exchange,
    )


HEAD = 128
BLOCK = 512
EPS = 1e-06
NEGATIVE = -1e30
GELU_C = 0.7978845608
GELU_K = 0.044715
SCALE = HEAD**-0.5
LOG2E = 1.4426950408889634
PAIR = 2 * HEAD
TILE = 256


def matmul(left, right):
    return jnp.dot(left, right, preferred_element_type=F32)


def matmul_nt(left, right):
    return lax.dot_general(left, right, (((1,), (1,)), ((), ())), preferred_element_type=F32)


def inverse_rms(values):
    return lax.rsqrt(jnp.mean(values * values, axis=-1, keepdims=True) + EPS)


def rms_backward(values, gain, grad):
    inverse = inverse_rms(values)
    unit = values * inverse
    weighted = grad * gain
    inner = jnp.mean(weighted * unit, axis=-1, keepdims=True)
    return inverse * (weighted - unit * inner), grad * unit


def whole(shape):
    return pl.BlockSpec(shape, lambda *_: (0,) * len(shape))


def project_kernel(poll, x_ref, gain_ref, wq, wk, wv, normed, q, k, v):
    @pl.when(pl.program_id(0) == 0)
    def _():
        x = x_ref[...].astype(F32)
        normed[...] = (x * inverse_rms(x) * gain_ref[...]).astype(BF16)

    poll()
    rows = normed[...]
    for weight, out in ((wq, q), (wk, k), (wv, v)):
        out[...] = matmul(rows, weight[...]).astype(BF16)


def project(x, gain, weights, exchange):
    rows, width = x.shape
    tile = pl.BlockSpec((width, TILE), lambda j: (0, j))
    out = pl.BlockSpec((rows, TILE), lambda j: (0, j))
    return run_kernel(
        project_kernel,
        (x, gain, *weights),
        grid=(width // TILE,),
        in_specs=[whole((rows, width)), whole((1, width)), tile, tile, tile],
        out_specs=[whole((rows, width)), out, out, out],
        out_shape=[jax.ShapeDtypeStruct((rows, width), BF16)] * 4,
        name="project_tokens",
        exchange=exchange,
    )


def attend(query, pieces):
    scores = []
    for keys, _, mask in pieces:
        score = matmul_nt(keys, query) * (SCALE * LOG2E)
        scores.append(score if mask is None else jnp.where(mask, score, NEGATIVE))
    top = functools.reduce(jnp.maximum, [jnp.max(s, axis=0, keepdims=True) for s in scores])
    total, mixed = 0.0, 0.0
    for score, (_, values, _) in zip(scores, pieces):
        weights = jnp.exp2(score - top)
        total = total + jnp.sum(weights, axis=0, keepdims=True)
        mixed = mixed + matmul(values.T, weights.astype(BF16))
    return (mixed / total).T.astype(BF16), top + jnp.log2(total)


def attend_backward(query, log_total, grad, centre, pieces):
    grad_query = 0.0
    for keys, values, mask, add_keys, add_values in pieces:
        score = matmul_nt(keys, query) * (SCALE * LOG2E)
        if mask is not None:
            score = jnp.where(mask, score, NEGATIVE)
        probs = jnp.exp2(score - log_total)
        add_values(matmul(probs.astype(BF16), grad))
        grad_probs = matmul_nt(values, grad)
        grad_scores = (probs * (grad_probs - centre)).astype(BF16)
        add_keys(matmul(grad_scores, query) * SCALE)
        grad_query = grad_query + matmul(keys.T, grad_scores)
    return (grad_query * SCALE).T


def centre_of(grad, mixed):
    return jnp.sum((grad.astype(F32) * mixed.astype(F32)).T, axis=0, keepdims=True)


def position(shape, axis):
    return lax.broadcasted_iota(jnp.int32, shape, axis)


def token_pieces(block, half, valid):
    key = position((TILE, TILE), 0)
    query = position((TILE, TILE), 1)
    causal, recent = key <= query, key > query
    pieces = []
    if block:
        start = (block - 1) * BLOCK
        pieces.append(("near", start + half * TILE, TILE, recent))
        if half == 0:
            pieces.append(("near", start + TILE, TILE, None))
    start = block * BLOCK
    for piece in range(half + 1):
        first = start + piece * TILE
        seen = first + key < valid
        mask = causal if piece == half else None
        if block:
            mask = seen if mask is None else mask & seen
        pieces.append(("near", first, TILE, mask))
    pieces.append(("state", block * BLOCK, BLOCK, None))
    return pieces


def state_forward_kernel(
    poll, valid, s0, gain, gate_bias, wq, wk, wv, wu, k, v,
    normed_out, sq, sk, sv, read, log_out, update_out, states, last,
    state, normed, total,
):
    block, pair = pl.program_id(0), pl.program_id(1)

    @pl.when((block == 0) & (pair == 0))
    def _():
        state[...] = s0[...].astype(F32)

    @pl.when(pair == 0)
    def _():
        now = state[...]
        rows = (now * inverse_rms(now) * gain[...]).astype(BF16)
        normed[...] = rows
        normed_out[...] = rows
        states[...] = now
        total[...] = jnp.zeros_like(total)

    poll()
    rows = normed[...]
    for weight, out in ((wq, sq), (wk, sk), (wv, sv)):
        out[...] = matmul(rows, weight[...]).astype(BF16)
    seen = block * BLOCK + position((BLOCK, BLOCK), 0) < valid[0]
    for head in range(2):
        lanes = pl.ds(head * HEAD, HEAD)
        read[:, lanes], log_out[0, 0, pl.ds(head, 1), :] = attend(
            sq[:, lanes], [(k[:, lanes], v[:, lanes], seen)]
        )
    total[...] += matmul(read[...], wu[...])

    @pl.when(pair == pl.num_programs(1) - 1)
    def _():
        update = total[...]
        gate = 1.0 / (1.0 + jnp.exp(-gate_bias[...]))
        later = gate * state[...] + (1.0 - gate) * update
        update_out[...] = update
        state[...] = later
        last[...] = later.astype(BF16)


def state_forward(valid, s0, gain, gate_bias, weights, update_weight, k, v, exchange):
    rows, width = s0.shape
    blocks, pairs = k.shape[0] // BLOCK, width // PAIR
    columns = pl.BlockSpec((width, PAIR), lambda b, p: (0, p))
    tile = pl.BlockSpec((rows, PAIR), lambda b, p: (b, p))
    band = pl.BlockSpec((rows, width), lambda b, p: (b, 0))
    small = whole((1, width))

    def stack(kind):
        return jax.ShapeDtypeStruct((blocks * rows, width), kind)

    return run_kernel(
        state_forward_kernel,
        (valid, s0, gain, gate_bias, *weights, update_weight, k, v),
        grid=(blocks, pairs),
        in_specs=[
            pl.BlockSpec(memory_space=pltpu.SMEM), whole((rows, width)), small, small,
            columns, columns, columns, pl.BlockSpec((PAIR, width), lambda b, p: (p, 0)),
            pl.BlockSpec((BLOCK, PAIR), lambda b, p: (b, p)),
            pl.BlockSpec((BLOCK, PAIR), lambda b, p: (b, p)),
        ],
        out_specs=[
            band, tile, tile, tile, tile,
            pl.BlockSpec((1, 1, 2, rows), lambda b, p: (b, p, 0, 0)),
            band, band, whole((rows, width)),
        ],
        out_shape=[
            stack(BF16), stack(BF16), stack(BF16), stack(BF16), stack(BF16),
            jax.ShapeDtypeStruct((blocks, pairs, 2, rows), F32),
            stack(F32), stack(F32), jax.ShapeDtypeStruct((rows, width), BF16),
        ],
        scratch_shapes=[
            pltpu.VMEM((rows, width), F32), pltpu.VMEM((rows, width), BF16),
            pltpu.VMEM((rows, width), F32),
        ],
        name="state_forward",
        exchange=exchange,
    )


def token_forward_kernel(
    poll, valid, x, gain, q, k, v, sk, sv, wo, mixed, log_out, resid, ynorm
):
    pair = pl.program_id(0)

    @pl.when(pair == 0)
    def _():
        resid[...] = x[...].astype(F32)

    count = valid[0]
    for head in range(2):
        poll()
        lanes = pl.ds(head * HEAD, HEAD)
        for block in range(q.shape[0] // BLOCK):
            for half in range(BLOCK // TILE):
                rows = pl.ds(block * BLOCK + half * TILE, TILE)
                pieces = []
                for kind, first, size, mask in token_pieces(block, half, count):
                    keys, values = (k, v) if kind == "near" else (sk, sv)
                    there = pl.ds(first, size)
                    pieces.append((keys[there, lanes], values[there, lanes], mask))
                mixed[rows, lanes], log_out[0, pl.ds(head, 1), rows] = attend(
                    q[rows, lanes], pieces
                )
    resid[...] += matmul(mixed[...], wo[...])

    @pl.when(pair == pl.num_programs(0) - 1)
    def _():
        rows = resid[...]
        ynorm[...] = (rows * inverse_rms(rows) * gain[...]).astype(BF16)


def token_forward(valid, x, gain, q, k, v, sk, sv, wo, exchange):
    rows, width = x.shape
    pairs = width // PAIR
    tile = pl.BlockSpec((rows, PAIR), lambda p: (0, p))
    states = pl.BlockSpec((sk.shape[0], PAIR), lambda p: (0, p))
    return run_kernel(
        token_forward_kernel,
        (valid, x, gain, q, k, v, sk, sv, wo),
        grid=(pairs,),
        in_specs=[
            pl.BlockSpec(memory_space=pltpu.SMEM), whole((rows, width)), whole((1, width)),
            tile, tile, tile, states, states, pl.BlockSpec((PAIR, width), lambda p: (p, 0)),
        ],
        out_specs=[
            tile, pl.BlockSpec((1, 2, rows), lambda p: (p, 0, 0)),
            whole((rows, width)), whole((rows, width)),
        ],
        out_shape=[
            jax.ShapeDtypeStruct((rows, width), BF16),
            jax.ShapeDtypeStruct((pairs, 2, rows), F32),
            jax.ShapeDtypeStruct((rows, width), F32),
            jax.ShapeDtypeStruct((rows, width), BF16),
        ],
        name="token_forward",
        exchange=exchange,
        polls=2,
    )


def feed_forward_kernel(
    first, final, poll, valid, ynorm, cot, total_in, grad_in, up_w, down_w,
    out, grad_out, up_grad, down_grad,
    ynorm_t, masked, masked_t, total, grad_total, sems,
):
    step, last = pl.program_id(0), pl.num_programs(0) - 1
    loads = [pltpu.make_async_copy(total_in, total, sems.at[0])]
    stores = [pltpu.make_async_copy(grad_total, grad_out, sems.at[1])]
    if not first:
        loads.append(pltpu.make_async_copy(grad_in, grad_total, sems.at[1]))
    if not final:
        stores.append(pltpu.make_async_copy(total, out, sems.at[0]))

    poll()

    @pl.when(step == 0)
    def _():
        for copy in loads:
            copy.start()
        keep = position(cot.shape, 0) < valid[0]
        grad = jnp.where(keep, cot[...], jnp.zeros_like(cot))
        masked[...] = grad
        masked_t[...] = grad.T
        ynorm_t[...] = ynorm[...].T
        if first:
            grad_total[...] = jnp.zeros_like(grad_total)

    up_part, down_part = up_w[0], down_w[0]
    up = matmul(ynorm[...], up_part)
    grad_hidden = matmul(masked[...], down_part)
    square = up * up
    bent = jnp.tanh(GELU_C * (up + GELU_K * square * up))
    hidden = (0.5 * up * (1.0 + bent)).astype(BF16)
    slope = 0.5 * (1.0 + bent) + 0.5 * up * (1.0 - bent * bent) * (
        GELU_C * (1.0 + 3.0 * GELU_K * square)
    )
    grad_up = (grad_hidden * slope).astype(BF16)
    poll()
    down_grad[0] = matmul(masked_t[...], hidden).astype(BF16)
    up_grad[0] = matmul(ynorm_t[...], grad_up).astype(BF16)

    @pl.when(step == 0)
    def _():
        for copy in loads:
            copy.wait()

    total[...] += matmul_nt(hidden, down_part)
    grad_total[...] += matmul_nt(grad_up, up_part)

    @pl.when(step == last)
    def _():
        for copy in stores:
            copy.start()
        if final:
            out[...] = total[...].astype(BF16)
        for copy in stores:
            copy.wait()


def feed_forward(first, final, valid, ynorm, cot, total, grad, up_w, down_w, exchange, chunk=512):
    rows, width = ynorm.shape
    parts, _, part = up_w.shape
    chunk = min(chunk, part)
    each = part // chunk
    weight = pl.BlockSpec((1, width, chunk), lambda j: (j // each, 0, j % each))
    once = pl.BlockSpec((rows, width), lambda j: (0, 0), pipeline_mode=pl.Buffered(1))
    anywhere = pl.BlockSpec(memory_space=pl.ANY)
    return run_kernel(
        functools.partial(feed_forward_kernel, first, final),
        (valid, ynorm, cot, total, grad, up_w, down_w),
        grid=(parts * each,),
        in_specs=[
            pl.BlockSpec(memory_space=pltpu.SMEM), once, once, anywhere, anywhere, weight, weight
        ],
        out_specs=[once if final else anywhere, anywhere, weight, weight],
        out_shape=[
            jax.ShapeDtypeStruct((rows, width), BF16 if final else F32),
            jax.ShapeDtypeStruct((rows, width), F32),
            jax.ShapeDtypeStruct(up_w.shape, BF16),
            jax.ShapeDtypeStruct(down_w.shape, BF16),
        ],
        scratch_shapes=[
            pltpu.VMEM((width, rows), BF16), pltpu.VMEM((rows, width), BF16),
            pltpu.VMEM((width, rows), BF16), pltpu.VMEM((rows, width), F32),
            pltpu.VMEM((rows, width), F32), pltpu.SemaphoreType.DMA((2,)),
        ],
        name="feed_forward_final" if final else "feed_forward_first",
        exchange=exchange,
        polls=2,
    )


def token_backward_kernel(
    poll, valid, resid, gain, cot, grad_ynorm, q, k, v, sk, sv, wo, mixed, log_total,
    grad_resid, gain_grad, dq, dk, dv, dsk, dsv, wo_grad,
    rounded, grad_mixed, near_k, near_v, state_k, state_v,
):
    poll()

    @pl.when(pl.program_id(0) == 0)
    def _():
        grad, gain_rows = rms_backward(resid[...], gain[...], grad_ynorm[...])
        keep = position(cot.shape, 0) < valid[0]
        grad = jnp.where(keep, cot[...].astype(F32), 0.0) + grad
        grad_resid[...] = grad
        rounded[...] = grad.astype(BF16)
        gain_grad[...] = jnp.sum(gain_rows, axis=0, keepdims=True)

    grad_rows = rounded[...]
    grad_mixed[...] = matmul_nt(grad_rows, wo[...]).astype(BF16)
    wo_grad[...] = matmul(mixed[...].T, grad_rows).astype(BF16)
    for ref in (near_k, near_v, state_k, state_v):
        ref[...] = jnp.zeros_like(ref)
    count = valid[0]
    for head in range(2):
        poll()
        lanes = pl.ds(head * HEAD, HEAD)

        def adder(ref, there):
            def add(term):
                ref[there, lanes] += term

            return add

        for block in range(q.shape[0] // BLOCK):
            for half in range(BLOCK // TILE):
                rows = pl.ds(block * BLOCK + half * TILE, TILE)
                pieces = []
                for kind, first, size, mask in token_pieces(block, half, count):
                    keys, values = (k, v) if kind == "near" else (sk, sv)
                    sums = (near_k, near_v) if kind == "near" else (state_k, state_v)
                    there = pl.ds(first, size)
                    pieces.append(
                        (keys[there, lanes], values[there, lanes], mask)
                        + tuple(adder(ref, there) for ref in sums)
                    )
                out_grad = grad_mixed[rows, lanes]
                dq[rows, lanes] = attend_backward(
                    q[rows, lanes],
                    log_total[0, pl.ds(head, 1), rows],
                    out_grad,
                    centre_of(out_grad, mixed[rows, lanes]),
                    pieces,
                ).astype(BF16)
    dk[...] = near_k[...]
    dv[...] = near_v[...]
    dsk[...] = state_k[...].astype(BF16)
    dsv[...] = state_v[...].astype(BF16)


def token_backward(
    valid, resid, gain, cot, grad_ynorm, q, k, v, sk, sv, wo, mixed, log_total, exchange
):
    rows, width = resid.shape
    once = pl.BlockSpec((rows, width), lambda p: (0, 0), pipeline_mode=pl.Buffered(1))
    pairs = width // PAIR
    tile = pl.BlockSpec((rows, PAIR), lambda p: (0, p))
    states = pl.BlockSpec((sk.shape[0], PAIR), lambda p: (0, p))
    band = pl.BlockSpec((PAIR, width), lambda p: (p, 0))
    return run_kernel(
        token_backward_kernel,
        (valid, resid, gain, cot, grad_ynorm, q, k, v, sk, sv, wo, mixed, log_total),
        grid=(pairs,),
        in_specs=[
            pl.BlockSpec(memory_space=pltpu.SMEM), once, whole((1, width)), once, once,
            tile, tile, tile, states, states, band, tile,
            pl.BlockSpec((1, 2, rows), lambda p: (p, 0, 0)),
        ],
        out_specs=[once, whole((1, width)), tile, tile, tile, states, states, band],
        out_shape=[
            jax.ShapeDtypeStruct((rows, width), F32),
            jax.ShapeDtypeStruct((1, width), F32),
            jax.ShapeDtypeStruct((rows, width), BF16),
            jax.ShapeDtypeStruct((rows, width), F32),
            jax.ShapeDtypeStruct((rows, width), F32),
            jax.ShapeDtypeStruct(sk.shape, BF16),
            jax.ShapeDtypeStruct(sk.shape, BF16),
            jax.ShapeDtypeStruct((width, width), BF16),
        ],
        scratch_shapes=[
            pltpu.VMEM((rows, width), BF16),
            pltpu.VMEM((rows, PAIR), BF16), pltpu.VMEM((rows, PAIR), F32),
            pltpu.VMEM((rows, PAIR), F32), pltpu.VMEM((sk.shape[0], PAIR), F32),
            pltpu.VMEM((sk.shape[0], PAIR), F32),
        ],
        name="token_backward",
        exchange=exchange,
        polls=3,
    )


def state_backward_kernel(
    poll, valid, cot, gain, gate_bias, wq, wk, wv, wu, states, updates,
    sq, k, v, read, log_total, near_k, near_v, dsk, dsv,
    dsq, dk, dv, dz_out, grad_state, gain_grad, bias_grad,
    later, dz, total, grad_read, sum_q, sum_k, sum_v,
):
    step, pair = pl.program_id(0), pl.program_id(1)
    block = pl.num_programs(0) - 1 - step
    gate = 1.0 / (1.0 + jnp.exp(-gate_bias[...]))

    @pl.when((step == 0) & (pair == 0))
    def _():
        later[...] = cot[...].astype(F32)
        gain_grad[...] = jnp.zeros_like(gain_grad)
        bias_grad[...] = jnp.zeros_like(bias_grad)

    @pl.when(pair == 0)
    def _():
        grad = later[...]
        rounded = (grad * (1.0 - gate)).astype(BF16)
        dz[...] = rounded
        dz_out[...] = rounded
        bias_grad[...] += (
            jnp.sum(grad * (states[...] - updates[...]), axis=0, keepdims=True) * gate * (1.0 - gate)
        )
        total[...] = jnp.zeros_like(total)

    poll()
    grad_read[...] = matmul_nt(dz[...], wu[...]).astype(BF16)
    seen = block * BLOCK + position((BLOCK, BLOCK), 0) < valid[0]
    sum_k[...] = near_k[...]
    sum_v[...] = near_v[...]
    for head in range(2):
        lanes = pl.ds(head * HEAD, HEAD)

        def adder(ref):
            def add(term):
                ref[:, lanes] += term

            return add

        out_grad = grad_read[:, lanes]
        dsq[:, lanes] = attend_backward(
            sq[:, lanes],
            log_total[0, 0, pl.ds(head, 1), :],
            out_grad,
            centre_of(out_grad, read[:, lanes]),
            [(k[:, lanes], v[:, lanes], seen, adder(sum_k), adder(sum_v))],
        ).astype(BF16)
    dk[...] = sum_k[...].astype(BF16)
    dv[...] = sum_v[...].astype(BF16)
    total[...] += (
        matmul_nt(dsq[...], wq[...]) + matmul_nt(dsk[...], wk[...]) + matmul_nt(dsv[...], wv[...])
    )

    @pl.when(pair == pl.num_programs(1) - 1)
    def _():
        grad, gain_rows = rms_backward(states[...], gain[...], total[...])
        grad = later[...] * gate + grad
        later[...] = grad
        grad_state[...] = grad
        gain_grad[...] += jnp.sum(gain_rows, axis=0, keepdims=True)


def state_backward(
    valid, cot, gain, gate_bias, weights, update_weight, states, updates,
    sq, k, v, read, log_total, near_k, near_v, dsk, dsv, exchange,
):
    rows, width = cot.shape
    blocks, pairs = k.shape[0] // BLOCK, width // PAIR
    columns = pl.BlockSpec((width, PAIR), lambda s, p: (0, p))
    tile = pl.BlockSpec((rows, PAIR), lambda s, p: (blocks - 1 - s, p))
    token = pl.BlockSpec((BLOCK, PAIR), lambda s, p: (blocks - 1 - s, p))
    band = pl.BlockSpec((rows, width), lambda s, p: (blocks - 1 - s, 0))
    small = whole((1, width))
    return run_kernel(
        state_backward_kernel,
        (
            valid, cot, gain, gate_bias, *weights, update_weight, states, updates,
            sq, k, v, read, log_total, near_k, near_v, dsk, dsv,
        ),
        grid=(blocks, pairs),
        in_specs=[
            pl.BlockSpec(memory_space=pltpu.SMEM), whole((rows, width)), small, small,
            columns, columns, columns, pl.BlockSpec((PAIR, width), lambda s, p: (p, 0)),
            band, band, tile, token, token, tile,
            pl.BlockSpec((1, 1, 2, rows), lambda s, p: (blocks - 1 - s, p, 0, 0)),
            token, token, tile, tile,
        ],
        out_specs=[tile, token, token, band, whole((rows, width)), small, small],
        out_shape=[
            jax.ShapeDtypeStruct((blocks * rows, width), BF16),
            jax.ShapeDtypeStruct(k.shape, BF16),
            jax.ShapeDtypeStruct(k.shape, BF16),
            jax.ShapeDtypeStruct((blocks * rows, width), BF16),
            jax.ShapeDtypeStruct((rows, width), F32),
            jax.ShapeDtypeStruct((1, width), F32),
            jax.ShapeDtypeStruct((1, width), F32),
        ],
        scratch_shapes=[
            pltpu.VMEM((rows, width), F32), pltpu.VMEM((rows, width), BF16),
            pltpu.VMEM((rows, width), F32), pltpu.VMEM((rows, PAIR), BF16),
            pltpu.VMEM((rows, PAIR), F32), pltpu.VMEM((BLOCK, PAIR), F32),
            pltpu.VMEM((BLOCK, PAIR), F32),
        ],
        name="state_backward",
        exchange=exchange,
    )


def weight_grad_kernel(counts, poll, *refs):
    refs = list(refs)
    lefts = [refs.pop(0) for _ in counts]
    rights = [[refs.pop(0) for _ in range(n)] for n in counts]
    outs = [[refs.pop(0) for _ in range(n)] for n in counts]
    poll()

    @pl.when(pl.program_id(0) == 0)
    def _():
        for left, left_t in zip(lefts, refs):
            left_t[...] = left[...].T

    for left_t, group, out_group in zip(refs, rights, outs):
        for right, out in zip(group, out_group):
            out[...] = matmul(left_t[...], right[...]).astype(BF16)


def weight_grad(pairs, name, exchange):
    lefts = [left for left, _ in pairs]
    rights = [right for _, group in pairs for right in group]
    rows, width = lefts[0].shape
    tile = pl.BlockSpec((rows, TILE), lambda j: (0, j))
    out = pl.BlockSpec((width, TILE), lambda j: (0, j))
    return run_kernel(
        functools.partial(weight_grad_kernel, [len(group) for _, group in pairs]),
        (*lefts, *rights),
        grid=(width // TILE,),
        in_specs=[whole((rows, width))] * len(lefts) + [tile] * len(rights),
        out_specs=[out] * len(rights),
        out_shape=[jax.ShapeDtypeStruct((width, width), BF16)] * len(rights),
        scratch_shapes=[pltpu.VMEM((width, rows), BF16)] * len(lefts),
        name=name,
        exchange=exchange,
    )


def token_grad_kernel(
    poll, x, gain, grad_resid, dq, dk, dv, wq, wk, wv, normed, dq_tile, dk_tile, dv_tile,
    grad_x, gain_grad, wq_grad, wk_grad, wv_grad, normed_t,
):
    poll()

    @pl.when(pl.program_id(0) == 0)
    def _():
        gain_grad[...] = jnp.zeros_like(gain_grad)
        normed_t[...] = normed[...].T

    for right, out in ((dq_tile, wq_grad), (dk_tile, wk_grad), (dv_tile, wv_grad)):
        out[...] = matmul(normed_t[...], right[...]).astype(BF16)
    poll()
    grad_normed = (
        matmul_nt(dq[...], wq[...]) + matmul_nt(dk[...], wk[...]) + matmul_nt(dv[...], wv[...])
    )
    grad, gain_rows = rms_backward(x[...].astype(F32), gain[...], grad_normed)
    grad_x[...] = grad_resid[...] + grad
    gain_grad[...] += jnp.sum(gain_rows, axis=0, keepdims=True)


def token_grad(x, gain, grad_resid, grads, weights, normed, exchange):
    rows, width = x.shape
    band = pl.BlockSpec((TILE, width), lambda i: (i, 0))
    tile = pl.BlockSpec((rows, TILE), lambda i: (0, i))
    out = pl.BlockSpec((width, TILE), lambda i: (0, i))
    weight = pl.BlockSpec((width, width), lambda i: (0, 0), pipeline_mode=pl.Buffered(1))
    return run_kernel(
        token_grad_kernel,
        (x, gain, grad_resid, *grads, *weights, normed, *grads),
        grid=(rows // TILE,),
        in_specs=[band, whole((1, width)), band, band, band, band, weight, weight, weight]
        + [weight, tile, tile, tile],
        out_specs=[band, whole((1, width)), out, out, out],
        out_shape=[
            jax.ShapeDtypeStruct((rows, width), F32), jax.ShapeDtypeStruct((1, width), F32)
        ]
        + [jax.ShapeDtypeStruct((width, width), BF16)] * 3,
        scratch_shapes=[pltpu.VMEM((width, rows), BF16)],
        name="token_grad",
        exchange=exchange,
        polls=2,
    )


def cut(width, pieces):
    return [(i * width // pieces, width // pieces) for i in range(pieces)]


def plan_gather(sizes, small, square, forward):
    width, part = square[0].shape[1], forward[0].shape[1]
    arrays = [small] + square + forward
    pieces = cut(width, SQUARE_PIECES)
    can_share = pieces[0][1] // sizes["m"] % 128 == 0
    lone = [
        (1 + i, columns)
        for trio in ((0, 1, 2), (3, 4, 5), (6, 7))
        for columns in pieces
        for i in trio
    ]
    units, together = [(0, "zx", False, (0, small.shape[1]))], [4]
    for n, (i, columns) in enumerate(lone):
        shared = can_share and n % 3 > 0
        units.append((i, "zxm" if shared else "zx", shared, columns))
        if n % 3 == 0 and n:
            together.append(0)
        if n >= 3:
            together[-1] += 1
    for i in range(4):
        for columns in cut(part, FORWARD_PIECES):
            units.append((9 + i, "zmx" if len(units) % 2 else "zxm", False, columns))
        together += [2] * (FORWARD_PIECES // 2)
    return Gather(sizes, arrays, units, together)


def plan_scatter(sizes, arrays, pieces, collective_id, group):
    units = []
    for columns in range(pieces):
        for i, array in enumerate(arrays):
            width = array.shape[-1]
            if array.dtype == F32:
                if columns == 0:
                    units.append((i, "xz", False, (0, width)))
                continue
            there = cut(width, pieces)[columns]
            if array.ndim == 6:
                units.append((i, ("mxz", "xmz")[len(units) % 2], False, there))
            else:
                shared = len(units) % 3 > 0 and there[1] // sizes["m"] % 128 == 0
                units.append((i, "mxz" if shared else "xz", shared, there))
    together = [group] * (len(units) // group)
    if len(units) % group:
        together.append(len(units) % group)
    return Scatter(sizes, arrays, units, together, collective_id)


def shards(
    mlp_size,
    tokens,
    initial_state,
    valid,
    token_query_weight,
    token_key_weight,
    token_value_weight,
    token_output_weight,
    state_query_weight,
    state_key_weight,
    state_value_weight,
    state_update_weight,
    up_projection_weight,
    down_projection_weight,
    token_norm_gain,
    state_norm_gain,
    feedforward_norm_gain,
    state_gate_bias,
    output_cotangent,
    final_state_cotangent,
):
    rows = token_query_weight.shape[0]
    width = tokens.shape[2]
    seg_size = width // rows
    sizes = {"z": seg_size // 4, "x": 2, "c": 2, "m": mlp_size}
    half = up_projection_weight.shape[1] // 2
    small = jnp.concatenate(
        [token_norm_gain, state_norm_gain, feedforward_norm_gain, state_gate_bias]
    ).reshape(-1, 128)
    small = jnp.pad(small, ((0, 16 - small.shape[0]), (0, 0)))
    square = [
        token_query_weight,
        token_key_weight,
        token_value_weight,
        state_query_weight,
        state_key_weight,
        state_value_weight,
        state_update_weight,
        token_output_weight,
    ]
    forward = [
        weight[:, first : first + half]
        for first in (0, half)
        for weight in (up_projection_weight, down_projection_weight)
    ]
    plan = plan_gather(sizes, small, square, forward)
    x, s0, cot = tokens[0], initial_state[0], output_cotangent[0]

    def full(*names):
        return [plan.targets[n].reshape(width, width) for n in names]

    def forward_full(*names):
        return [plan.targets[n].reshape(mlp_size, width, half) for n in names]

    exchange_alone(plan.until(plan.ready((0, 1, 2, 3)), 1), "gather_first")
    gains = plan.targets[0].reshape(seg_size, -1)[:, : 4 * rows].reshape(seg_size, 4, rows)
    gains = gains.transpose(1, 0, 2).reshape(4, 1, width).astype(F32)
    token_gain, state_gain, mlp_gain, gate_bias = [gains[i] for i in range(4)]
    token_weights = full(1, 2, 3)
    normed, q, k, v = project(
        x, token_gain, token_weights, plan.until(plan.ready((4, 5, 6, 7)), 2)
    )
    state_weights, (wu,) = full(4, 5, 6), full(7)
    ready = plan.ready((9, 10))
    middle = max(plan.ready((8,)), (plan.round + ready) // 2)
    snormed, sq, sk, sv, read, read_log, updates, states, last = state_forward(
        valid, s0, state_gain, gate_bias, state_weights, wu, k, v, plan.until(middle, 3)
    )
    (wo,) = full(8)
    mixed, token_log, resid, ynorm = token_forward(
        valid, x, mlp_gain, q, k, v, sk, sv, wo, plan.until(ready, 4)
    )
    total, grad_total, *first_grads = feed_forward(
        True, False, valid, ynorm, cot, resid, resid, *forward_full(9, 10),
        plan.until(plan.ready((11, 12)), 5),
    )

    def parted(grads):
        shape = (seg_size // 4, 2, 2, rows)
        return [
            g.reshape((mlp_size,) + shape + (half,)) if g.ndim == 3 else g.reshape(shape + (width,))
            for g in grads
        ]

    first_sums = plan_scatter(sizes, parted(first_grads), FORWARD_PIECES, 6, 2)
    out, grad_total, *last_grads = feed_forward(
        False, True, valid, ynorm, cot, total, grad_total, *forward_full(11, 12), first_sums
    )
    last_sums = plan_scatter(sizes, parted(last_grads), FORWARD_PIECES, 7, 2)
    grad_resid, mlp_gain_grad, dq, near_k, near_v, dsk, dsv, wo_grad = token_backward(
        valid, resid, mlp_gain, cot, grad_total, q, k, v, sk, sv, wo, mixed, token_log, last_sums
    )
    out_sum = plan_scatter(sizes, parted([wo_grad]), SQUARE_PIECES // 2, 8, 1)
    dsq, dk, dv, dz, grad_state, state_gain_grad, bias_grad = state_backward(
        valid, final_state_cotangent[0], state_gain, gate_bias, state_weights, wu,
        states, updates, sq, k, v, read, read_log, near_k, near_v, dsk, dsv, out_sum,
    )
    state_grads = weight_grad([(read, [dz]), (snormed, [dsq, dsk, dsv])], "weight_grad", None)
    state_sums = plan_scatter(sizes, parted(state_grads), SQUARE_PIECES // 2, 9, 4)
    grad_tokens, token_gain_grad, *token_grads = token_grad(
        x, token_gain, grad_resid, [dq, dk, dv], token_weights, normed, state_sums
    )
    small_grads = jnp.concatenate([token_gain_grad, state_gain_grad, mlp_gain_grad, bias_grad])
    small_grads = small_grads.reshape(4, seg_size, rows).transpose(1, 0, 2)
    small_grads = small_grads.reshape(seg_size, -1, 128)
    lines = small_grads.shape[1]
    small_grads = jnp.pad(small_grads, ((0, 0), (0, 8 - lines), (0, 0)))
    small_grads = small_grads.reshape(seg_size // 4, 2, 2, 8, 128)
    token_sums = plan_scatter(
        sizes, [small_grads] + parted(token_grads), SQUARE_PIECES // 2, 10, 4
    )
    exchange_alone(token_sums, "scatter_last")
    small_sum, *token_sums = token_sums.sums
    small_sum = small_sum[:lines].reshape(4, rows)
    update_sum, *state_sums = state_sums.sums
    forward_sums = [
        jnp.concatenate([a, b], axis=1) for a, b in zip(first_sums.sums, last_sums.sums)
    ]
    return (
        out[None],
        last[None],
        grad_tokens[None],
        grad_state[None],
        *token_sums,
        *out_sum.sums,
        *state_sums,
        update_sum,
        *forward_sums,
        *[small_sum[i] for i in range(4)],
    )


def solution(mesh):
    own = P(("seg", "mlp"), None, None)
    square, forward, small = P("seg", None), P("seg", "mlp"), P("seg")
    return jax.shard_map(
        functools.partial(shards, mesh.shape["mlp"]),
        mesh=mesh,
        in_specs=(own, own, P(("seg", "mlp")))
        + (square,) * 8
        + (forward,) * 2
        + (small,) * 4
        + (own, own),
        out_specs=(own,) * 4 + (square,) * 8 + (forward,) * 2 + (small,) * 4,
        check_vma=False,
    )
```

```python
import functools
import jax
import jax.numpy as jnp
from jax import lax
from jax.experimental import pallas as pl
from jax.experimental.pallas import tpu as pltpu
from jax.sharding import PartitionSpec as P

BF16 = jnp.bfloat16
F32 = jnp.float32
VMEM_LIMIT = 60 << 20
SQUARE_PIECES = 2
FORWARD_PIECES = 2
SCATTER_PIECES = 2
GATHER_SQUARE = (0, 2, 4, 5)
GATHER_FORWARD = (7, 8, 10, 11)
GATHER_MIDDLE = 10
SCATTER_ROUNDS = (3, 3, 3)
LINK_RATE = 92e3
CORE_RATE = 560e3
ROUND_COST = 2.0


class Place:
    def __init__(self, sizes):
        seg = lax.axis_index("seg")
        self.sizes = sizes
        self.at = {
            "z": lax.div(seg, 4),
            "x": lax.rem(lax.div(seg, 2), 2),
            "c": lax.rem(seg, 2),
            "m": lax.axis_index("mlp"),
        }

    def device(self, moved):
        at = {**self.at, **moved}
        return (at["z"] * 4 + at["x"] * 2 + at["c"], at["m"])

    def ahead(self, axis, step):
        return lax.rem(self.at[axis] + step, self.sizes[axis])

    def behind(self, axis, step):
        return lax.rem(self.at[axis] + self.sizes[axis] - step, self.sizes[axis])

    def greet(self):
        barrier = pltpu.get_barrier_semaphore()
        count = 0
        for axis in "zxcm":
            for step in range(1, self.sizes[axis]):
                pl.semaphore_signal(
                    barrier,
                    inc=1,
                    device_id=self.device({axis: self.ahead(axis, step)}),
                    device_id_type=pl.DeviceIdType.MESH,
                )
                count += 1
        pl.semaphore_wait(barrier, count)


class Flow:
    def __init__(self, place, send, recv, taken):
        self.place, self.send, self.recv, self.taken = place, send, recv, taken
        self.steps, self.arriving, self.sent = [], [], []

    def move(self, actions, make):
        pair = self.taken[0]
        self.taken[0] += 1

        def copy(source, target, moved):
            return pltpu.make_async_remote_copy(
                src_ref=source,
                dst_ref=target,
                send_sem=self.send.at[pair],
                recv_sem=self.recv.at[pair],
                device_id=self.place.device(moved),
                device_id_type=pl.DeviceIdType.MESH,
            )

        def outgoing():
            source, target, moved, _ = make()
            return copy(source, target, moved)

        def incoming():
            _, _, moved, landing = make()
            return copy(landing, landing, moved)

        actions.append(lambda: outgoing().start())
        self.sent.append(lambda: outgoing().wait_send())
        self.arriving.append(lambda: incoming().wait_recv())

    def arrived(self):
        waits, self.arriving = self.arriving, []
        return waits


def gather_steps(flow, source, target, order, split, columns, local_sem, begin, end):
    place = flow.place
    at, sizes = place.at, place.sizes
    lead = ("m" if len(target.shape) == 6 else "") + "zxc"
    first_column, width = columns
    share = width // sizes["m"] if split else width

    def block(done, moved):
        if not split or "m" in done:
            lanes = pl.ds(first_column, width)
        else:
            lanes = pl.ds(pl.multiple_of(first_column + moved.get("m", at["m"]) * share, 128), share)
        return (pl.ds(0, source.shape[0]), lanes)

    def view(done, **moved):
        index = tuple(
            moved[a] if a in moved else pl.ds(0, sizes[a]) if a in done else at[a] for a in lead
        )
        return target.at[index + block(done, moved)]

    def own_source():
        return source.at[block("", {})]

    def own():
        return pltpu.make_async_copy(own_source(), view(""), local_sem)

    waits = []
    for i, axis in enumerate(order + "c"):
        done = order[:i]
        if not begin <= i < end:
            continue
        actions = flow.arrived() + waits
        waits = []
        if i == 0:
            actions.append(lambda: own().start())
            waits.append(lambda: own().wait())
        for step in range(1, sizes[axis]):

            def make(axis=axis, step=step, done=done):
                return (
                    view(done) if done else own_source(),
                    view(done),
                    {axis: place.ahead(axis, step)},
                    view(done, **{axis: place.behind(axis, step)}),
                )

            flow.move(actions, make)
        flow.steps.append(actions)
    flow.last = flow.arrived() + waits + flow.sent


def add_into(total, term):
    lead = total.shape[:-2]

    def body(i, carry):
        index, rest = [], i
        for size in reversed(lead):
            index.append(lax.rem(rest, size))
            rest = lax.div(rest, size)
        there = tuple(reversed(index)) + (Ellipsis,)
        total[there] = total[there] + term[there]
        return carry

    lax.fori_loop(0, functools.reduce(lambda a, b: a * b, lead, 1), body, 0)


class ScatterUnit:
    def __init__(self, sizes, grad, order, split, columns, start):
        self.sizes, self.grad, self.order, self.split = sizes, grad, order, split
        self.columns, self.start = columns, start
        self.whole_m = grad.ndim == 6
        self.lead = ("m" if self.whole_m else "") + "zx"
        self.rows, self.width = grad.shape[-2], columns[1]
        self.share = self.width // sizes["m"] if split else self.width
        self.count = 1 + len(order) + (not self.whole_m)
        self.spec = pl.BlockSpec(memory_space=pl.ANY)
        self.state = self.result = None

    def left(self, done):
        width = self.share if "m" in done else self.width
        return tuple(self.sizes[a] for a in self.lead if a not in done) + (self.rows, width)

    def shapes(self, begin, end):
        shapes = [self.left(self.order[: max(begin - 1, 0)])]
        for i in range(begin, end):
            if i == 0:
                shapes.append(self.left(""))
            elif i <= len(self.order):
                axis = self.order[i - 1]
                shapes.append((self.sizes[axis] - 1,) + self.left(self.order[:i]))
            elif self.split:
                shapes.append((self.rows, self.width))
            else:
                shapes.append((self.sizes["m"], self.rows, self.width))
        return shapes

    def steps(self, flow, grad, state, saved, result, buffers, local_sem, begin, end):
        place, at, sizes, order = flow.place, flow.place.at, self.sizes, self.order
        own, landings = buffers[0], dict(zip(range(begin, end), buffers[1:]))
        gone = order[: max(begin - 1, 0)]
        lead = [a for a in self.lead if a not in gone]
        narrow = self.split and "m" in gone

        def lanes_of(place_m):
            return pl.ds(pl.multiple_of(place_m * self.share, 128), self.share)

        def grad_half(core):
            index = tuple(pl.ds(0, sizes[a]) for a in self.lead)
            return grad.at[index + (core, pl.ds(0, self.rows), pl.ds(*self.columns))]

        def view(done, **moved):
            index = tuple(
                moved[a] if a in moved else at[a] if a in done else pl.ds(0, sizes[a]) for a in lead
            )
            lanes = pl.ds(0, self.share if narrow else self.width)
            if self.split and not narrow and ("m" in done or "m" in moved):
                lanes = lanes_of(moved.get("m", at["m"]))
            return own.at[index + (pl.ds(0, self.rows), lanes)]

        def load():
            return pltpu.make_async_copy(grad_half(at["c"]) if begin == 0 else state, own, local_sem)

        def added(axis, done, landing):
            return [
                lambda step=step: add_into(view(done), landing.at[step - 1])
                for step in range(1, sizes[axis])
            ]

        ahead = [lambda: load().start()]
        actions = []
        if begin > 0:
            actions.append(lambda: load().wait())
        for i in range(begin, end):
            landing = landings[i]
            if i == 0:
                flow.move(
                    actions,
                    lambda landing=landing: (
                        grad_half(1 - at["c"]), landing, {"c": 1 - at["c"]}, landing
                    ),
                )
                flow.steps.append(actions)
                actions = [lambda: load().wait()] + flow.arrived()
                actions.append(lambda landing=landing: add_into(own, landing))
            elif i <= len(order):
                axis, done = order[i - 1], order[: i - 1]
                for step in range(1, sizes[axis]):

                    def make(axis=axis, step=step, done=done, landing=landing):
                        there = place.ahead(axis, step)
                        slot = landing.at[step - 1]
                        return (view(done, **{axis: there}), slot, {axis: there}, slot)

                    flow.move(actions, make)
                flow.steps.append(actions)
                actions = flow.arrived() + added(axis, order[:i], landing)
            else:

                def part(place_m, landing=landing):
                    if self.split:
                        return landing.at[pl.ds(0, self.rows), lanes_of(place_m)]
                    return landing.at[place_m]

                def keep():
                    part(at["m"])[...] = view(order)[...]

                actions.append(keep)
                for step in range(1, sizes["m"]):
                    flow.move(
                        actions,
                        lambda step=step: (
                            part(at["m"]),
                            part(at["m"]),
                            {"m": place.ahead("m", step)},
                            part(place.behind("m", step)),
                        ),
                    )
                flow.steps.append(actions)
                actions = flow.arrived()
        if end == self.count:

            def store():
                if self.whole_m:
                    total = view(order)[...].astype(F32)
                elif self.split:
                    total = landing[...].astype(F32)
                else:
                    total = landing[0].astype(F32)
                    for i in range(1, sizes["m"]):
                        total = total + landing[i].astype(F32)
                result[...] = total

            return ahead, actions + [store], flow.sent

        def save():
            return pltpu.make_async_copy(view(order[: end - 1]), saved, local_sem)

        return ahead, actions + [lambda: save().start()], flow.sent + [lambda: save().wait()]


def step_time(sizes, axis, size):
    if axis == "c":
        return size / CORE_RATE
    return 2 * size * ((sizes["z"] // 2) ** 2 if axis == "z" else sizes[axis] - 1) / LINK_RATE


def round_times(sizes, rounds):
    times = []
    for there in rounds:
        load = {axis: 0.0 for axis in "zxcm"}
        for axis, size in there:
            load[axis] += step_time(sizes, axis, size)
        times.append(max(load.values()) + ROUND_COST)
    return times


class Gather:
    def __init__(self, sizes, arrays, units):
        self.sizes, self.arrays, self.round = sizes, arrays, 0
        self.units = [unit[:-1] for unit in units]
        self.starts = [unit[-1] for unit in units]
        self.targets = [None] * len(arrays)

    def ready(self, names):
        return max(
            self.stop(start, unit) for start, unit in zip(self.starts, self.units) if unit[0] in names
        )

    def stop(self, start, unit):
        return start + len(unit[1]) + 1

    def until(self, end, collective_id):
        begin, self.round = self.round, max(end, self.round)
        return GatherPart(self, begin, end, collective_id) if begin < end else None


class GatherPart:
    def __init__(self, plan, begin, end, collective_id):
        self.plan, self.begin, self.end, self.collective_id = plan, begin, end, collective_id
        self.units = [
            (start, unit)
            for start, unit in zip(plan.starts, plan.units)
            if start < end and plan.stop(start, unit) > begin
        ]
        self.names = sorted({unit[0] for _, unit in self.units})
        split = {unit[0]: unit[2] for _, unit in self.units}
        order = {unit[0]: unit[1] for _, unit in self.units}
        sizes = plan.sizes
        anywhere = pl.BlockSpec(memory_space=pl.ANY)
        old = [n for n in self.names if plan.targets[n] is not None]
        self.arrays = [plan.arrays[n] for n in self.names] + [plan.targets[n] for n in old]
        self.specs = [anywhere] * len(self.arrays)
        self.out_shape = [
            jax.ShapeDtypeStruct(
                ((sizes["m"],) if "m" in order[n] and not split[n] else ())
                + (sizes["z"], 2, 2)
                + plan.arrays[n].shape,
                plan.arrays[n].dtype,
            )
            for n in self.names
        ]
        self.out_specs = [anywhere] * len(self.names)
        self.aliases = {len(self.names) + i: self.names.index(n) for i, n in enumerate(old)}
        pairs = len(self.units) * (sum(sizes.values()) - 4)
        self.scratch = [
            pltpu.SemaphoreType.DMA((pairs,)),
            pltpu.SemaphoreType.DMA((pairs,)),
            pltpu.SemaphoreType.DMA((len(self.units),)),
        ]

    def times(self):
        rounds = [[] for _ in range(self.end - self.begin)]
        sizes = self.plan.sizes
        for start, (n, order, split, columns) in self.units:
            size = self.plan.arrays[n].shape[0] * columns[1] * self.plan.arrays[n].dtype.itemsize
            if split:
                size //= sizes["m"]
            for i, axis in enumerate(order + "c"):
                if self.begin <= start + i < self.end:
                    rounds[start + i - self.begin].append((axis, size))
                size *= sizes[axis]
        return round_times(sizes, rounds)

    def rounds(self, ins, outs, scratch):
        place = Place(self.plan.sizes)
        send, recv, local = scratch
        taken = [0]
        rounds = [[] for _ in range(self.end - self.begin)]
        last = []
        for i, (start, (n, order, split, columns)) in enumerate(self.units):
            flow = Flow(place, send, recv, taken)
            begin, end = max(self.begin - start, 0), self.end - start
            slot = self.names.index(n)
            gather_steps(flow, ins[slot], outs[slot], order, split, columns, local.at[i], begin, end)
            for step, actions in enumerate(flow.steps):
                there = rounds[start + begin + step - self.begin]
                there.insert(0 if begin + step == 0 else len(there), actions)
            last += flow.last
        rounds = [[action for actions in there for action in actions] for there in rounds]
        rounds[0].insert(0, place.greet)
        return rounds, last

    def received(self, outs):
        for n, out in zip(self.names, outs):
            self.plan.targets[n] = out


class SmallUnit:
    def __init__(self, plan, rows, start):
        self.plan, self.grad, self.start = plan, rows, start
        self.order, self.count = "xzm", 4
        self.rows, self.width = rows.shape
        self.share = self.width
        self.spec = pl.BlockSpec(rows.shape, lambda *_: (0, 0))
        self.state = self.result = None

    def left(self, done):
        return (self.rows, self.width)

    def shapes(self, begin, end):
        sizes = self.plan.sizes
        return [self.left("")] + [(sizes[axis],) + self.left("") for axis in "c" + self.order]

    def steps(self, flow, rows, state, saved, result, buffers, local_sem, begin, end):
        place, at = flow.place, flow.place.at
        own, landings = buffers[0], buffers[1:]
        actions = []

        def fill():
            own[...] = rows[...]
            own[pl.ds(0, 1), :] = self.plan.first_row[...]

        actions.append(fill)
        for axis, landing in zip("c" + self.order, landings):

            def keep(axis=axis, landing=landing):
                landing[at[axis]] = own[...]

            actions.append(keep)
            for step in range(1, place.sizes[axis]):

                def make(axis=axis, landing=landing, step=step):
                    slot = landing.at[at[axis]]
                    return (slot, slot, {axis: place.ahead(axis, step)}, landing.at[place.behind(axis, step)])

                flow.move(actions, make)
            flow.steps.append(actions)

            def add(axis=axis, landing=landing):
                total = landing[0]
                for i in range(1, place.sizes[axis]):
                    total = total + landing[i]
                own[...] = total

            actions = flow.arrived() + [add]

        def store():
            result[...] = own[...]

        return [], actions + [store], flow.sent


class Scatter:
    def __init__(self, sizes):
        self.sizes, self.units, self.round = sizes, [], 0

    def add(self, arrays, units):
        for i, order, split, columns, start in units:
            assert start >= self.round
            self.units.append(ScatterUnit(self.sizes, arrays[i], order, split, columns, start))
        return self.units[len(self.units) - len(units) :]

    def add_small(self, rows):
        self.units.append(SmallUnit(self, rows, self.all() - 4))
        return self.units[-1]

    def all(self):
        return max(unit.start + unit.count for unit in self.units)

    def until(self, end, collective_id):
        begin, self.round = self.round, max(end, self.round)
        part = ScatterPart(self, begin, end, collective_id)
        return part if part.units else None


class ScatterPart:
    aliases = {}

    def __init__(self, plan, begin, end, collective_id):
        self.sizes, self.begin, self.end, self.collective_id = plan.sizes, begin, end, collective_id
        self.units = []
        buffers, pairs = [], 0
        self.arrays, self.out_shape, self.out_specs = [], [], []
        for unit in plan.units:
            first, stop = max(begin - unit.start, 0), min(end - unit.start, unit.count)
            if first >= stop:
                continue
            self.units.append((unit, first, stop))
            self.arrays.append(unit.state if first else unit.grad)
            if stop == unit.count:
                shape = (unit.rows, unit.width)
                self.out_shape.append(jax.ShapeDtypeStruct(shape, F32))
                self.out_specs.append(
                    pl.BlockSpec(shape, lambda *_: (0, 0), pipeline_mode=pl.Buffered(1))
                )
            else:
                shape = unit.left(unit.order[: stop - 1])
                self.out_shape.append(jax.ShapeDtypeStruct(shape, unit.grad.dtype))
                self.out_specs.append(pl.BlockSpec(memory_space=pl.ANY))
            buffers += [pltpu.VMEM(shape, unit.grad.dtype) for shape in unit.shapes(first, stop)]
            pairs += sum(self.sizes.values()) - 4 + self.sizes["m"] - 1
        self.specs = [unit.spec for unit, _, _ in self.units]
        self.scratch = buffers + [
            pltpu.SemaphoreType.DMA((pairs,)),
            pltpu.SemaphoreType.DMA((pairs,)),
            pltpu.SemaphoreType.DMA((len(self.units),)),
        ]

    def times(self):
        rounds = [[] for _ in range(self.end - self.begin)]
        for unit, first, stop in self.units:
            for i in range(first, stop):
                done = unit.order[:i]
                axis = ("c" + unit.order + "m")[i]
                shape = unit.left(done) if i <= len(unit.order) else (unit.rows, unit.share)
                size = functools.reduce(lambda a, b: a * b, shape, unit.grad.dtype.itemsize)
                rounds[unit.start + i - self.begin].append((axis, size))
        return round_times(self.sizes, rounds)

    def rounds(self, ins, outs, scratch):
        place = Place(self.sizes)
        send, recv, local = scratch[-3:]
        buffers = list(scratch[:-3])
        taken = [0]
        rounds = [[] for _ in range(self.end - self.begin)]
        start_up, ends, waits = [], [], []
        for i, (unit, first, stop) in enumerate(self.units):
            flow = Flow(place, send, recv, taken)
            count = 1 + stop - first
            mine, buffers = buffers[:count], buffers[count:]
            done = stop == unit.count
            ahead, end, wait = unit.steps(
                flow, ins[i], ins[i], None if done else outs[i], outs[i] if done else None,
                mine, local.at[i], first, stop,
            )
            if first:
                start_up += ahead
            else:
                flow.steps[0][:0] = ahead
            for step, actions in enumerate(flow.steps):
                rounds[unit.start + first + step - self.begin].append(actions)
            after = unit.start + stop - self.begin
            if after < len(rounds):
                rounds[after].append(end)
            else:
                ends += end
            waits += wait
        rounds = [[action for actions in there for action in actions] for there in rounds]
        rounds[0][:0] = start_up + [place.greet]
        return rounds, ends + waits

    def received(self, outs):
        for (unit, first, stop), out in zip(self.units, outs):
            if stop == unit.count:
                unit.result = out
            else:
                unit.state = out


def run_all(actions):
    for action in actions:
        action()


def run_kernel(
    body, args, *, grid, in_specs, out_specs, out_shape, name, scratch_shapes=(), exchange=None, polls=1,
    busy=0.0,
):
    if exchange is None:
        return pl.pallas_call(
            functools.partial(body, lambda: None),
            grid=grid,
            in_specs=in_specs,
            out_specs=out_specs,
            out_shape=out_shape,
            scratch_shapes=scratch_shapes,
            compiler_params=pltpu.CompilerParams(vmem_limit_bytes=VMEM_LIMIT),
            name=name,
        )(*args)
    counts = (len(args), len(exchange.arrays), len(out_shape), len(exchange.out_shape))
    total = functools.reduce(lambda a, b: a * b, grid, 1)
    times = exchange.times()

    def kernel(*refs):
        refs = list(refs)
        ins, sent, outs, received = [[refs.pop(0) for _ in range(n)] for n in counts]
        own = [refs.pop(0) for _ in range(len(scratch_shapes))]
        step = 0
        for i, size in enumerate(grid):
            step = step * size + pl.program_id(i)
        rounds, last = exchange.rounds(sent, received, refs)
        slots, spent, after = {}, 0.0, []
        for actions, time in zip(rounds, times):
            slot = int(total * polls * spent / busy + 0.5) if busy else total * polls
            spent += time
            if slot and slot >= total * polls:
                after += actions
            else:
                slots.setdefault((slot % polls, slot // polls), []).extend(actions)
        called = [0]

        def poll():
            for at_step in range(total):
                actions = slots.get((called[0], at_step))
                if actions:
                    pl.when(step == at_step)(functools.partial(run_all, actions))
            called[0] += 1

        body(poll, *ins, *outs, *own)
        assert called[0] == polls
        pl.when(step == total - 1)(functools.partial(run_all, after + last))

    outs = pl.pallas_call(
        kernel,
        grid=grid,
        in_specs=list(in_specs) + exchange.specs,
        out_specs=list(out_specs) + exchange.out_specs,
        out_shape=list(out_shape) + exchange.out_shape,
        scratch_shapes=list(scratch_shapes) + exchange.scratch,
        input_output_aliases={counts[0] + i: counts[2] + o for i, o in exchange.aliases.items()},
        compiler_params=pltpu.CompilerParams(
            vmem_limit_bytes=VMEM_LIMIT,
            collective_id=exchange.collective_id,
            has_side_effects=True,
        ),
        name=name,
    )(*args, *exchange.arrays)
    exchange.received(outs[counts[2] :])
    return outs[: counts[2]]


def exchange_alone(exchange, name):
    run_kernel(
        lambda poll: poll(), [], grid=(1,), in_specs=[], out_specs=[], out_shape=[], name=name,
        exchange=exchange,
    )


HEAD = 128
BLOCK = 512
EPS = 1e-06
NEGATIVE = -1e30
GELU_C = 0.7978845608
GELU_K = 0.044715
SCALE = HEAD**-0.5
LOG2E = 1.4426950408889634
PAIR = 2 * HEAD
TILE = 256


def matmul(left, right):
    return jnp.dot(left, right, preferred_element_type=F32)


def matmul_nt(left, right):
    return lax.dot_general(left, right, (((1,), (1,)), ((), ())), preferred_element_type=F32)


def inverse_rms(values):
    return lax.rsqrt(jnp.mean(values * values, axis=-1, keepdims=True) + EPS)


def rms_backward(values, gain, grad):
    inverse = inverse_rms(values)
    unit = values * inverse
    weighted = grad * gain
    inner = jnp.mean(weighted * unit, axis=-1, keepdims=True)
    return inverse * (weighted - unit * inner), grad * unit


def whole(shape):
    return pl.BlockSpec(shape, lambda *_: (0,) * len(shape))


def project_kernel(
    poll, valid, x_ref, gain_ref, cot, wq, wk, wv, normed_t, masked, masked_t, q, k, v, normed
):
    @pl.when(pl.program_id(0) == 0)
    def _():
        x = x_ref[...].astype(F32)
        rows = (x * inverse_rms(x) * gain_ref[...]).astype(BF16)
        normed[...] = rows
        normed_t[...] = rows.T
        keep = position(cot.shape, 0) < valid[0]
        grad = jnp.where(keep, cot[...], jnp.zeros_like(cot))
        masked[...] = grad
        masked_t[...] = grad.T

    rows = normed[...]
    for weight, out in ((wq, q), (wk, k), (wv, v)):
        poll()
        out[...] = matmul(rows, weight[...]).astype(BF16)


def project(valid, x, gain, cot, weights, exchange):
    rows, width = x.shape
    tile = pl.BlockSpec((width, TILE), lambda j: (0, j))
    out = pl.BlockSpec((rows, TILE), lambda j: (0, j))
    full = whole((rows, width))
    turned = whole((width, rows))
    return run_kernel(
        project_kernel,
        (valid, x, gain, cot, *weights),
        grid=(width // TILE,),
        in_specs=[pl.BlockSpec(memory_space=pltpu.SMEM), full, whole((1, width)), full]
        + [tile] * 3,
        out_specs=[turned, full, turned, out, out, out],
        out_shape=[
            jax.ShapeDtypeStruct((width, rows), BF16),
            jax.ShapeDtypeStruct((rows, width), BF16),
            jax.ShapeDtypeStruct((width, rows), BF16),
        ]
        + [jax.ShapeDtypeStruct((rows, width), BF16)] * 3,
        scratch_shapes=[pltpu.VMEM((rows, width), BF16)],
        name="project_tokens",
        exchange=exchange,
        busy=14.0,
        polls=3,
    )


def attend(query, pieces):
    scores = []
    for keys, _, mask in pieces:
        score = matmul_nt(keys, query) * (SCALE * LOG2E)
        scores.append(score if mask is None else jnp.where(mask, score, NEGATIVE))
    top = functools.reduce(jnp.maximum, [jnp.max(s, axis=0, keepdims=True) for s in scores])
    total, mixed = 0.0, 0.0
    for score, (_, values, _) in zip(scores, pieces):
        weights = jnp.exp2(score - top)
        total = total + jnp.sum(weights, axis=0, keepdims=True)
        mixed = mixed + matmul(values.T, weights.astype(BF16))
    return (mixed / total).T.astype(BF16), top + jnp.log2(total)


def attend_backward(query, log_total, grad, centre, pieces):
    grad_query = 0.0
    for keys, values, mask, add_keys, add_values in pieces:
        score = matmul_nt(keys, query) * (SCALE * LOG2E)
        if mask is not None:
            score = jnp.where(mask, score, NEGATIVE)
        probs = jnp.exp2(score - log_total)
        add_values(matmul(probs.astype(BF16), grad))
        grad_probs = matmul_nt(values, grad)
        grad_scores = (probs * (grad_probs - centre)).astype(BF16)
        add_keys(matmul(grad_scores, query) * SCALE)
        grad_query = grad_query + matmul(keys.T, grad_scores)
    return (grad_query * SCALE).T


def centre_of(grad, mixed):
    return jnp.sum((grad.astype(F32) * mixed.astype(F32)).T, axis=0, keepdims=True)


def position(shape, axis):
    return lax.broadcasted_iota(jnp.int32, shape, axis)


def token_pieces(block, half, valid):
    key = position((TILE, TILE), 0)
    query = position((TILE, TILE), 1)
    causal, recent = key <= query, key > query
    pieces = []
    if block:
        start = (block - 1) * BLOCK
        pieces.append(("near", start + half * TILE, TILE, recent))
        if half == 0:
            pieces.append(("near", start + TILE, TILE, None))
    start = block * BLOCK
    for piece in range(half + 1):
        first = start + piece * TILE
        seen = first + key < valid
        mask = causal if piece == half else None
        if block:
            mask = seen if mask is None else mask & seen
        pieces.append(("near", first, TILE, mask))
    pieces.append(("state", block * BLOCK, BLOCK, None))
    return pieces


def state_forward_kernel(
    poll, valid, s0, gain, gate_bias, wq, wk, wv, wu, k, v,
    normed_t, sq, sk, sv, read, log_out, update_out, states, last,
    state, normed, total,
):
    block, pair = pl.program_id(0), pl.program_id(1)

    @pl.when((block == 0) & (pair == 0))
    def _():
        state[...] = s0[...].astype(F32)

    @pl.when(pair == 0)
    def _():
        now = state[...]
        rows = (now * inverse_rms(now) * gain[...]).astype(BF16)
        normed[...] = rows
        normed_t[...] = rows.T
        states[...] = now
        total[...] = jnp.zeros_like(total)

    poll()
    rows = normed[...]
    for weight, out in ((wq, sq), (wk, sk), (wv, sv)):
        out[...] = matmul(rows, weight[...]).astype(BF16)
    poll()
    seen = block * BLOCK + position((BLOCK, BLOCK), 0) < valid[0]
    for head in range(2):
        lanes = pl.ds(head * HEAD, HEAD)
        read[:, lanes], log_out[0, 0, pl.ds(head, 1), :] = attend(
            sq[:, lanes], [(k[:, lanes], v[:, lanes], seen)]
        )
    total[...] += matmul(read[...], wu[...])

    @pl.when(pair == pl.num_programs(1) - 1)
    def _():
        update = total[...]
        gate = 1.0 / (1.0 + jnp.exp(-gate_bias[...]))
        later = gate * state[...] + (1.0 - gate) * update
        update_out[...] = update
        state[...] = later
        last[...] = later.astype(BF16)


def state_forward(valid, s0, gain, gate_bias, weights, update_weight, k, v, exchange):
    rows, width = s0.shape
    blocks, pairs = k.shape[0] // BLOCK, width // PAIR
    columns = pl.BlockSpec((width, PAIR), lambda b, p: (0, p))
    tile = pl.BlockSpec((rows, PAIR), lambda b, p: (b, p))
    band = pl.BlockSpec((rows, width), lambda b, p: (b, 0))
    small = whole((1, width))

    def stack(kind):
        return jax.ShapeDtypeStruct((blocks * rows, width), kind)

    return run_kernel(
        state_forward_kernel,
        (valid, s0, gain, gate_bias, *weights, update_weight, k, v),
        grid=(blocks, pairs),
        in_specs=[
            pl.BlockSpec(memory_space=pltpu.SMEM), whole((rows, width)), small, small,
            columns, columns, columns, pl.BlockSpec((PAIR, width), lambda b, p: (p, 0)),
            pl.BlockSpec((BLOCK, PAIR), lambda b, p: (b, p)),
            pl.BlockSpec((BLOCK, PAIR), lambda b, p: (b, p)),
        ],
        out_specs=[
            pl.BlockSpec((width, rows), lambda b, p: (0, b)), tile, tile, tile, tile,
            pl.BlockSpec((1, 1, 2, rows), lambda b, p: (b, p, 0, 0)),
            band, band, whole((rows, width)),
        ],
        out_shape=[
            jax.ShapeDtypeStruct((width, blocks * rows), BF16),
            stack(BF16), stack(BF16), stack(BF16), stack(BF16),
            jax.ShapeDtypeStruct((blocks, pairs, 2, rows), F32),
            stack(F32), stack(F32), jax.ShapeDtypeStruct((rows, width), BF16),
        ],
        scratch_shapes=[
            pltpu.VMEM((rows, width), F32), pltpu.VMEM((rows, width), BF16),
            pltpu.VMEM((rows, width), F32),
        ],
        name="state_forward",
        exchange=exchange,
        busy=27.7,
        polls=2,
    )


def token_forward_kernel(
    poll, valid, x, gain, q, k, v, sk, sv, wo, mixed, log_out, resid, ynorm, ynorm_t
):
    pair = pl.program_id(0)

    @pl.when(pair == 0)
    def _():
        resid[...] = x[...].astype(F32)

    count = valid[0]
    for head in range(2):
        lanes = pl.ds(head * HEAD, HEAD)
        for block in range(q.shape[0] // BLOCK):
            poll()
            for half in range(BLOCK // TILE):
                rows = pl.ds(block * BLOCK + half * TILE, TILE)
                pieces = []
                for kind, first, size, mask in token_pieces(block, half, count):
                    keys, values = (k, v) if kind == "near" else (sk, sv)
                    there = pl.ds(first, size)
                    pieces.append((keys[there, lanes], values[there, lanes], mask))
                mixed[rows, lanes], log_out[0, pl.ds(head, 1), rows] = attend(
                    q[rows, lanes], pieces
                )
    resid[...] += matmul(mixed[...], wo[...])

    @pl.when(pair == pl.num_programs(0) - 1)
    def _():
        rows = resid[...]
        rounded = (rows * inverse_rms(rows) * gain[...]).astype(BF16)
        ynorm[...] = rounded
        ynorm_t[...] = rounded.T


def token_forward(valid, x, gain, q, k, v, sk, sv, wo, exchange):
    rows, width = x.shape
    pairs = width // PAIR
    tile = pl.BlockSpec((rows, PAIR), lambda p: (0, p))
    states = pl.BlockSpec((sk.shape[0], PAIR), lambda p: (0, p))
    return run_kernel(
        token_forward_kernel,
        (valid, x, gain, q, k, v, sk, sv, wo),
        grid=(pairs,),
        in_specs=[
            pl.BlockSpec(memory_space=pltpu.SMEM), whole((rows, width)), whole((1, width)),
            tile, tile, tile, states, states, pl.BlockSpec((PAIR, width), lambda p: (p, 0)),
        ],
        out_specs=[
            tile, pl.BlockSpec((1, 2, rows), lambda p: (p, 0, 0)),
            whole((rows, width)), whole((rows, width)), whole((width, rows)),
        ],
        out_shape=[
            jax.ShapeDtypeStruct((rows, width), BF16),
            jax.ShapeDtypeStruct((pairs, 2, rows), F32),
            jax.ShapeDtypeStruct((rows, width), F32),
            jax.ShapeDtypeStruct((rows, width), BF16),
            jax.ShapeDtypeStruct((width, rows), BF16),
        ],
        name="token_forward",
        exchange=exchange,
        busy=28.4,
        polls=2 * rows // BLOCK,
    )


def feed_forward_kernel(
    first, final, poll, ynorm, ynorm_t, masked, masked_t, total_in, grad_in, up_w, down_w,
    out, grad_out, up_grad, down_grad,
    total, grad_total, sems,
):
    step, last = pl.program_id(0), pl.num_programs(0) - 1
    loads = [pltpu.make_async_copy(total_in, total, sems.at[0])]
    stores = [pltpu.make_async_copy(grad_total, grad_out, sems.at[1])]
    if not first:
        loads.append(pltpu.make_async_copy(grad_in, grad_total, sems.at[1]))
    if not final:
        stores.append(pltpu.make_async_copy(total, out, sems.at[0]))

    poll()

    @pl.when(step == 0)
    def _():
        for copy in loads:
            copy.start()
        if first:
            grad_total[...] = jnp.zeros_like(grad_total)

    up_part, down_part = up_w[0], down_w[0]
    up = matmul(ynorm[...], up_part)
    grad_hidden = matmul(masked[...], down_part)
    square = up * up
    bent = jnp.tanh(GELU_C * (up + GELU_K * square * up))
    hidden = (0.5 * up * (1.0 + bent)).astype(BF16)
    slope = 0.5 * (1.0 + bent) + 0.5 * up * (1.0 - bent * bent) * (
        GELU_C * (1.0 + 3.0 * GELU_K * square)
    )
    grad_up = (grad_hidden * slope).astype(BF16)
    poll()
    down_grad[0] = matmul(masked_t[...], hidden).astype(BF16)
    poll()
    up_grad[0] = matmul(ynorm_t[...], grad_up).astype(BF16)

    @pl.when(step == 0)
    def _():
        for copy in loads:
            copy.wait()

    poll()
    total[...] += matmul_nt(hidden, down_part)
    grad_total[...] += matmul_nt(grad_up, up_part)

    @pl.when(step == last)
    def _():
        for copy in stores:
            copy.start()
        if final:
            out[...] = total[...].astype(BF16)
        for copy in stores:
            copy.wait()


def feed_forward(first, final, rows_in, total, grad, up_w, down_w, exchange, chunk=512):
    rows, width = total.shape
    parts, _, part = up_w.shape
    chunk = min(chunk, part)
    each = part // chunk
    weight = pl.BlockSpec((1, width, chunk), lambda j: (j // each, 0, j % each))
    once = pl.BlockSpec((rows, width), lambda j: (0, 0), pipeline_mode=pl.Buffered(1))
    turned = pl.BlockSpec((width, rows), lambda j: (0, 0), pipeline_mode=pl.Buffered(1))
    anywhere = pl.BlockSpec(memory_space=pl.ANY)
    return run_kernel(
        functools.partial(feed_forward_kernel, first, final),
        (*rows_in, total, grad, up_w, down_w),
        grid=(parts * each,),
        in_specs=[once, turned, once, turned, anywhere, anywhere, weight, weight],
        out_specs=[once if final else anywhere, anywhere, weight, weight],
        out_shape=[
            jax.ShapeDtypeStruct((rows, width), BF16 if final else F32),
            jax.ShapeDtypeStruct((rows, width), F32),
            jax.ShapeDtypeStruct(up_w.shape, BF16),
            jax.ShapeDtypeStruct(down_w.shape, BF16),
        ],
        scratch_shapes=[
            pltpu.VMEM((rows, width), F32), pltpu.VMEM((rows, width), F32),
            pltpu.SemaphoreType.DMA((2,)),
        ],
        name="feed_forward_final" if final else "feed_forward_first",
        exchange=exchange,
        busy=38.0,
        polls=4,
    )


def token_backward_kernel(
    poll, valid, resid, gain, masked, grad_ynorm, normed_t, snormed_t,
    q, k, v, sk, sv, wo, mixed, log_total,
    grad_resid, gain_grad, dq, dk, dv, dsk, dsv, wo_grad, wq_grad, skw_grad, svw_grad,
    rounded, work, other, sems, grad_mixed, near_k, near_v, state_k, state_v,
):
    loads = [
        pltpu.make_async_copy(source, target, sems.at[i])
        for i, (source, target) in enumerate(((resid, work), (grad_ynorm, other), (masked, rounded)))
    ]
    store = pltpu.make_async_copy(work, grad_resid, sems.at[3])

    @pl.when(pl.program_id(0) == 0)
    def _():
        for copy in loads:
            copy.start()

    poll()

    @pl.when(pl.program_id(0) == 0)
    def _():
        for copy in loads:
            copy.wait()
        grad, gain_rows = rms_backward(work[...], gain[...], other[...])
        grad = rounded[...].astype(F32) + grad
        work[...] = grad
        rounded[...] = grad.astype(BF16)
        gain_grad[...] = jnp.sum(gain_rows, axis=0, keepdims=True)
        store.start()

    @pl.when(pl.program_id(0) == pl.num_programs(0) - 1)
    def _():
        store.wait()

    grad_rows = rounded[...]
    grad_mixed[...] = matmul_nt(grad_rows, wo[...]).astype(BF16)
    wo_grad[...] = matmul(mixed[...].T, grad_rows).astype(BF16)
    for ref in (near_k, near_v, state_k, state_v):
        ref[...] = jnp.zeros_like(ref)
    count = valid[0]
    for head in range(2):
        lanes = pl.ds(head * HEAD, HEAD)

        def adder(ref, there):
            def add(term):
                ref[there, lanes] += term

            return add

        for block in range(q.shape[0] // BLOCK):
            poll()
            for half in range(BLOCK // TILE):
                rows = pl.ds(block * BLOCK + half * TILE, TILE)
                pieces = []
                for kind, first, size, mask in token_pieces(block, half, count):
                    keys, values = (k, v) if kind == "near" else (sk, sv)
                    sums = (near_k, near_v) if kind == "near" else (state_k, state_v)
                    there = pl.ds(first, size)
                    pieces.append(
                        (keys[there, lanes], values[there, lanes], mask)
                        + tuple(adder(ref, there) for ref in sums)
                    )
                out_grad = grad_mixed[rows, lanes]
                dq[rows, lanes] = attend_backward(
                    q[rows, lanes],
                    log_total[0, pl.ds(head, 1), rows],
                    out_grad,
                    centre_of(out_grad, mixed[rows, lanes]),
                    pieces,
                ).astype(BF16)
    dk[...] = near_k[...]
    dv[...] = near_v[...]
    dsk[...] = state_k[...].astype(BF16)
    dsv[...] = state_v[...].astype(BF16)
    wq_grad[...] = matmul(normed_t[...], dq[...]).astype(BF16)
    skw_grad[...] = matmul(snormed_t[...], dsk[...]).astype(BF16)
    svw_grad[...] = matmul(snormed_t[...], dsv[...]).astype(BF16)


def token_backward(
    valid, resid, gain, masked, grad_ynorm, normed_t, snormed_t,
    q, k, v, sk, sv, wo, mixed, log_total, exchange,
):
    rows, width = resid.shape
    anywhere = pl.BlockSpec(memory_space=pl.ANY)
    turned = pl.BlockSpec((width, rows), lambda p: (0, 0), pipeline_mode=pl.Buffered(1))
    turned_state = pl.BlockSpec(snormed_t.shape, lambda p: (0, 0), pipeline_mode=pl.Buffered(1))
    columns = pl.BlockSpec((width, PAIR), lambda p: (0, p))
    once = pl.BlockSpec((rows, width), lambda p: (0, 0), pipeline_mode=pl.Buffered(1))
    pairs = width // PAIR
    tile = pl.BlockSpec((rows, PAIR), lambda p: (0, p))
    states = pl.BlockSpec((sk.shape[0], PAIR), lambda p: (0, p))
    band = pl.BlockSpec((PAIR, width), lambda p: (p, 0))
    return run_kernel(
        token_backward_kernel,
        (
            valid, resid, gain, masked, grad_ynorm, normed_t, snormed_t,
            q, k, v, sk, sv, wo, mixed, log_total,
        ),
        grid=(pairs,),
        in_specs=[
            pl.BlockSpec(memory_space=pltpu.SMEM), anywhere, whole((1, width)), anywhere, anywhere,
            turned, turned_state, tile, tile, tile, states, states, band, tile,
            pl.BlockSpec((1, 2, rows), lambda p: (p, 0, 0)),
        ],
        out_specs=[anywhere, whole((1, width)), tile, tile, tile, states, states, band]
        + [columns] * 3,
        out_shape=[
            jax.ShapeDtypeStruct((rows, width), F32),
            jax.ShapeDtypeStruct((1, width), F32),
            jax.ShapeDtypeStruct((rows, width), BF16),
            jax.ShapeDtypeStruct((rows, width), F32),
            jax.ShapeDtypeStruct((rows, width), F32),
            jax.ShapeDtypeStruct(sk.shape, BF16),
            jax.ShapeDtypeStruct(sk.shape, BF16),
        ]
        + [jax.ShapeDtypeStruct((width, width), BF16)] * 4,
        scratch_shapes=[
            pltpu.VMEM((rows, width), BF16), pltpu.VMEM((rows, width), F32),
            pltpu.VMEM((rows, width), F32), pltpu.SemaphoreType.DMA((4,)),
            pltpu.VMEM((rows, PAIR), BF16), pltpu.VMEM((rows, PAIR), F32),
            pltpu.VMEM((rows, PAIR), F32), pltpu.VMEM((sk.shape[0], PAIR), F32),
            pltpu.VMEM((sk.shape[0], PAIR), F32),
        ],
        name="token_backward",
        exchange=exchange,
        busy=55.0,
        polls=1 + 2 * rows // BLOCK,
    )


def state_backward_kernel(
    poll, valid, cot, gain, gate_bias, wq, wk, wv, wu, states, updates,
    sq, k, v, read, log_total, near_k, near_v, dsk, dsv, read_last, normed_t, snormed_t,
    dk, dv, grad_state, gain_grad, bias_grad, wk_grad, wv_grad, sqw_grad, wu_grad,
    later, dz, total, grad_read, sum_k, sum_v, dsq, kept_dz, kept,
):
    step, pair = pl.program_id(0), pl.program_id(1)
    block = pl.num_programs(0) - 1 - step
    gate = 1.0 / (1.0 + jnp.exp(-gate_bias[...]))

    @pl.when((step == 0) & (pair == 0))
    def _():
        later[...] = cot[...].astype(F32)
        gain_grad[...] = jnp.zeros_like(gain_grad)
        bias_grad[...] = jnp.zeros_like(bias_grad)

    @pl.when(pair == 0)
    def _():
        grad = later[...]
        rounded = (grad * (1.0 - gate)).astype(BF16)
        dz[...] = rounded

        @pl.when(step == 0)
        def _():
            kept_dz[...] = rounded

        bias_grad[...] += (
            jnp.sum(grad * (states[...] - updates[...]), axis=0, keepdims=True) * gate * (1.0 - gate)
        )
        total[...] = jnp.zeros_like(total)

    poll()
    grad_read[...] = matmul_nt(dz[...], wu[...]).astype(BF16)
    seen = block * BLOCK + position((BLOCK, BLOCK), 0) < valid[0]
    sum_k[...] = near_k[...]
    sum_v[...] = near_v[...]
    for head in range(2):
        lanes = pl.ds(head * HEAD, HEAD)

        def adder(ref):
            def add(term):
                ref[:, lanes] += term

            return add

        out_grad = grad_read[:, lanes]
        dsq[:, lanes] = attend_backward(
            sq[:, lanes],
            log_total[0, 0, pl.ds(head, 1), :],
            out_grad,
            centre_of(out_grad, read[:, lanes]),
            [(k[:, lanes], v[:, lanes], seen, adder(sum_k), adder(sum_v))],
        ).astype(BF16)
    poll()
    dk[...] = sum_k[...].astype(BF16)
    dv[...] = sum_v[...].astype(BF16)
    total[...] += (
        matmul_nt(dsq[...], wq[...]) + matmul_nt(dsk[...], wk[...]) + matmul_nt(dsv[...], wv[...])
    )

    @pl.when(step == 0)
    def _():
        for i, ref in enumerate((dk, dv, dsq)):
            kept[i, pair] = ref[...]

    @pl.when(step == 1)
    def _():
        for i, (left, ref, out) in enumerate(
            ((normed_t, dk, wk_grad), (normed_t, dv, wv_grad), (snormed_t, dsq, sqw_grad))
        ):
            half = left.shape[1] // 2
            out[...] = (
                matmul(left[:, :half], ref[...]) + matmul(left[:, half:], kept[i, pair])
            ).astype(BF16)
        wu_grad[...] = (
            matmul(read[...].T, dz[...]) + matmul(read_last[...].T, kept_dz[...])
        ).astype(BF16)

    @pl.when(pair == pl.num_programs(1) - 1)
    def _():
        grad, gain_rows = rms_backward(states[...], gain[...], total[...])
        grad = later[...] * gate + grad
        later[...] = grad
        grad_state[...] = grad
        gain_grad[...] += jnp.sum(gain_rows, axis=0, keepdims=True)


def state_backward(
    valid, cot, gain, gate_bias, weights, update_weight, states, updates,
    sq, k, v, read, log_total, near_k, near_v, dsk, dsv, normed_t, snormed_t, exchange,
):
    rows, width = cot.shape
    blocks, pairs = k.shape[0] // BLOCK, width // PAIR
    columns = pl.BlockSpec((width, PAIR), lambda s, p: (0, p))
    tile = pl.BlockSpec((rows, PAIR), lambda s, p: (blocks - 1 - s, p))
    token = pl.BlockSpec((BLOCK, PAIR), lambda s, p: (blocks - 1 - s, p))
    band = pl.BlockSpec((rows, width), lambda s, p: (blocks - 1 - s, 0))
    small = whole((1, width))
    return run_kernel(
        state_backward_kernel,
        (
            valid, cot, gain, gate_bias, *weights, update_weight, states, updates,
            sq, k, v, read, log_total, near_k, near_v, dsk, dsv, read, normed_t, snormed_t,
        ),
        grid=(blocks, pairs),
        in_specs=[
            pl.BlockSpec(memory_space=pltpu.SMEM), whole((rows, width)), small, small,
            columns, columns, columns, pl.BlockSpec((PAIR, width), lambda s, p: (p, 0)),
            band, band, tile, token, token, tile,
            pl.BlockSpec((1, 1, 2, rows), lambda s, p: (blocks - 1 - s, p, 0, 0)),
            token, token, tile, tile,
            pl.BlockSpec((rows, PAIR), lambda s, p: (blocks - 1, p)),
            pl.BlockSpec(normed_t.shape, lambda s, p: (0, 0), pipeline_mode=pl.Buffered(1)),
            pl.BlockSpec(snormed_t.shape, lambda s, p: (0, 0), pipeline_mode=pl.Buffered(1)),
        ],
        out_specs=[token, token, whole((rows, width)), small, small]
        + [pl.BlockSpec((width, PAIR), lambda s, p: (0, p * s))] * 3
        + [pl.BlockSpec((PAIR, width), lambda s, p: (p * s, 0))],
        out_shape=[
            jax.ShapeDtypeStruct(k.shape, BF16),
            jax.ShapeDtypeStruct(k.shape, BF16),
            jax.ShapeDtypeStruct((rows, width), F32),
            jax.ShapeDtypeStruct((1, width), F32),
            jax.ShapeDtypeStruct((1, width), F32),
        ]
        + [jax.ShapeDtypeStruct((width, width), BF16)] * 4,
        scratch_shapes=[
            pltpu.VMEM((rows, width), F32), pltpu.VMEM((rows, width), BF16),
            pltpu.VMEM((rows, width), F32), pltpu.VMEM((rows, PAIR), BF16),
            pltpu.VMEM((BLOCK, PAIR), F32), pltpu.VMEM((BLOCK, PAIR), F32),
            pltpu.VMEM((rows, PAIR), BF16), pltpu.VMEM((rows, width), BF16),
            pltpu.VMEM((3, pairs, BLOCK, PAIR), BF16),
        ],
        name="state_backward",
        exchange=exchange,
        busy=51.0,
        polls=2,
    )


def token_grad_kernel(
    plan, poll, x, gain, grad_resid, dq, dk, dv, wq, wk, wv, grad_x, gain_grad
):
    plan.first_row = gain_grad
    poll()

    @pl.when(pl.program_id(0) == 0)
    def _():
        gain_grad[...] = jnp.zeros_like(gain_grad)

    grad_normed = matmul_nt(dq[...], wq[...]) + matmul_nt(dk[...], wk[...])
    poll()
    grad_normed = grad_normed + matmul_nt(dv[...], wv[...])
    grad, gain_rows = rms_backward(x[...].astype(F32), gain[...], grad_normed)
    grad_x[...] = grad_resid[...] + grad
    gain_grad[...] += jnp.sum(gain_rows, axis=0, keepdims=True)


def token_grad(x, gain, grad_resid, grads, weights, plan, exchange):
    rows, width = x.shape
    band = pl.BlockSpec((TILE, width), lambda i: (i, 0))
    weight = pl.BlockSpec((width, width), lambda i: (0, 0), pipeline_mode=pl.Buffered(1))
    return run_kernel(
        functools.partial(token_grad_kernel, plan),
        (x, gain, grad_resid, *grads, *weights),
        grid=(rows // TILE,),
        in_specs=[band, whole((1, width)), band, band, band, band, weight, weight, weight],
        out_specs=[band, whole((1, width))],
        out_shape=[
            jax.ShapeDtypeStruct((rows, width), F32), jax.ShapeDtypeStruct((1, width), F32)
        ],
        name="token_grad",
        exchange=exchange,
        busy=13.8,
        polls=2,
    )


def cut(width, pieces):
    return [(i * width // pieces, width // pieces) for i in range(pieces)]


def plan_gather(sizes, small, square, forward):
    width, half = square[0].shape[1], forward[0].shape[1]
    pieces = cut(width, SQUARE_PIECES)
    can_share = pieces[0][1] // sizes["m"] % 128 == 0
    units = [(0, "zx", False, (0, small.shape[1]), 0)]
    for group, start in zip(((0, 1, 2), (3, 4, 5), (6,), (7,)), GATHER_SQUARE):
        if len(group) == 1:
            spans = [pieces]
        else:
            spans = [[columns] for columns in pieces]
        for n, span in enumerate(spans):
            for j, (i, columns) in enumerate((i, columns) for columns in span for i in group):
                shared = can_share and j > 0
                units.append((1 + i, "zxm" if shared else "zx", shared, columns, start + n))
    for i, start in enumerate(GATHER_FORWARD):
        for n, columns in enumerate(cut(half, FORWARD_PIECES)):
            units.append((9 + i, ("zxm", "zmx")[n % 2], False, columns, start + n // 2))
    return Gather(sizes, [small] + square + forward, units)


def forward_units(arrays, start):
    units = []
    for i, array in enumerate(arrays):
        for n, columns in enumerate(cut(array.shape[-1], FORWARD_PIECES)):
            units.append((i, ("mxz", "xmz")[n % 2], False, columns))
    return [unit + (start + n // 2,) for n, unit in enumerate(units)]


def square_units(sizes, arrays, start, group, pieces):
    units = []
    for columns in cut(arrays[0].shape[-1], pieces):
        for i in range(len(arrays)):
            shared = len(units) % 3 > 0 and columns[1] // sizes["m"] % 128 == 0
            units.append((i, "mxz" if shared else "xz", shared, columns))
    return [unit + (start + n // group,) for n, unit in enumerate(units)]


def finish_kernel(counts, *refs):
    refs = list(refs)
    parts = [[refs.pop(0) for _ in range(n)] for n in counts]
    for group, out in zip(parts, refs):
        first = 0
        for part in group:
            out[:, pl.ds(first, part.shape[1])] = part[...]
            first += part.shape[1]


def finish(groups):
    shapes = [
        jax.ShapeDtypeStruct((g[0].shape[0], sum(p.shape[1] for p in g)), F32) for g in groups
    ]
    return pl.pallas_call(
        functools.partial(finish_kernel, [len(g) for g in groups]),
        out_shape=shapes,
        compiler_params=pltpu.CompilerParams(vmem_limit_bytes=VMEM_LIMIT),
        name="finish",
    )(*[part for g in groups for part in g])


def shards(
    mlp_size,
    tokens,
    initial_state,
    valid,
    token_query_weight,
    token_key_weight,
    token_value_weight,
    token_output_weight,
    state_query_weight,
    state_key_weight,
    state_value_weight,
    state_update_weight,
    up_projection_weight,
    down_projection_weight,
    token_norm_gain,
    state_norm_gain,
    feedforward_norm_gain,
    state_gate_bias,
    output_cotangent,
    final_state_cotangent,
):
    rows = token_query_weight.shape[0]
    width = tokens.shape[2]
    seg_size = width // rows
    sizes = {"z": seg_size // 4, "x": 2, "c": 2, "m": mlp_size}
    half = up_projection_weight.shape[1] // 2
    small = jnp.concatenate(
        [token_norm_gain, state_norm_gain, feedforward_norm_gain, state_gate_bias]
    ).reshape(-1, 128)
    small = jnp.pad(small, ((0, 16 - small.shape[0]), (0, 0)))
    square = [
        token_query_weight,
        token_key_weight,
        token_value_weight,
        state_query_weight,
        state_key_weight,
        state_value_weight,
        state_update_weight,
        token_output_weight,
    ]
    forward = [
        weight[:, first : first + half]
        for first in (0, half)
        for weight in (up_projection_weight, down_projection_weight)
    ]
    plan = plan_gather(sizes, small, square, forward)
    x, s0, cot = tokens[0], initial_state[0], output_cotangent[0]

    def full(*names):
        return [plan.targets[n].reshape(width, width) for n in names]

    def forward_full(*names):
        return [plan.targets[n].reshape(mlp_size, width, half) for n in names]

    exchange_alone(plan.until(plan.ready((0, 1, 2, 3)), 1), "gather_first")
    gains = plan.targets[0].reshape(seg_size, -1)[:, : 4 * rows].reshape(seg_size, 4, rows)
    gains = gains.transpose(1, 0, 2).reshape(4, 1, width).astype(F32)
    token_gain, state_gain, mlp_gain, gate_bias = [gains[i] for i in range(4)]
    token_weights = full(1, 2, 3)
    normed_t, masked, masked_t, q, k, v = project(
        valid, x, token_gain, cot, token_weights, plan.until(plan.ready((4, 5, 6, 7)), 2)
    )
    state_weights, (wu,) = full(4, 5, 6), full(7)
    ready = plan.ready((9, 10))
    middle = max(plan.ready((8,)), GATHER_MIDDLE)
    snormed_t, sq, sk, sv, read, read_log, updates, states, last = state_forward(
        valid, s0, state_gain, gate_bias, state_weights, wu, k, v, plan.until(middle, 3)
    )
    (wo,) = full(8)
    mixed, token_log, resid, *ynorms = token_forward(
        valid, x, mlp_gain, q, k, v, sk, sv, wo, plan.until(ready, 4)
    )
    total, grad_total, *first_grads = feed_forward(
        True, False, (*ynorms, masked, masked_t), resid, resid, *forward_full(9, 10),
        plan.until(plan.ready((11, 12)), 5),
    )

    def parted(grads):
        shape = (seg_size // 4, 2, 2, rows)
        return [
            g.reshape((mlp_size,) + shape + (half,)) if g.ndim == 3 else g.reshape(shape + (width,))
            for g in grads
        ]

    sums = Scatter(sizes)
    rounds = iter(SCATTER_ROUNDS)

    def next_rounds(collective_id):
        return sums.until(sums.round + next(rounds), collective_id)

    units_first = sums.add(parted(first_grads), forward_units(first_grads, 0))
    out, grad_total, *last_grads = feed_forward(
        False, True, (*ynorms, masked, masked_t), total, grad_total, *forward_full(11, 12),
        next_rounds(6),
    )
    units_last = sums.add(parted(last_grads), forward_units(last_grads, sums.round))
    grad_resid, mlp_gain_grad, dq, near_k, near_v, dsk, dsv, *early_grads = token_backward(
        valid, resid, mlp_gain, masked, grad_total, normed_t, snormed_t,
        q, k, v, sk, sv, wo, mixed, token_log, next_rounds(7),
    )
    units_early = sums.add(
        parted(early_grads), square_units(sizes, early_grads, sums.round, 4, SCATTER_PIECES)
    )
    dk, dv, grad_state, state_gain_grad, bias_grad, *late_grads = state_backward(
        valid, final_state_cotangent[0], state_gain, gate_bias, state_weights, wu,
        states, updates, sq, k, v, read, read_log, near_k, near_v, dsk, dsv, normed_t, snormed_t,
        next_rounds(8),
    )
    units_late = sums.add(
        parted(late_grads), square_units(sizes, late_grads, sums.round, 4, SCATTER_PIECES)
    )
    small_unit = sums.add_small(
        jnp.concatenate(
            [jnp.zeros_like(mlp_gain_grad), state_gain_grad, mlp_gain_grad, bias_grad]
            + [jnp.zeros((4, width), F32)]
        )
    )
    grad_tokens, _ = token_grad(
        x, token_gain, grad_resid, [dq, dk, dv], token_weights, sums, sums.until(sums.all(), 9)
    )
    small_sum = small_unit.result[:4].reshape(4, seg_size, rows)
    small_sum = lax.dynamic_index_in_dim(small_sum, lax.axis_index("seg"), 1, keepdims=False)

    def group(units, i, count):
        return [unit.result for unit in units[i::count]]

    def forward_group(i):
        return [
            unit.result
            for units in (units_first, units_last)
            for unit in units[i * FORWARD_PIECES : (i + 1) * FORWARD_PIECES]
        ]

    weight_sums = finish(
        [
            group(units_early, 1, 4),
            group(units_late, 0, 4),
            group(units_late, 1, 4),
            group(units_early, 0, 4),
            group(units_late, 2, 4),
            group(units_early, 2, 4),
            group(units_early, 3, 4),
            group(units_late, 3, 4),
            forward_group(0),
            forward_group(1),
        ]
    )
    return (
        out[None],
        last[None],
        grad_tokens[None],
        grad_state[None],
        *weight_sums,
        *[small_sum[i] for i in range(4)],
    )


def solution(mesh):
    own = P(("seg", "mlp"), None, None)
    square, forward, small = P("seg", None), P("seg", "mlp"), P("seg")
    return jax.shard_map(
        functools.partial(shards, mesh.shape["mlp"]),
        mesh=mesh,
        in_specs=(own, own, P(("seg", "mlp")))
        + (square,) * 8
        + (forward,) * 2
        + (small,) * 4
        + (own, own),
        out_specs=(own,) * 4 + (square,) * 8 + (forward,) * 2 + (small,) * 4,
        check_vma=False,
    )
```

```python
import functools
import jax
import jax.numpy as jnp
from jax import lax
from jax.experimental import pallas as pl
from jax.experimental.pallas import tpu as pltpu
from jax.sharding import PartitionSpec as P

BF16 = jnp.bfloat16
F32 = jnp.float32
VMEM_LIMIT = 60 << 20
GATHER_SQUARE = (
    ((0, 1), ("zx", "zxm", "zxm"), 1),
    ((2, 3), ("zx", "zxm", "zxm"), 1),
    ((4, 4), ("zx", "zxm"), 1),
    ((5, 5), ("zx", "zxm"), 1),
)
GATHER_FORWARD = (((6, 6), 1), ((7, 7), 1), ((9, 9), 1), ((10, 10), 1))
GATHER_MIDDLE = 9
SCATTER_FIRST = ((("mxz", 0, 1), ("xmz", 0, 1)), (("mxz", 1, 1), ("xmz", 1, 1)))
SCATTER_LAST = SCATTER_FIRST
SCATTER_EARLY = (
    (("xz", 0, 1), ("mxz", 0, 1), ("mxz", 0, 1), ("xz", 0, 1)),
    (("mxz", 1, 1), ("mxz", 1, 1), ("xz", 1, 1), ("mxz", 1, 1)),
)
SCATTER_LATE = SCATTER_EARLY
SCATTER_ROUNDS = (3, 3, 3)
LINK_RATE = 85e3
CORE_RATE = 560e3
START_COST = 2.5
STEP_COST = 0.3
LATENCY = 2.0


class Place:
    def __init__(self, sizes):
        seg = lax.axis_index("seg")
        self.sizes = sizes
        self.at = {
            "z": lax.div(seg, 4),
            "x": lax.rem(lax.div(seg, 2), 2),
            "c": lax.rem(seg, 2),
            "m": lax.axis_index("mlp"),
        }

    def device(self, moved):
        at = {**self.at, **moved}
        return (at["z"] * 4 + at["x"] * 2 + at["c"], at["m"])

    def ahead(self, axis, step):
        return lax.rem(self.at[axis] + step, self.sizes[axis])

    def behind(self, axis, step):
        return lax.rem(self.at[axis] + self.sizes[axis] - step, self.sizes[axis])

    def greet(self):
        barrier = pltpu.get_barrier_semaphore()
        count = 0
        for axis in "zxcm":
            for step in range(1, self.sizes[axis]):
                pl.semaphore_signal(
                    barrier,
                    inc=1,
                    device_id=self.device({axis: self.ahead(axis, step)}),
                    device_id_type=pl.DeviceIdType.MESH,
                )
                count += 1
        pl.semaphore_wait(barrier, count)


class Flow:
    def __init__(self, place, send, recv, taken):
        self.place, self.send, self.recv, self.taken = place, send, recv, taken
        self.steps, self.arriving, self.sent = [], [], []

    def move(self, actions, make):
        pair = self.taken[0]
        self.taken[0] += 1

        def copy(source, target, moved):
            return pltpu.make_async_remote_copy(
                src_ref=source,
                dst_ref=target,
                send_sem=self.send.at[pair],
                recv_sem=self.recv.at[pair],
                device_id=self.place.device(moved),
                device_id_type=pl.DeviceIdType.MESH,
            )

        def outgoing():
            source, target, moved, _ = make()
            return copy(source, target, moved)

        def incoming():
            _, _, moved, landing = make()
            return copy(landing, landing, moved)

        actions.append(lambda: outgoing().start())
        self.sent.append(lambda: outgoing().wait_send())
        self.arriving.append(lambda: incoming().wait_recv())

    def arrived(self):
        waits, self.arriving = self.arriving, []
        return waits


def gather_steps(flow, source, target, order, split, columns, skipped, local_sem, begin, end):
    place = flow.place
    at, sizes = place.at, place.sizes
    lead = ("m" if len(target.shape) == 6 else "") + "zxc"
    first_column, width = columns
    share = width // sizes["m"] if split else width

    def block(done, moved, skip=0):
        first = first_column + skip
        if not split or "m" in done:
            lanes = pl.ds(first, width)
        else:
            lanes = pl.ds(pl.multiple_of(first + moved.get("m", at["m"]) * share, 128), share)
        return (pl.ds(0, source.shape[0]), lanes)

    def view(done, **moved):
        index = tuple(
            moved[a] if a in moved else pl.ds(0, sizes[a]) if a in done else at[a] for a in lead
        )
        return target.at[index + block(done, moved)]

    def own_source():
        return source.at[block("", {}, skipped)]

    def own():
        return pltpu.make_async_copy(own_source(), view(""), local_sem)

    waits = []
    for i, axis in enumerate(order + "c"):
        done = order[:i]
        if not begin <= i < end:
            continue
        actions = flow.arrived() + waits
        waits = []
        if i == 0:
            actions.append(lambda: own().start())
            waits.append(lambda: own().wait())
        for step in range(1, sizes[axis]):

            def make(axis=axis, step=step, done=done):
                return (
                    view(done) if done else own_source(),
                    view(done),
                    {axis: place.ahead(axis, step)},
                    view(done, **{axis: place.behind(axis, step)}),
                )

            flow.move(actions, make)
        flow.steps.append(actions)
    flow.last = flow.arrived() + waits + flow.sent


def add_into(total, term):
    lead = total.shape[:-2]

    def body(i, carry):
        index, rest = [], i
        for size in reversed(lead):
            index.append(lax.rem(rest, size))
            rest = lax.div(rest, size)
        there = tuple(reversed(index)) + (Ellipsis,)
        total[there] = total[there] + term[there]
        return carry

    lax.fori_loop(0, functools.reduce(lambda a, b: a * b, lead, 1), body, 0)


class ScatterUnit:
    def __init__(self, sizes, grad, order, split, columns, start, stride):
        self.sizes, self.grad, self.order, self.split = sizes, grad, order, split
        self.columns, self.start, self.stride = columns, start, stride
        self.whole_m = grad.ndim == 6
        self.lead = ("m" if self.whole_m else "") + "zx"
        self.rows, self.width = grad.shape[-2], columns[1]
        self.share = self.width // sizes["m"] if split else self.width
        self.count = 1 + len(order) + (not self.whole_m)
        self.spec = pl.BlockSpec(memory_space=pl.ANY)
        self.state = self.result = None

    def left(self, done):
        width = self.share if "m" in done else self.width
        return tuple(self.sizes[a] for a in self.lead if a not in done) + (self.rows, width)

    def shapes(self, begin, end):
        shapes = [self.left(self.order[: max(begin - 1, 0)])]
        for i in range(begin, end):
            if i == 0:
                shapes.append(self.left(""))
            elif i <= len(self.order):
                axis = self.order[i - 1]
                shapes.append((self.sizes[axis] - 1,) + self.left(self.order[:i]))
            elif self.split:
                shapes.append((self.rows, self.width))
            else:
                shapes.append((self.sizes["m"], self.rows, self.width))
        return shapes

    def steps(self, flow, grad, state, saved, result, buffers, local_sem, begin, end):
        place, at, sizes, order = flow.place, flow.place.at, self.sizes, self.order
        own, landings = buffers[0], dict(zip(range(begin, end), buffers[1:]))
        gone = order[: max(begin - 1, 0)]
        lead = [a for a in self.lead if a not in gone]
        narrow = self.split and "m" in gone

        def lanes_of(place_m):
            return pl.ds(pl.multiple_of(place_m * self.share, 128), self.share)

        def grad_half(core):
            index = tuple(pl.ds(0, sizes[a]) for a in self.lead)
            return grad.at[index + (core, pl.ds(0, self.rows), pl.ds(*self.columns))]

        def view(done, **moved):
            index = tuple(
                moved[a] if a in moved else at[a] if a in done else pl.ds(0, sizes[a]) for a in lead
            )
            lanes = pl.ds(0, self.share if narrow else self.width)
            if self.split and not narrow and ("m" in done or "m" in moved):
                lanes = lanes_of(moved.get("m", at["m"]))
            return own.at[index + (pl.ds(0, self.rows), lanes)]

        def load():
            return pltpu.make_async_copy(grad_half(at["c"]) if begin == 0 else state, own, local_sem)

        def added(axis, done, landing):
            return [
                lambda step=step: add_into(view(done), landing.at[step - 1])
                for step in range(1, sizes[axis])
            ]

        ahead = [lambda: load().start()]
        actions = []
        if begin > 0:
            actions.append(lambda: load().wait())
        for i in range(begin, end):
            landing = landings[i]
            if i == 0:
                flow.move(
                    actions,
                    lambda landing=landing: (
                        grad_half(1 - at["c"]), landing, {"c": 1 - at["c"]}, landing
                    ),
                )
                flow.steps.append(actions)
                actions = [lambda: load().wait()] + flow.arrived()
                actions.append(lambda landing=landing: add_into(own, landing))
            elif i <= len(order):
                axis, done = order[i - 1], order[: i - 1]
                for step in range(1, sizes[axis]):

                    def make(axis=axis, step=step, done=done, landing=landing):
                        there = place.ahead(axis, step)
                        slot = landing.at[step - 1]
                        return (view(done, **{axis: there}), slot, {axis: there}, slot)

                    flow.move(actions, make)
                flow.steps.append(actions)
                actions = flow.arrived() + added(axis, order[:i], landing)
            else:

                def part(place_m, landing=landing):
                    if self.split:
                        return landing.at[pl.ds(0, self.rows), lanes_of(place_m)]
                    return landing.at[place_m]

                def keep():
                    part(at["m"])[...] = view(order)[...]

                actions.append(keep)
                for step in range(1, sizes["m"]):
                    flow.move(
                        actions,
                        lambda step=step: (
                            part(at["m"]),
                            part(at["m"]),
                            {"m": place.ahead("m", step)},
                            part(place.behind("m", step)),
                        ),
                    )
                flow.steps.append(actions)
                actions = flow.arrived()
        if end == self.count:

            def store():
                if self.whole_m:
                    total = view(order)[...].astype(F32)
                elif self.split:
                    total = landing[...].astype(F32)
                else:
                    total = landing[0].astype(F32)
                    for i in range(1, sizes["m"]):
                        total = total + landing[i].astype(F32)
                result[...] = total

            return ahead, actions + [store], flow.sent

        def save():
            return pltpu.make_async_copy(view(order[: end - 1]), saved, local_sem)

        return ahead, actions + [lambda: save().start()], flow.sent + [lambda: save().wait()]


def step_time(sizes, axis, size):
    if axis == "c":
        return size / CORE_RATE
    return 2 * size * ((sizes["z"] // 2) ** 2 if axis == "z" else sizes[axis] - 1) / LINK_RATE


def round_times(sizes, rounds):
    now, free, ended, times = START_COST, {axis: 0.0 for axis in "zxcm"}, {}, []
    for there in rounds:
        for unit, step, axis, size in there:
            now = max(now, ended.get((unit, step - 1), 0.0)) + STEP_COST
            free[axis] = max(free[axis], now) + step_time(sizes, axis, size)
            ended[unit, step] = free[axis] + LATENCY
        times.append(now)
    return times, max(ended.values())


class Gather:
    def __init__(self, sizes, arrays, spans, units):
        self.sizes, self.arrays, self.spans, self.round = sizes, arrays, spans, 0
        self.units = [unit[:-2] for unit in units]
        self.starts = [unit[-2:] for unit in units]
        self.targets = [None] * len(arrays)

    def ready(self, names):
        return max(
            self.stop(start, unit) for start, unit in zip(self.starts, self.units) if unit[0] in names
        )

    def stop(self, start, unit):
        return start[0] + len(unit[1]) * start[1] + 1

    def until(self, end, collective_id):
        begin, self.round = self.round, max(end, self.round)
        return GatherPart(self, begin, end, collective_id) if begin < end else None


class GatherPart:
    def __init__(self, plan, begin, end, collective_id):
        self.plan, self.begin, self.end, self.collective_id = plan, begin, end, collective_id
        self.units = [
            (start, unit)
            for start, unit in zip(plan.starts, plan.units)
            if start[0] < end and plan.stop(start, unit) > begin
        ]
        self.names = sorted({unit[0] for _, unit in self.units})
        split = {unit[0]: unit[2] for _, unit in self.units}
        order = {unit[0]: unit[1] for _, unit in self.units}
        sizes = plan.sizes
        anywhere = pl.BlockSpec(memory_space=pl.ANY)
        old = [n for n in self.names if plan.targets[n] is not None]
        self.arrays = [plan.arrays[n] for n in self.names] + [plan.targets[n] for n in old]
        self.specs = [anywhere] * len(self.arrays)
        self.out_shape = [
            jax.ShapeDtypeStruct(
                ((sizes["m"],) if "m" in order[n] and not split[n] else ())
                + (sizes["z"], 2, 2)
                + (plan.arrays[n].shape[0], plan.spans[n][1]),
                plan.arrays[n].dtype,
            )
            for n in self.names
        ]
        self.out_specs = [anywhere] * len(self.names)
        self.aliases = {len(self.names) + i: self.names.index(n) for i, n in enumerate(old)}
        pairs = len(self.units) * (sum(sizes.values()) - 4)
        self.scratch = [
            pltpu.SemaphoreType.DMA((pairs,)),
            pltpu.SemaphoreType.DMA((pairs,)),
            pltpu.SemaphoreType.DMA((len(self.units),)),
        ]

    def times(self, busy):
        sizes = self.plan.sizes
        loads = [{axis: 0.0 for axis in "zxcm"} for _ in range(self.end - self.begin)]
        for (start, stride), (n, order, split, columns) in self.units:
            size = self.plan.arrays[n].shape[0] * columns[1] * self.plan.arrays[n].dtype.itemsize
            if split:
                size //= sizes["m"]
            for i, axis in enumerate(order + "c"):
                if self.begin <= start + i * stride < self.end:
                    loads[start + i * stride - self.begin][axis] += step_time(sizes, axis, size)
                size *= sizes[axis]
        times = [0.0]
        for load in loads:
            times.append(times[-1] + max(load.values()) + LATENCY)
        return times[:-1], busy

    def rounds(self, ins, outs, scratch):
        place = Place(self.plan.sizes)
        send, recv, local = scratch
        taken = [0]
        rounds = [[] for _ in range(self.end - self.begin)]
        last = []
        for i, ((start, stride), (n, order, split, columns)) in enumerate(self.units):
            flow = Flow(place, send, recv, taken)
            begin, end = [max(-((start - to) // stride), 0) for to in (self.begin, self.end)]
            slot = self.names.index(n)
            gather_steps(
                flow, ins[slot], outs[slot], order, split, columns, self.plan.spans[n][0],
                local.at[i], begin, end,
            )
            for step, actions in enumerate(flow.steps):
                there = rounds[start + (begin + step) * stride - self.begin]
                there.insert(0 if begin + step == 0 else len(there), actions)
            last += flow.last
        rounds = [[action for actions in there for action in actions] for there in rounds]
        rounds[0].insert(0, place.greet)
        return rounds, last

    def received(self, outs):
        for n, out in zip(self.names, outs):
            self.plan.targets[n] = out


class SmallUnit:
    def __init__(self, plan, row, start):
        self.plan, self.grad, self.start, self.stride = plan, row, start, 1
        self.order, self.count = "xzm", 4
        self.rows, self.width = 8, row.shape[1]
        self.share = self.width
        self.spec = pl.BlockSpec(memory_space=pl.ANY)
        self.state = self.result = None

    def left(self, done):
        return (self.rows, self.width)

    def shapes(self, begin, end):
        sizes = self.plan.sizes
        return [self.left("")] + [(sizes[axis],) + self.left("") for axis in "c" + self.order]

    def steps(self, flow, row, state, saved, result, buffers, local_sem, begin, end):
        place, at = flow.place, flow.place.at
        own, landings = buffers[0], buffers[1:]
        actions = []

        def fill():
            own[...] = jnp.zeros_like(own)
            for i, row in enumerate(self.plan.rows):
                own[pl.ds(i, 1), :] = row[...]

        actions.append(fill)
        for axis, landing in zip("c" + self.order, landings):

            def keep(axis=axis, landing=landing):
                landing[at[axis]] = own[...]

            actions.append(keep)
            for step in range(1, place.sizes[axis]):

                def make(axis=axis, landing=landing, step=step):
                    slot = landing.at[at[axis]]
                    return (slot, slot, {axis: place.ahead(axis, step)}, landing.at[place.behind(axis, step)])

                flow.move(actions, make)
            flow.steps.append(actions)

            def add(axis=axis, landing=landing):
                total = landing[0]
                for i in range(1, place.sizes[axis]):
                    total = total + landing[i]
                own[...] = total

            actions = flow.arrived() + [add]

        def store():
            result[...] = own[...]

        return [], actions + [store], flow.sent


class Scatter:
    def __init__(self, sizes):
        self.sizes, self.units, self.round = sizes, [], 0

    def add(self, arrays, units):
        for i, order, split, columns, start, stride in units:
            assert start >= self.round
            self.units.append(
                ScatterUnit(self.sizes, arrays[i], order, split, columns, start, stride)
            )
        return self.units[len(self.units) - len(units) :]

    def add_small(self, row):
        self.units.append(SmallUnit(self, row, self.all() - 4))
        return self.units[-1]

    def all(self):
        return max(unit.start + (unit.count - 1) * unit.stride + 1 for unit in self.units)

    def until(self, end, collective_id):
        begin, self.round = self.round, max(end, self.round)
        part = ScatterPart(self, begin, end, collective_id)
        return part if part.units else None


class ScatterPart:
    aliases = {}

    def __init__(self, plan, begin, end, collective_id):
        self.sizes, self.begin, self.end, self.collective_id = plan.sizes, begin, end, collective_id
        self.units = []
        buffers, pairs = [], 0
        self.arrays, self.out_shape, self.out_specs = [], [], []
        for unit in plan.units:
            first, stop = [
                min(max(-((unit.start - to) // unit.stride), 0), unit.count) for to in (begin, end)
            ]
            if first >= stop:
                continue
            self.units.append((unit, first, stop))
            self.arrays.append(unit.state if first else unit.grad)
            if stop == unit.count:
                shape = (unit.rows, unit.width)
                self.out_shape.append(jax.ShapeDtypeStruct(shape, F32))
                self.out_specs.append(
                    pl.BlockSpec(shape, lambda *_: (0, 0), pipeline_mode=pl.Buffered(1))
                )
            else:
                shape = unit.left(unit.order[: stop - 1])
                self.out_shape.append(jax.ShapeDtypeStruct(shape, unit.grad.dtype))
                self.out_specs.append(pl.BlockSpec(memory_space=pl.ANY))
            buffers += [pltpu.VMEM(shape, unit.grad.dtype) for shape in unit.shapes(first, stop)]
            pairs += sum(self.sizes.values()) - 4 + self.sizes["m"] - 1
        self.specs = [unit.spec for unit, _, _ in self.units]
        self.scratch = buffers + [
            pltpu.SemaphoreType.DMA((pairs,)),
            pltpu.SemaphoreType.DMA((pairs,)),
            pltpu.SemaphoreType.DMA((len(self.units),)),
        ]

    def times(self, busy):
        rounds = [[] for _ in range(self.end - self.begin)]
        for n, (unit, first, stop) in enumerate(self.units):
            for i in range(first, stop):
                done = unit.order[:i]
                axis = ("c" + unit.order + "m")[i]
                shape = unit.left(done) if i <= len(unit.order) else (unit.rows, unit.share)
                size = functools.reduce(lambda a, b: a * b, shape, unit.grad.dtype.itemsize)
                rounds[unit.start + i * unit.stride - self.begin].append((n, i, axis, size))
        times, length = round_times(self.sizes, rounds)
        return times, busy if length > 2.0 * busy else length

    def rounds(self, ins, outs, scratch):
        place = Place(self.sizes)
        send, recv, local = scratch[-3:]
        buffers = list(scratch[:-3])
        taken = [0]
        rounds = [[] for _ in range(self.end - self.begin)]
        start_up, ends, waits = [], [], []
        for i, (unit, first, stop) in enumerate(self.units):
            flow = Flow(place, send, recv, taken)
            count = 1 + stop - first
            mine, buffers = buffers[:count], buffers[count:]
            done = stop == unit.count
            ahead, end, wait = unit.steps(
                flow, ins[i], ins[i], None if done else outs[i], outs[i] if done else None,
                mine, local.at[i], first, stop,
            )
            if first:
                start_up += ahead
            else:
                flow.steps[0][:0] = ahead
            for step, actions in enumerate(flow.steps):
                rounds[unit.start + (first + step) * unit.stride - self.begin].append(actions)
            after = unit.start + stop * unit.stride - self.begin
            if done and after < len(rounds):
                rounds[after].append(end)
            else:
                ends += end
            waits += wait
        rounds = [[action for actions in there for action in actions] for there in rounds]
        rounds[0][:0] = start_up + [place.greet]
        return rounds, ends + waits

    def received(self, outs):
        for (unit, first, stop), out in zip(self.units, outs):
            if stop == unit.count:
                unit.result = out
            else:
                unit.state = out


def run_all(actions):
    for action in actions:
        action()


def run_kernel(
    body, args, *, grid, in_specs, out_specs, out_shape, name, scratch_shapes=(), exchange=None, polls=1,
    busy=0.0,
):
    if exchange is None:
        return pl.pallas_call(
            functools.partial(body, lambda: None),
            grid=grid,
            in_specs=in_specs,
            out_specs=out_specs,
            out_shape=out_shape,
            scratch_shapes=scratch_shapes,
            compiler_params=pltpu.CompilerParams(vmem_limit_bytes=VMEM_LIMIT),
            name=name,
        )(*args)
    counts = (len(args), len(exchange.arrays), len(out_shape), len(exchange.out_shape))
    total = functools.reduce(lambda a, b: a * b, grid, 1)
    times, pace = exchange.times(busy)

    def kernel(*refs):
        refs = list(refs)
        ins, sent, outs, received = [[refs.pop(0) for _ in range(n)] for n in counts]
        own = [refs.pop(0) for _ in range(len(scratch_shapes))]
        step = 0
        for i, size in enumerate(grid):
            step = step * size + pl.program_id(i)
        rounds, last = exchange.rounds(sent, received, refs)
        slots, after = {}, []
        for i, (actions, time) in enumerate(zip(rounds, times)):
            slot = int(total * polls * time / pace + 0.5) if busy and i else 0
            if slot >= total * polls or i and not busy:
                after += actions
            else:
                slots.setdefault((slot % polls, slot // polls), []).extend(actions)
        called = [0]

        def poll():
            for at_step in range(total):
                actions = slots.get((called[0], at_step))
                if actions:
                    pl.when(step == at_step)(functools.partial(run_all, actions))
            called[0] += 1

        body(poll, *ins, *outs, *own)
        assert called[0] == polls
        pl.when(step == total - 1)(functools.partial(run_all, after + last))

    outs = pl.pallas_call(
        kernel,
        grid=grid,
        in_specs=list(in_specs) + exchange.specs,
        out_specs=list(out_specs) + exchange.out_specs,
        out_shape=list(out_shape) + exchange.out_shape,
        scratch_shapes=list(scratch_shapes) + exchange.scratch,
        input_output_aliases={counts[0] + i: counts[2] + o for i, o in exchange.aliases.items()},
        compiler_params=pltpu.CompilerParams(
            vmem_limit_bytes=VMEM_LIMIT,
            collective_id=exchange.collective_id,
            has_side_effects=True,
        ),
        name=name,
    )(*args, *exchange.arrays)
    exchange.received(outs[counts[2] :])
    return outs[: counts[2]]


def exchange_alone(exchange, name):
    run_kernel(
        lambda poll: poll(), [], grid=(1,), in_specs=[], out_specs=[], out_shape=[], name=name,
        exchange=exchange,
    )


HEAD = 128
BLOCK = 512
EPS = 1e-06
NEGATIVE = -1e30
GELU_C = 0.7978845608
GELU_K = 0.044715
SCALE = HEAD**-0.5
LOG2E = 1.4426950408889634
PAIR = 2 * HEAD
TILE = 256


def matmul(left, right):
    return jnp.dot(left, right, preferred_element_type=F32)


def matmul_nt(left, right):
    return lax.dot_general(left, right, (((1,), (1,)), ((), ())), preferred_element_type=F32)


def inverse_rms(values):
    return lax.rsqrt(jnp.mean(values * values, axis=-1, keepdims=True) + EPS)


def rms_backward(values, gain, grad):
    inverse = inverse_rms(values)
    unit = values * inverse
    weighted = grad * gain
    inner = jnp.mean(weighted * unit, axis=-1, keepdims=True)
    return inverse * (weighted - unit * inner), grad * unit


def row_of(gains, i):
    return gains[pl.ds(i, 1), :]


def whole(shape):
    return pl.BlockSpec(shape, lambda *_: (0,) * len(shape))


def project_kernel(
    poll, valid, x_ref, gains, cot, wq, wk, wv, normed_t, masked, masked_t, q, k, v, normed
):
    @pl.when(pl.program_id(0) == 0)
    def _():
        x = x_ref[...].astype(F32)
        rows = (x * inverse_rms(x) * row_of(gains, 0)).astype(BF16)
        normed[...] = rows
        normed_t[...] = rows.T
        keep = position(cot.shape, 0) < valid[0]
        grad = jnp.where(keep, cot[...], jnp.zeros_like(cot))
        masked[...] = grad
        masked_t[...] = grad.T

    rows = normed[...]
    for weight, out in ((wq, q), (wk, k), (wv, v)):
        poll()
        out[...] = matmul(rows, weight[...]).astype(BF16)


def project(valid, x, gains, cot, weights, exchange):
    rows, width = x.shape
    tile = pl.BlockSpec((width, TILE), lambda j: (0, j))
    out = pl.BlockSpec((rows, TILE), lambda j: (0, j))
    full = whole((rows, width))
    turned = whole((width, rows))
    return run_kernel(
        project_kernel,
        (valid, x, gains, cot, *weights),
        grid=(width // TILE,),
        in_specs=[pl.BlockSpec(memory_space=pltpu.SMEM), full, whole(gains.shape), full]
        + [tile] * 3,
        out_specs=[turned, full, turned, out, out, out],
        out_shape=[
            jax.ShapeDtypeStruct((width, rows), BF16),
            jax.ShapeDtypeStruct((rows, width), BF16),
            jax.ShapeDtypeStruct((width, rows), BF16),
        ]
        + [jax.ShapeDtypeStruct((rows, width), BF16)] * 3,
        scratch_shapes=[pltpu.VMEM((rows, width), BF16)],
        name="project_tokens",
        exchange=exchange,
        busy=14.0,
        polls=3,
    )


def attend(query, pieces):
    scores = []
    for keys, _, mask in pieces:
        score = matmul_nt(keys, query) * (SCALE * LOG2E)
        scores.append(score if mask is None else jnp.where(mask, score, NEGATIVE))
    top = functools.reduce(jnp.maximum, [jnp.max(s, axis=0, keepdims=True) for s in scores])
    total, mixed = 0.0, 0.0
    for score, (_, values, _) in zip(scores, pieces):
        weights = jnp.exp2(score - top)
        total = total + jnp.sum(weights, axis=0, keepdims=True)
        mixed = mixed + matmul(values.T, weights.astype(BF16))
    return (mixed / total).T.astype(BF16), top + jnp.log2(total)


def attend_backward(query, log_total, grad, centre, pieces):
    grad_query = 0.0
    for keys, values, mask, add_keys, add_values in pieces:
        score = matmul_nt(keys, query) * (SCALE * LOG2E)
        if mask is not None:
            score = jnp.where(mask, score, NEGATIVE)
        probs = jnp.exp2(score - log_total)
        add_values(matmul(probs.astype(BF16), grad))
        grad_probs = matmul_nt(values, grad)
        grad_scores = (probs * (grad_probs - centre)).astype(BF16)
        add_keys(matmul(grad_scores, query) * SCALE)
        grad_query = grad_query + matmul(keys.T, grad_scores)
    return (grad_query * SCALE).T


def centre_of(grad, mixed):
    return jnp.sum((grad.astype(F32) * mixed.astype(F32)).T, axis=0, keepdims=True)


def position(shape, axis):
    return lax.broadcasted_iota(jnp.int32, shape, axis)


def token_pieces(block, half, valid):
    key = position((TILE, TILE), 0)
    query = position((TILE, TILE), 1)
    causal, recent = key <= query, key > query
    pieces = []
    if block:
        start = (block - 1) * BLOCK
        pieces.append(("near", start + half * TILE, TILE, recent))
        if half == 0:
            pieces.append(("near", start + TILE, TILE, None))
    start = block * BLOCK
    for piece in range(half + 1):
        first = start + piece * TILE
        seen = first + key < valid
        mask = causal if piece == half else None
        if block:
            mask = seen if mask is None else mask & seen
        pieces.append(("near", first, TILE, mask))
    pieces.append(("state", block * BLOCK, BLOCK, None))
    return pieces


def state_forward_kernel(
    poll, valid, s0, gains, wq, wk, wv, wu, k, v,
    normed_t, sq, sk, sv, read, log_out, update_out, states, last,
    state, normed, total,
):
    block, pair = pl.program_id(0), pl.program_id(1)

    @pl.when((block == 0) & (pair == 0))
    def _():
        state[...] = s0[...].astype(F32)

    @pl.when(pair == 0)
    def _():
        now = state[...]
        rows = (now * inverse_rms(now) * row_of(gains, 1)).astype(BF16)
        normed[...] = rows
        normed_t[...] = rows.T
        states[...] = now
        total[...] = jnp.zeros_like(total)

    poll()
    rows = normed[...]
    for weight, out in ((wq, sq), (wk, sk), (wv, sv)):
        out[...] = matmul(rows, weight[...]).astype(BF16)
    poll()
    seen = block * BLOCK + position((BLOCK, BLOCK), 0) < valid[0]
    for head in range(2):
        lanes = pl.ds(head * HEAD, HEAD)
        read[:, lanes], log_out[0, 0, pl.ds(head, 1), :] = attend(
            sq[:, lanes], [(k[:, lanes], v[:, lanes], seen)]
        )
    total[...] += matmul(read[...], wu[...])

    @pl.when(pair == pl.num_programs(1) - 1)
    def _():
        update = total[...]
        gate = 1.0 / (1.0 + jnp.exp(-row_of(gains, 3)))
        later = gate * state[...] + (1.0 - gate) * update
        update_out[...] = update
        state[...] = later
        last[...] = later.astype(BF16)


def state_forward(valid, s0, gains, weights, update_weight, k, v, exchange):
    rows, width = s0.shape
    blocks, pairs = k.shape[0] // BLOCK, width // PAIR
    columns = pl.BlockSpec((width, PAIR), lambda b, p: (0, p))
    tile = pl.BlockSpec((rows, PAIR), lambda b, p: (b, p))
    band = pl.BlockSpec((rows, width), lambda b, p: (b, 0))

    def stack(kind):
        return jax.ShapeDtypeStruct((blocks * rows, width), kind)

    return run_kernel(
        state_forward_kernel,
        (valid, s0, gains, *weights, update_weight, k, v),
        grid=(blocks, pairs),
        in_specs=[
            pl.BlockSpec(memory_space=pltpu.SMEM), whole((rows, width)), whole(gains.shape),
            columns, columns, columns, pl.BlockSpec((PAIR, width), lambda b, p: (p, 0)),
            pl.BlockSpec((BLOCK, PAIR), lambda b, p: (b, p)),
            pl.BlockSpec((BLOCK, PAIR), lambda b, p: (b, p)),
        ],
        out_specs=[
            pl.BlockSpec((width, rows), lambda b, p: (0, b)), tile, tile, tile, tile,
            pl.BlockSpec((1, 1, 2, rows), lambda b, p: (b, p, 0, 0)),
            band, band, whole((rows, width)),
        ],
        out_shape=[
            jax.ShapeDtypeStruct((width, blocks * rows), BF16),
            stack(BF16), stack(BF16), stack(BF16), stack(BF16),
            jax.ShapeDtypeStruct((blocks, pairs, 2, rows), F32),
            stack(F32), stack(F32), jax.ShapeDtypeStruct((rows, width), BF16),
        ],
        scratch_shapes=[
            pltpu.VMEM((rows, width), F32), pltpu.VMEM((rows, width), BF16),
            pltpu.VMEM((rows, width), F32),
        ],
        name="state_forward",
        exchange=exchange,
        busy=27.7,
        polls=2,
    )


def token_forward_kernel(
    poll, valid, x, gains, q, k, v, sk, sv, wo, mixed, log_out, resid, ynorm, ynorm_t
):
    pair = pl.program_id(0)

    @pl.when(pair == 0)
    def _():
        resid[...] = x[...].astype(F32)

    count = valid[0]
    for head in range(2):
        lanes = pl.ds(head * HEAD, HEAD)
        for block in range(q.shape[0] // BLOCK):
            poll()
            for half in range(BLOCK // TILE):
                rows = pl.ds(block * BLOCK + half * TILE, TILE)
                pieces = []
                for kind, first, size, mask in token_pieces(block, half, count):
                    keys, values = (k, v) if kind == "near" else (sk, sv)
                    there = pl.ds(first, size)
                    pieces.append((keys[there, lanes], values[there, lanes], mask))
                mixed[rows, lanes], log_out[0, pl.ds(head, 1), rows] = attend(
                    q[rows, lanes], pieces
                )
    resid[...] += matmul(mixed[...], wo[...])

    @pl.when(pair == pl.num_programs(0) - 1)
    def _():
        rows = resid[...]
        rounded = (rows * inverse_rms(rows) * row_of(gains, 2)).astype(BF16)
        ynorm[...] = rounded
        ynorm_t[...] = rounded.T


def token_forward(valid, x, gains, q, k, v, sk, sv, wo, exchange):
    rows, width = x.shape
    pairs = width // PAIR
    tile = pl.BlockSpec((rows, PAIR), lambda p: (0, p))
    states = pl.BlockSpec((sk.shape[0], PAIR), lambda p: (0, p))
    return run_kernel(
        token_forward_kernel,
        (valid, x, gains, q, k, v, sk, sv, wo),
        grid=(pairs,),
        in_specs=[
            pl.BlockSpec(memory_space=pltpu.SMEM), whole((rows, width)), whole(gains.shape),
            tile, tile, tile, states, states, pl.BlockSpec((PAIR, width), lambda p: (p, 0)),
        ],
        out_specs=[
            tile, pl.BlockSpec((1, 2, rows), lambda p: (p, 0, 0)),
            whole((rows, width)), whole((rows, width)), whole((width, rows)),
        ],
        out_shape=[
            jax.ShapeDtypeStruct((rows, width), BF16),
            jax.ShapeDtypeStruct((pairs, 2, rows), F32),
            jax.ShapeDtypeStruct((rows, width), F32),
            jax.ShapeDtypeStruct((rows, width), BF16),
            jax.ShapeDtypeStruct((width, rows), BF16),
        ],
        name="token_forward",
        exchange=exchange,
        busy=28.4,
        polls=2 * rows // BLOCK,
    )


def feed_forward_kernel(
    first, final, poll, ynorm, ynorm_t, masked, masked_t, total_in, grad_in, up_w, down_w,
    out, grad_out, up_grad, down_grad,
    total, grad_total, sems,
):
    step, last = pl.program_id(0), pl.num_programs(0) - 1
    loads = [pltpu.make_async_copy(total_in, total, sems.at[0])]
    stores = [pltpu.make_async_copy(grad_total, grad_out, sems.at[1])]
    if not first:
        loads.append(pltpu.make_async_copy(grad_in, grad_total, sems.at[1]))
    if not final:
        stores.append(pltpu.make_async_copy(total, out, sems.at[0]))

    poll()

    @pl.when(step == 0)
    def _():
        for copy in loads:
            copy.start()
        if first:
            grad_total[...] = jnp.zeros_like(grad_total)

    up_part, down_part = up_w[0], down_w[0]
    up = matmul(ynorm[...], up_part)
    grad_hidden = matmul(masked[...], down_part)
    square = up * up
    bent = jnp.tanh(GELU_C * (up + GELU_K * square * up))
    hidden = (0.5 * up * (1.0 + bent)).astype(BF16)
    slope = 0.5 * (1.0 + bent) + 0.5 * up * (1.0 - bent * bent) * (
        GELU_C * (1.0 + 3.0 * GELU_K * square)
    )
    grad_up = (grad_hidden * slope).astype(BF16)
    poll()
    down_grad[0] = matmul(masked_t[...], hidden).astype(BF16)
    poll()
    up_grad[0] = matmul(ynorm_t[...], grad_up).astype(BF16)

    @pl.when(step == 0)
    def _():
        for copy in loads:
            copy.wait()

    poll()
    total[...] += matmul_nt(hidden, down_part)
    grad_total[...] += matmul_nt(grad_up, up_part)

    @pl.when(step == last)
    def _():
        for copy in stores:
            copy.start()
        if final:
            out[...] = total[...].astype(BF16)
        for copy in stores:
            copy.wait()


def feed_forward(first, final, rows_in, total, grad, up_w, down_w, exchange, chunk=512):
    rows, width = total.shape
    parts, _, part = up_w.shape
    chunk = min(chunk, part)
    each = part // chunk
    weight = pl.BlockSpec((1, width, chunk), lambda j: (j // each, 0, j % each))
    once = pl.BlockSpec((rows, width), lambda j: (0, 0), pipeline_mode=pl.Buffered(1))
    turned = pl.BlockSpec((width, rows), lambda j: (0, 0), pipeline_mode=pl.Buffered(1))
    anywhere = pl.BlockSpec(memory_space=pl.ANY)
    return run_kernel(
        functools.partial(feed_forward_kernel, first, final),
        (*rows_in, total, grad, up_w, down_w),
        grid=(parts * each,),
        in_specs=[once, turned, once, turned, anywhere, anywhere, weight, weight],
        out_specs=[once if final else anywhere, anywhere, weight, weight],
        out_shape=[
            jax.ShapeDtypeStruct((rows, width), BF16 if final else F32),
            jax.ShapeDtypeStruct((rows, width), F32),
            jax.ShapeDtypeStruct(up_w.shape, BF16),
            jax.ShapeDtypeStruct(down_w.shape, BF16),
        ],
        scratch_shapes=[
            pltpu.VMEM((rows, width), F32), pltpu.VMEM((rows, width), F32),
            pltpu.SemaphoreType.DMA((2,)),
        ],
        name="feed_forward_final" if final else "feed_forward_first",
        exchange=exchange,
        busy=38.0,
        polls=4,
    )


def token_backward_kernel(
    poll, valid, resid, gains, masked, grad_ynorm, normed_t, snormed_t,
    q, k, v, sk, sv, wo, mixed, log_total,
    grad_resid, gain_grad, dq, dk, dv, dsk, dsv, wo_grad, wq_grad, skw_grad, svw_grad,
    rounded, work, other, sems, grad_mixed, near_k, near_v, state_k, state_v,
):
    loads = [
        pltpu.make_async_copy(source, target, sems.at[i])
        for i, (source, target) in enumerate(((resid, work), (grad_ynorm, other), (masked, rounded)))
    ]
    store = pltpu.make_async_copy(work, grad_resid, sems.at[3])

    @pl.when(pl.program_id(0) == 0)
    def _():
        for copy in loads:
            copy.start()

    poll()

    @pl.when(pl.program_id(0) == 0)
    def _():
        for copy in loads:
            copy.wait()
        grad, gain_rows = rms_backward(work[...], row_of(gains, 2), other[...])
        grad = rounded[...].astype(F32) + grad
        work[...] = grad
        rounded[...] = grad.astype(BF16)
        gain_grad[...] = jnp.sum(gain_rows, axis=0, keepdims=True)
        store.start()

    @pl.when(pl.program_id(0) == pl.num_programs(0) - 1)
    def _():
        store.wait()

    grad_rows = rounded[...]
    grad_mixed[...] = matmul_nt(grad_rows, wo[...]).astype(BF16)
    wo_grad[...] = matmul(mixed[...].T, grad_rows).astype(BF16)
    for ref in (near_k, near_v, state_k, state_v):
        ref[...] = jnp.zeros_like(ref)
    count = valid[0]
    for head in range(2):
        lanes = pl.ds(head * HEAD, HEAD)

        def adder(ref, there):
            def add(term):
                ref[there, lanes] += term

            return add

        for block in range(q.shape[0] // BLOCK):
            poll()
            for half in range(BLOCK // TILE):
                rows = pl.ds(block * BLOCK + half * TILE, TILE)
                pieces = []
                for kind, first, size, mask in token_pieces(block, half, count):
                    keys, values = (k, v) if kind == "near" else (sk, sv)
                    sums = (near_k, near_v) if kind == "near" else (state_k, state_v)
                    there = pl.ds(first, size)
                    pieces.append(
                        (keys[there, lanes], values[there, lanes], mask)
                        + tuple(adder(ref, there) for ref in sums)
                    )
                out_grad = grad_mixed[rows, lanes]
                dq[rows, lanes] = attend_backward(
                    q[rows, lanes],
                    log_total[0, pl.ds(head, 1), rows],
                    out_grad,
                    centre_of(out_grad, mixed[rows, lanes]),
                    pieces,
                ).astype(BF16)
    dk[...] = near_k[...]
    dv[...] = near_v[...]
    dsk[...] = state_k[...].astype(BF16)
    dsv[...] = state_v[...].astype(BF16)
    wq_grad[...] = matmul(normed_t[...], dq[...]).astype(BF16)
    skw_grad[...] = matmul(snormed_t[...], dsk[...]).astype(BF16)
    svw_grad[...] = matmul(snormed_t[...], dsv[...]).astype(BF16)


def token_backward(
    valid, resid, gains, masked, grad_ynorm, normed_t, snormed_t,
    q, k, v, sk, sv, wo, mixed, log_total, exchange,
):
    rows, width = resid.shape
    anywhere = pl.BlockSpec(memory_space=pl.ANY)
    turned = pl.BlockSpec((width, rows), lambda p: (0, 0), pipeline_mode=pl.Buffered(1))
    turned_state = pl.BlockSpec(snormed_t.shape, lambda p: (0, 0), pipeline_mode=pl.Buffered(1))
    columns = pl.BlockSpec((width, PAIR), lambda p: (0, p))
    once = pl.BlockSpec((rows, width), lambda p: (0, 0), pipeline_mode=pl.Buffered(1))
    pairs = width // PAIR
    tile = pl.BlockSpec((rows, PAIR), lambda p: (0, p))
    states = pl.BlockSpec((sk.shape[0], PAIR), lambda p: (0, p))
    band = pl.BlockSpec((PAIR, width), lambda p: (p, 0))
    return run_kernel(
        token_backward_kernel,
        (
            valid, resid, gains, masked, grad_ynorm, normed_t, snormed_t,
            q, k, v, sk, sv, wo, mixed, log_total,
        ),
        grid=(pairs,),
        in_specs=[
            pl.BlockSpec(memory_space=pltpu.SMEM), anywhere, whole(gains.shape), anywhere, anywhere,
            turned, turned_state, tile, tile, tile, states, states, band, tile,
            pl.BlockSpec((1, 2, rows), lambda p: (p, 0, 0)),
        ],
        out_specs=[anywhere, whole((1, width)), tile, tile, tile, states, states, band]
        + [columns] * 3,
        out_shape=[
            jax.ShapeDtypeStruct((rows, width), F32),
            jax.ShapeDtypeStruct((1, width), F32),
            jax.ShapeDtypeStruct((rows, width), BF16),
            jax.ShapeDtypeStruct((rows, width), F32),
            jax.ShapeDtypeStruct((rows, width), F32),
            jax.ShapeDtypeStruct(sk.shape, BF16),
            jax.ShapeDtypeStruct(sk.shape, BF16),
        ]
        + [jax.ShapeDtypeStruct((width, width), BF16)] * 4,
        scratch_shapes=[
            pltpu.VMEM((rows, width), BF16), pltpu.VMEM((rows, width), F32),
            pltpu.VMEM((rows, width), F32), pltpu.SemaphoreType.DMA((4,)),
            pltpu.VMEM((rows, PAIR), BF16), pltpu.VMEM((rows, PAIR), F32),
            pltpu.VMEM((rows, PAIR), F32), pltpu.VMEM((sk.shape[0], PAIR), F32),
            pltpu.VMEM((sk.shape[0], PAIR), F32),
        ],
        name="token_backward",
        exchange=exchange,
        busy=55.0,
        polls=1 + 2 * rows // BLOCK,
    )


def state_backward_kernel(
    poll, valid, cot, gains, wq, wk, wv, wu, states, updates,
    sq, k, v, read, log_total, near_k, near_v, dsk, dsv, read_last, normed_t, snormed_t,
    dk, dv, grad_state, gain_grad, bias_grad, wk_grad, wv_grad, sqw_grad, wu_grad,
    later, dz, total, grad_read, sum_k, sum_v, dsq, kept_dz, kept,
):
    step, pair = pl.program_id(0), pl.program_id(1)
    block = pl.num_programs(0) - 1 - step
    gate = 1.0 / (1.0 + jnp.exp(-row_of(gains, 3)))

    @pl.when((step == 0) & (pair == 0))
    def _():
        later[...] = cot[...].astype(F32)
        gain_grad[...] = jnp.zeros_like(gain_grad)
        bias_grad[...] = jnp.zeros_like(bias_grad)

    @pl.when(pair == 0)
    def _():
        grad = later[...]
        rounded = (grad * (1.0 - gate)).astype(BF16)
        dz[...] = rounded

        @pl.when(step == 0)
        def _():
            kept_dz[...] = rounded

        bias_grad[...] += (
            jnp.sum(grad * (states[...] - updates[...]), axis=0, keepdims=True) * gate * (1.0 - gate)
        )
        total[...] = jnp.zeros_like(total)

    poll()
    grad_read[...] = matmul_nt(dz[...], wu[...]).astype(BF16)
    seen = block * BLOCK + position((BLOCK, BLOCK), 0) < valid[0]
    sum_k[...] = near_k[...]
    sum_v[...] = near_v[...]
    for head in range(2):
        lanes = pl.ds(head * HEAD, HEAD)

        def adder(ref):
            def add(term):
                ref[:, lanes] += term

            return add

        out_grad = grad_read[:, lanes]
        dsq[:, lanes] = attend_backward(
            sq[:, lanes],
            log_total[0, 0, pl.ds(head, 1), :],
            out_grad,
            centre_of(out_grad, read[:, lanes]),
            [(k[:, lanes], v[:, lanes], seen, adder(sum_k), adder(sum_v))],
        ).astype(BF16)
    poll()
    dk[...] = sum_k[...].astype(BF16)
    dv[...] = sum_v[...].astype(BF16)
    total[...] += (
        matmul_nt(dsq[...], wq[...]) + matmul_nt(dsk[...], wk[...]) + matmul_nt(dsv[...], wv[...])
    )

    @pl.when(step == 0)
    def _():
        for i, ref in enumerate((dk, dv, dsq)):
            kept[i, pair] = ref[...]

    @pl.when(step == 1)
    def _():
        for i, (left, ref, out) in enumerate(
            ((normed_t, dk, wk_grad), (normed_t, dv, wv_grad), (snormed_t, dsq, sqw_grad))
        ):
            half = left.shape[1] // 2
            out[...] = (
                matmul(left[:, :half], ref[...]) + matmul(left[:, half:], kept[i, pair])
            ).astype(BF16)
        wu_grad[...] = (
            matmul(read[...].T, dz[...]) + matmul(read_last[...].T, kept_dz[...])
        ).astype(BF16)

    @pl.when(pair == pl.num_programs(1) - 1)
    def _():
        grad, gain_rows = rms_backward(states[...], row_of(gains, 1), total[...])
        grad = later[...] * gate + grad
        later[...] = grad
        grad_state[...] = grad
        gain_grad[...] += jnp.sum(gain_rows, axis=0, keepdims=True)


def state_backward(
    valid, cot, gains, weights, update_weight, states, updates,
    sq, k, v, read, log_total, near_k, near_v, dsk, dsv, normed_t, snormed_t, exchange,
):
    rows, width = cot.shape
    blocks, pairs = k.shape[0] // BLOCK, width // PAIR
    columns = pl.BlockSpec((width, PAIR), lambda s, p: (0, p))
    tile = pl.BlockSpec((rows, PAIR), lambda s, p: (blocks - 1 - s, p))
    token = pl.BlockSpec((BLOCK, PAIR), lambda s, p: (blocks - 1 - s, p))
    band = pl.BlockSpec((rows, width), lambda s, p: (blocks - 1 - s, 0))
    small = whole((1, width))
    return run_kernel(
        state_backward_kernel,
        (
            valid, cot, gains, *weights, update_weight, states, updates,
            sq, k, v, read, log_total, near_k, near_v, dsk, dsv, read, normed_t, snormed_t,
        ),
        grid=(blocks, pairs),
        in_specs=[
            pl.BlockSpec(memory_space=pltpu.SMEM), whole((rows, width)), whole(gains.shape),
            columns, columns, columns, pl.BlockSpec((PAIR, width), lambda s, p: (p, 0)),
            band, band, tile, token, token, tile,
            pl.BlockSpec((1, 1, 2, rows), lambda s, p: (blocks - 1 - s, p, 0, 0)),
            token, token, tile, tile,
            pl.BlockSpec((rows, PAIR), lambda s, p: (blocks - 1, p)),
            pl.BlockSpec(normed_t.shape, lambda s, p: (0, 0), pipeline_mode=pl.Buffered(1)),
            pl.BlockSpec(snormed_t.shape, lambda s, p: (0, 0), pipeline_mode=pl.Buffered(1)),
        ],
        out_specs=[token, token, whole((rows, width)), small, small]
        + [pl.BlockSpec((width, PAIR), lambda s, p: (0, p * s))] * 3
        + [pl.BlockSpec((PAIR, width), lambda s, p: (p * s, 0))],
        out_shape=[
            jax.ShapeDtypeStruct(k.shape, BF16),
            jax.ShapeDtypeStruct(k.shape, BF16),
            jax.ShapeDtypeStruct((rows, width), F32),
            jax.ShapeDtypeStruct((1, width), F32),
            jax.ShapeDtypeStruct((1, width), F32),
        ]
        + [jax.ShapeDtypeStruct((width, width), BF16)] * 4,
        scratch_shapes=[
            pltpu.VMEM((rows, width), F32), pltpu.VMEM((rows, width), BF16),
            pltpu.VMEM((rows, width), F32), pltpu.VMEM((rows, PAIR), BF16),
            pltpu.VMEM((BLOCK, PAIR), F32), pltpu.VMEM((BLOCK, PAIR), F32),
            pltpu.VMEM((rows, PAIR), BF16), pltpu.VMEM((rows, width), BF16),
            pltpu.VMEM((3, pairs, BLOCK, PAIR), BF16),
        ],
        name="state_backward",
        exchange=exchange,
        busy=51.0,
        polls=2,
    )


def token_grad_kernel(
    plan, poll, x, gains, grad_resid, dq, dk, dv, wq, wk, wv, *refs
):
    *others, grad_x, gain_grad = refs
    plan.rows = [gain_grad] + others
    poll()

    @pl.when(pl.program_id(0) == 0)
    def _():
        gain_grad[...] = jnp.zeros_like(gain_grad)

    grad_normed = matmul_nt(dq[...], wq[...]) + matmul_nt(dk[...], wk[...])
    poll()
    grad_normed = grad_normed + matmul_nt(dv[...], wv[...])
    grad, gain_rows = rms_backward(x[...].astype(F32), row_of(gains, 0), grad_normed)
    grad_x[...] = grad_resid[...] + grad
    gain_grad[...] += jnp.sum(gain_rows, axis=0, keepdims=True)


def token_grad(x, gains, grad_resid, grads, weights, other_rows, plan, exchange):
    rows, width = x.shape
    band = pl.BlockSpec((TILE, width), lambda i: (i, 0))
    weight = pl.BlockSpec((width, width), lambda i: (0, 0), pipeline_mode=pl.Buffered(1))
    return run_kernel(
        functools.partial(token_grad_kernel, plan),
        (x, gains, grad_resid, *grads, *weights, *other_rows),
        grid=(rows // TILE,),
        in_specs=[band, whole(gains.shape), band, band, band, band, weight, weight, weight]
        + [whole((1, width))] * len(other_rows),
        out_specs=[band, whole((1, width))],
        out_shape=[
            jax.ShapeDtypeStruct((rows, width), F32), jax.ShapeDtypeStruct((1, width), F32)
        ],
        name="token_grad",
        exchange=exchange,
        busy=13.8,
        polls=2,
    )


def cut(width, pieces):
    return [(i * width // pieces, width // pieces) for i in range(pieces)]


def plan_gather(sizes, small, square, forward):
    width, half = square[0].shape[1], forward[0].shape[1]
    units = [(0, "zx", False, (0, small.shape[1]), 0, 1)]
    for group, (starts, routes, stride) in zip(((1, 2, 3), (4, 5, 6), (7,), (8,)), GATHER_SQUARE):
        pieces = cut(width, len(starts))
        can_share = pieces[0][1] // sizes["m"] % 128 == 0
        for n, (columns, start) in enumerate(zip(pieces, starts)):
            for j, i in enumerate(group):
                order = routes[(n * len(group) + j) % len(routes)]
                shared = can_share and "m" in order
                units.append((i, order if shared else "zx", shared, columns, start, stride))
    for i, (starts, stride) in enumerate(GATHER_FORWARD):
        for n, columns in enumerate(cut(half, min(len(starts), half // 128))):
            order = ("zxm", "zmx")[n % 2]
            units.append((9 + i, order, False, columns, starts[n], stride))
    arrays = [small] + square + forward
    return Gather(sizes, arrays, [(0, array.shape[1]) for array in arrays], units)


def forward_units(arrays, start, table):
    units = []
    for i, (array, pieces) in enumerate(zip(arrays, table)):
        columns = cut(array.shape[-1], min(len(pieces), array.shape[-1] // 128))
        units += [
            (i, order, False, there, start + offset, stride)
            for there, (order, offset, stride) in zip(columns, pieces)
        ]
    return units


def square_units(sizes, arrays, start, table):
    units = []
    for columns, pieces in zip(cut(arrays[0].shape[-1], len(table)), table):
        can_share = columns[1] // sizes["m"] % 128 == 0
        for i, (order, offset, stride) in enumerate(pieces):
            shared = can_share and "m" in order
            units.append(
                (i, order if shared else "xz", shared, columns, start + offset, stride)
            )
    return units


def finish_kernel(kept, counts, *refs):
    refs = list(refs)
    sources = [refs.pop(0) for _ in range(kept)]
    parts = [[refs.pop(0) for _ in range(n)] for n in counts]
    targets = [refs.pop(0) for _ in range(kept)]
    stages, sems = refs[-1 - kept : -1], refs[-1]
    loads, stores = [], []
    for i, (source, stage, target) in enumerate(zip(sources, stages, targets)):
        loads.append(pltpu.make_async_copy(source, stage, sems.at[i]))
        stores.append(pltpu.make_async_copy(stage, target, sems.at[kept + i]))
    for load in loads:
        load.start()
    for load, store in zip(loads, stores):
        load.wait()
        store.start()
    for group, out in zip(parts, refs):
        first = 0
        for part in group:
            out[:, pl.ds(first, part.shape[1])] = part[...]
            first += part.shape[1]
    for store in stores:
        store.wait()


def finish(arrays, groups):
    anywhere, inside = pl.BlockSpec(memory_space=pl.ANY), pl.BlockSpec(memory_space=pltpu.VMEM)
    shapes = [
        jax.ShapeDtypeStruct((g[0].shape[0], sum(p.shape[1] for p in g)), F32) for g in groups
    ]
    parts = [part for g in groups for part in g]
    outs = pl.pallas_call(
        functools.partial(finish_kernel, len(arrays), [len(g) for g in groups]),
        in_specs=[anywhere] * len(arrays) + [inside] * len(parts),
        out_specs=[anywhere] * len(arrays) + [inside] * len(groups),
        out_shape=[jax.ShapeDtypeStruct(a.shape, a.dtype) for a in arrays] + shapes,
        scratch_shapes=[pltpu.VMEM(a.shape, a.dtype) for a in arrays]
        + [pltpu.SemaphoreType.DMA((2 * len(arrays),))],
        compiler_params=pltpu.CompilerParams(vmem_limit_bytes=VMEM_LIMIT),
        name="finish",
    )(*arrays, *parts)
    return outs[: len(arrays)], outs[len(arrays) :]


def shards(
    mlp_size,
    tokens,
    initial_state,
    valid,
    token_query_weight,
    token_key_weight,
    token_value_weight,
    token_output_weight,
    state_query_weight,
    state_key_weight,
    state_value_weight,
    state_update_weight,
    up_projection_weight,
    down_projection_weight,
    token_norm_gain,
    state_norm_gain,
    feedforward_norm_gain,
    state_gate_bias,
    output_cotangent,
    final_state_cotangent,
):
    rows = token_query_weight.shape[0]
    width = tokens.shape[2]
    seg_size = width // rows
    sizes = {"z": seg_size // 4, "x": 2, "c": 2, "m": mlp_size}
    half = up_projection_weight.shape[1] // 2
    small = jnp.concatenate(
        [token_norm_gain, state_norm_gain, feedforward_norm_gain, state_gate_bias]
    ).reshape(-1, 128)
    small = jnp.pad(small, ((0, 16 - small.shape[0]), (0, 0)))
    square = [
        token_query_weight,
        token_key_weight,
        token_value_weight,
        state_query_weight,
        state_key_weight,
        state_value_weight,
        state_update_weight,
        token_output_weight,
    ]
    forward = [
        weight[:, first : first + half]
        for first in (0, half)
        for weight in (up_projection_weight, down_projection_weight)
    ]
    plan = plan_gather(sizes, small, square, forward)
    x, s0, cot = tokens[0], initial_state[0], output_cotangent[0]

    def full(*names):
        return [plan.targets[n].reshape(width, width) for n in names]

    def forward_full(*names):
        return [plan.targets[n].reshape(mlp_size, width, half) for n in names]

    exchange_alone(plan.until(plan.ready((0, 1, 2, 3)), 1), "gather_first")
    gains = plan.targets[0].reshape(seg_size, -1)[:, : 4 * rows].reshape(seg_size, 4, rows)
    gains = gains.transpose(1, 0, 2).reshape(4, width).astype(F32)
    token_weights = full(1, 2, 3)
    normed_t, masked, masked_t, q, k, v = project(
        valid, x, gains, cot, token_weights, plan.until(plan.ready((4, 5, 6, 7)), 2)
    )
    state_weights, (wu,) = full(4, 5, 6), full(7)
    ready = plan.ready((9, 10))
    middle = max(plan.ready((8,)), GATHER_MIDDLE)
    snormed_t, sq, sk, sv, read, read_log, updates, states, last = state_forward(
        valid, s0, gains, state_weights, wu, k, v, plan.until(middle, 3)
    )
    (wo,) = full(8)
    mixed, token_log, resid, *ynorms = token_forward(
        valid, x, gains, q, k, v, sk, sv, wo, plan.until(ready, 4)
    )
    total, grad_total, *first_grads = feed_forward(
        True, False, (*ynorms, masked, masked_t), resid, resid, *forward_full(9, 10),
        plan.until(plan.ready((11, 12)), 5),
    )

    def parted(grads):
        shape = (seg_size // 4, 2, 2, rows)
        return [
            g.reshape((mlp_size,) + shape + (half,)) if g.ndim == 3 else g.reshape(shape + (width,))
            for g in grads
        ]

    sums = Scatter(sizes)
    rounds = iter(SCATTER_ROUNDS)

    def next_rounds(collective_id):
        return sums.until(sums.round + next(rounds), collective_id)

    units_first = sums.add(parted(first_grads), forward_units(first_grads, 0, SCATTER_FIRST))
    out, grad_total, *last_grads = feed_forward(
        False, True, (*ynorms, masked, masked_t), total, grad_total, *forward_full(11, 12),
        next_rounds(6),
    )
    units_last = sums.add(parted(last_grads), forward_units(last_grads, sums.round, SCATTER_LAST))
    grad_resid, mlp_gain_grad, dq, near_k, near_v, dsk, dsv, *early_grads = token_backward(
        valid, resid, gains, masked, grad_total, normed_t, snormed_t,
        q, k, v, sk, sv, wo, mixed, token_log, next_rounds(7),
    )
    units_early = sums.add(
        parted(early_grads), square_units(sizes, early_grads, sums.round, SCATTER_EARLY)
    )
    dk, dv, grad_state, state_gain_grad, bias_grad, *late_grads = state_backward(
        valid, final_state_cotangent[0], gains, state_weights, wu,
        states, updates, sq, k, v, read, read_log, near_k, near_v, dsk, dsv, normed_t, snormed_t,
        next_rounds(8),
    )
    units_late = sums.add(
        parted(late_grads), square_units(sizes, late_grads, sums.round, SCATTER_LATE)
    )
    small_unit = sums.add_small(mlp_gain_grad)
    grad_tokens, _ = token_grad(
        x, gains, grad_resid, [dq, dk, dv], token_weights,
        [state_gain_grad, mlp_gain_grad, bias_grad], sums, sums.until(sums.all(), 9),
    )
    small_sum = small_unit.result[:4].reshape(4, seg_size, rows)
    small_sum = lax.dynamic_index_in_dim(small_sum, lax.axis_index("seg"), 1, keepdims=False)

    def group(units, i, count):
        return [unit.result for unit in units[i::count]]

    def forward_group(i):
        return [
            unit.result
            for units in (units_first, units_last)
            for unit in units[i * len(units) // 2 : (i + 1) * len(units) // 2]
        ]

    own_results, weight_sums = finish(
        [last, out, grad_state, grad_tokens],
        [
            group(units_early, 1, 4),
            group(units_late, 0, 4),
            group(units_late, 1, 4),
            group(units_early, 0, 4),
            group(units_late, 2, 4),
            group(units_early, 2, 4),
            group(units_early, 3, 4),
            group(units_late, 3, 4),
            forward_group(0),
            forward_group(1),
        ],
    )
    return (
        *[own_results[i][None] for i in (1, 0, 3, 2)],
        *weight_sums,
        *[small_sum[i] for i in range(4)],
    )


def solution(mesh):
    own = P(("seg", "mlp"), None, None)
    square, forward, small = P("seg", None), P("seg", "mlp"), P("seg")
    return jax.shard_map(
        functools.partial(shards, mesh.shape["mlp"]),
        mesh=mesh,
        in_specs=(own, own, P(("seg", "mlp")))
        + (square,) * 8
        + (forward,) * 2
        + (small,) * 4
        + (own, own),
        out_specs=(own,) * 4 + (square,) * 8 + (forward,) * 2 + (small,) * 4,
        check_vma=False,
    )
```

```python
import functools
import jax
import jax.numpy as jnp
from jax import lax
from jax.experimental import pallas as pl
from jax.experimental.pallas import tpu as pltpu
from jax.sharding import PartitionSpec as P

BF16 = jnp.bfloat16
F32 = jnp.float32
VMEM_LIMIT = 60 << 20
GATHER_SQUARE = (
    ((0, 1), ("zx", "zxm", "zxm"), 1),
    ((2, 3), ("zx", "zxm", "zxm"), 1),
    ((4, 4), ("zx", "zxm"), 1),
    ((5, 5), ("zx", "zxm"), 1),
)
GATHER_FORWARD = (((6, 6), 1), ((7, 7), 1), ((9, 9), 1), ((10, 10), 1))
GATHER_MIDDLE = 9
SCATTER_FIRST = ((("mxz", 0, 1), ("xmz", 0, 1)), (("mxz", 1, 1), ("xmz", 1, 1)))
SCATTER_LAST = SCATTER_FIRST
SCATTER_EARLY = (
    (("xz", 0, 1), ("mxz", 0, 1), ("mxz", 0, 1), ("xz", 0, 1)),
    (("mxz", 1, 1), ("mxz", 1, 1), ("xz", 1, 1), ("mxz", 1, 1)),
)
SCATTER_LATE = SCATTER_EARLY
SCATTER_ROUNDS = (3, 3, 2)
LINK_RATE = 85e3
CORE_RATE = 560e3
START_COST = 2.5
STEP_COST = 0.3
LATENCY = 2.0


class Place:
    def __init__(self, sizes):
        seg = lax.axis_index("seg")
        self.sizes = sizes
        self.at = {
            "z": lax.div(seg, 4),
            "x": lax.rem(lax.div(seg, 2), 2),
            "c": lax.rem(seg, 2),
            "m": lax.axis_index("mlp"),
        }

    def device(self, moved):
        at = {**self.at, **moved}
        return (at["z"] * 4 + at["x"] * 2 + at["c"], at["m"])

    def ahead(self, axis, step):
        return lax.rem(self.at[axis] + step, self.sizes[axis])

    def behind(self, axis, step):
        return lax.rem(self.at[axis] + self.sizes[axis] - step, self.sizes[axis])

    def greet(self):
        barrier = pltpu.get_barrier_semaphore()
        count = 0
        for axis in "zxcm":
            for step in range(1, self.sizes[axis]):
                pl.semaphore_signal(
                    barrier,
                    inc=1,
                    device_id=self.device({axis: self.ahead(axis, step)}),
                    device_id_type=pl.DeviceIdType.MESH,
                )
                count += 1
        pl.semaphore_wait(barrier, count)


class Flow:
    def __init__(self, place, send, recv, taken):
        self.place, self.send, self.recv, self.taken = place, send, recv, taken
        self.steps, self.arriving, self.sent = [], [], []

    def move(self, actions, make):
        pair = self.taken[0]
        self.taken[0] += 1

        def copy(source, target, moved):
            return pltpu.make_async_remote_copy(
                src_ref=source,
                dst_ref=target,
                send_sem=self.send.at[pair],
                recv_sem=self.recv.at[pair],
                device_id=self.place.device(moved),
                device_id_type=pl.DeviceIdType.MESH,
            )

        def outgoing():
            source, target, moved, _ = make()
            return copy(source, target, moved)

        def incoming():
            _, _, moved, landing = make()
            return copy(landing, landing, moved)

        actions.append(lambda: outgoing().start())
        self.sent.append(lambda: outgoing().wait_send())
        self.arriving.append(lambda: incoming().wait_recv())

    def arrived(self):
        waits, self.arriving = self.arriving, []
        return waits


def gather_steps(flow, source, target, order, split, columns, skipped, local_sem, begin, end):
    place = flow.place
    at, sizes = place.at, place.sizes
    lead = ("m" if len(target.shape) == 6 else "") + "zxc"
    first_column, width = columns
    share = width // sizes["m"] if split else width

    def block(done, moved, skip=0):
        first = first_column + skip
        if not split or "m" in done:
            lanes = pl.ds(first, width)
        else:
            lanes = pl.ds(pl.multiple_of(first + moved.get("m", at["m"]) * share, 128), share)
        return (pl.ds(0, source.shape[0]), lanes)

    def view(done, **moved):
        index = tuple(
            moved[a] if a in moved else pl.ds(0, sizes[a]) if a in done else at[a] for a in lead
        )
        return target.at[index + block(done, moved)]

    def own_source():
        return source.at[block("", {}, skipped)]

    def own():
        return pltpu.make_async_copy(own_source(), view(""), local_sem)

    waits = []
    for i, axis in enumerate(order + "c"):
        done = order[:i]
        if not begin <= i < end:
            continue
        actions = flow.arrived() + waits
        waits = []
        if i == 0:
            actions.append(lambda: own().start())
            waits.append(lambda: own().wait())
        for step in range(1, sizes[axis]):

            def make(axis=axis, step=step, done=done):
                return (
                    view(done) if done else own_source(),
                    view(done),
                    {axis: place.ahead(axis, step)},
                    view(done, **{axis: place.behind(axis, step)}),
                )

            flow.move(actions, make)
        flow.steps.append(actions)
    flow.last = flow.arrived() + waits + flow.sent


def add_into(total, term):
    lead = total.shape[:-2]

    def body(i, carry):
        index, rest = [], i
        for size in reversed(lead):
            index.append(lax.rem(rest, size))
            rest = lax.div(rest, size)
        there = tuple(reversed(index)) + (Ellipsis,)
        total[there] = total[there] + term[there]
        return carry

    lax.fori_loop(0, functools.reduce(lambda a, b: a * b, lead, 1), body, 0)


class ScatterUnit:
    def __init__(self, sizes, grad, order, split, columns, start, stride):
        self.sizes, self.grad, self.order, self.split = sizes, grad, order, split
        self.columns, self.start, self.stride = columns, start, stride
        self.whole_m = grad.ndim == 6
        self.lead = ("m" if self.whole_m else "") + "zx"
        self.rows, self.width = grad.shape[-2], columns[1]
        self.share = self.width // sizes["m"] if split else self.width
        self.count = 1 + len(order) + (not self.whole_m)
        self.spec = pl.BlockSpec(memory_space=pl.ANY)
        self.state = self.result = None

    def left(self, done):
        width = self.share if "m" in done else self.width
        return tuple(self.sizes[a] for a in self.lead if a not in done) + (self.rows, width)

    def shapes(self, begin, end):
        shapes = [self.left(self.order[: max(begin - 1, 0)])]
        for i in range(begin, end):
            if i == 0:
                shapes.append(self.left(""))
            elif i <= len(self.order):
                axis = self.order[i - 1]
                shapes.append((self.sizes[axis] - 1,) + self.left(self.order[:i]))
            elif self.split:
                shapes.append((self.rows, self.width))
            else:
                shapes.append((self.sizes["m"], self.rows, self.width))
        return shapes

    def steps(self, flow, grad, state, saved, result, buffers, local_sem, begin, end):
        place, at, sizes, order = flow.place, flow.place.at, self.sizes, self.order
        own, landings = buffers[0], dict(zip(range(begin, end), buffers[1:]))
        gone = order[: max(begin - 1, 0)]
        lead = [a for a in self.lead if a not in gone]
        narrow = self.split and "m" in gone

        def lanes_of(place_m):
            return pl.ds(pl.multiple_of(place_m * self.share, 128), self.share)

        def grad_half(core):
            index = tuple(pl.ds(0, sizes[a]) for a in self.lead)
            return grad.at[index + (core, pl.ds(0, self.rows), pl.ds(*self.columns))]

        def view(done, **moved):
            index = tuple(
                moved[a] if a in moved else at[a] if a in done else pl.ds(0, sizes[a]) for a in lead
            )
            lanes = pl.ds(0, self.share if narrow else self.width)
            if self.split and not narrow and ("m" in done or "m" in moved):
                lanes = lanes_of(moved.get("m", at["m"]))
            return own.at[index + (pl.ds(0, self.rows), lanes)]

        def load():
            return pltpu.make_async_copy(grad_half(at["c"]) if begin == 0 else state, own, local_sem)

        def added(axis, done, landing):
            return [
                lambda step=step: add_into(view(done), landing.at[step - 1])
                for step in range(1, sizes[axis])
            ]

        ahead = [lambda: load().start()]
        actions = []
        if begin > 0:
            actions.append(lambda: load().wait())
        for i in range(begin, end):
            landing = landings[i]
            if i == 0:
                flow.move(
                    actions,
                    lambda landing=landing: (
                        grad_half(1 - at["c"]), landing, {"c": 1 - at["c"]}, landing
                    ),
                )
                flow.steps.append(actions)
                actions = [lambda: load().wait()] + flow.arrived()
                actions.append(lambda landing=landing: add_into(own, landing))
            elif i <= len(order):
                axis, done = order[i - 1], order[: i - 1]
                for step in range(1, sizes[axis]):

                    def make(axis=axis, step=step, done=done, landing=landing):
                        there = place.ahead(axis, step)
                        slot = landing.at[step - 1]
                        return (view(done, **{axis: there}), slot, {axis: there}, slot)

                    flow.move(actions, make)
                flow.steps.append(actions)
                actions = flow.arrived() + added(axis, order[:i], landing)
            else:

                def part(place_m, landing=landing):
                    if self.split:
                        return landing.at[pl.ds(0, self.rows), lanes_of(place_m)]
                    return landing.at[place_m]

                def keep():
                    part(at["m"])[...] = view(order)[...]

                actions.append(keep)
                for step in range(1, sizes["m"]):
                    flow.move(
                        actions,
                        lambda step=step: (
                            part(at["m"]),
                            part(at["m"]),
                            {"m": place.ahead("m", step)},
                            part(place.behind("m", step)),
                        ),
                    )
                flow.steps.append(actions)
                actions = flow.arrived()
        if end == self.count:

            def store():
                if self.whole_m:
                    total = view(order)[...].astype(F32)
                elif self.split:
                    total = landing[...].astype(F32)
                else:
                    total = landing[0].astype(F32)
                    for i in range(1, sizes["m"]):
                        total = total + landing[i].astype(F32)
                result[...] = total

            return ahead, actions + [store], flow.sent

        def save():
            return pltpu.make_async_copy(view(order[: end - 1]), saved, local_sem)

        return ahead, actions + [lambda: save().start()], flow.sent + [lambda: save().wait()]


def step_time(sizes, axis, size):
    if axis == "c":
        return size / CORE_RATE
    return 2 * size * ((sizes["z"] // 2) ** 2 if axis == "z" else sizes[axis] - 1) / LINK_RATE


def round_times(sizes, rounds):
    now, free, ended, times = START_COST, {axis: 0.0 for axis in "zxcm"}, {}, []
    for there in rounds:
        for unit, step, axis, size in there:
            now = max(now, ended.get((unit, step - 1), 0.0)) + STEP_COST
            free[axis] = max(free[axis], now) + step_time(sizes, axis, size)
            ended[unit, step] = free[axis] + LATENCY
        times.append(now)
    return times, max(ended.values())


class Gather:
    def __init__(self, sizes, arrays, spans, units):
        self.sizes, self.arrays, self.spans, self.round = sizes, arrays, spans, 0
        self.units = [unit[:-2] for unit in units]
        self.starts = [unit[-2:] for unit in units]
        self.targets = [None] * len(arrays)

    def ready(self, names):
        return max(
            self.stop(start, unit) for start, unit in zip(self.starts, self.units) if unit[0] in names
        )

    def stop(self, start, unit):
        return start[0] + len(unit[1]) * start[1] + 1

    def until(self, end, collective_id):
        begin, self.round = self.round, max(end, self.round)
        return GatherPart(self, begin, end, collective_id) if begin < end else None


class GatherPart:
    def __init__(self, plan, begin, end, collective_id):
        self.plan, self.begin, self.end, self.collective_id = plan, begin, end, collective_id
        self.units = [
            (start, unit)
            for start, unit in zip(plan.starts, plan.units)
            if start[0] < end and plan.stop(start, unit) > begin
        ]
        self.names = sorted({unit[0] for _, unit in self.units})
        split = {unit[0]: unit[2] for _, unit in self.units}
        order = {unit[0]: unit[1] for _, unit in self.units}
        sizes = plan.sizes
        anywhere = pl.BlockSpec(memory_space=pl.ANY)
        old = [n for n in self.names if plan.targets[n] is not None]
        self.arrays = [plan.arrays[n] for n in self.names] + [plan.targets[n] for n in old]
        self.specs = [anywhere] * len(self.arrays)
        self.out_shape = [
            jax.ShapeDtypeStruct(
                ((sizes["m"],) if "m" in order[n] and not split[n] else ())
                + (sizes["z"], 2, 2)
                + (plan.arrays[n].shape[0], plan.spans[n][1]),
                plan.arrays[n].dtype,
            )
            for n in self.names
        ]
        self.out_specs = [anywhere] * len(self.names)
        self.aliases = {len(self.names) + i: self.names.index(n) for i, n in enumerate(old)}
        pairs = len(self.units) * (sum(sizes.values()) - 4)
        self.scratch = [
            pltpu.SemaphoreType.DMA((pairs,)),
            pltpu.SemaphoreType.DMA((pairs,)),
            pltpu.SemaphoreType.DMA((len(self.units),)),
        ]

    def times(self, busy):
        sizes = self.plan.sizes
        loads = [{axis: 0.0 for axis in "zxcm"} for _ in range(self.end - self.begin)]
        for (start, stride), (n, order, split, columns) in self.units:
            size = self.plan.arrays[n].shape[0] * columns[1] * self.plan.arrays[n].dtype.itemsize
            if split:
                size //= sizes["m"]
            for i, axis in enumerate(order + "c"):
                if self.begin <= start + i * stride < self.end:
                    loads[start + i * stride - self.begin][axis] += step_time(sizes, axis, size)
                size *= sizes[axis]
        times = [0.0]
        for load in loads:
            times.append(times[-1] + max(load.values()) + LATENCY)
        return times[:-1], busy

    def rounds(self, ins, outs, scratch):
        place = Place(self.plan.sizes)
        send, recv, local = scratch
        taken = [0]
        rounds = [[] for _ in range(self.end - self.begin)]
        last = []
        for i, ((start, stride), (n, order, split, columns)) in enumerate(self.units):
            flow = Flow(place, send, recv, taken)
            begin, end = [max(-((start - to) // stride), 0) for to in (self.begin, self.end)]
            slot = self.names.index(n)
            gather_steps(
                flow, ins[slot], outs[slot], order, split, columns, self.plan.spans[n][0],
                local.at[i], begin, end,
            )
            for step, actions in enumerate(flow.steps):
                there = rounds[start + (begin + step) * stride - self.begin]
                there.insert(0 if begin + step == 0 else len(there), actions)
            last += flow.last
        rounds = [[action for actions in there for action in actions] for there in rounds]
        rounds[0].insert(0, place.greet)
        return rounds, last

    def received(self, outs):
        for n, out in zip(self.names, outs):
            self.plan.targets[n] = out


class SmallUnit:
    def __init__(self, plan, row, start):
        self.plan, self.grad, self.start, self.stride = plan, row, start, 1
        self.order, self.count = "xzm", 4
        self.rows, self.width = 8, row.shape[1]
        self.share = self.width
        self.spec = pl.BlockSpec(memory_space=pl.ANY)
        self.state = self.result = None

    def left(self, done):
        return (self.rows, self.width)

    def shapes(self, begin, end):
        sizes = self.plan.sizes
        return [self.left("")] + [(sizes[axis],) + self.left("") for axis in "c" + self.order]

    def steps(self, flow, row, state, saved, result, buffers, local_sem, begin, end):
        place, at = flow.place, flow.place.at
        own, landings = buffers[0], buffers[1:]
        actions = []

        def fill():
            own[...] = jnp.zeros_like(own)
            for i, row in enumerate(self.plan.rows):
                own[pl.ds(i, 1), :] = row[...]

        actions.append(fill)
        for axis, landing in zip("c" + self.order, landings):

            def keep(axis=axis, landing=landing):
                landing[at[axis]] = own[...]

            actions.append(keep)
            for step in range(1, place.sizes[axis]):

                def make(axis=axis, landing=landing, step=step):
                    slot = landing.at[at[axis]]
                    return (slot, slot, {axis: place.ahead(axis, step)}, landing.at[place.behind(axis, step)])

                flow.move(actions, make)
            flow.steps.append(actions)

            def add(axis=axis, landing=landing):
                total = landing[0]
                for i in range(1, place.sizes[axis]):
                    total = total + landing[i]
                own[...] = total

            actions = flow.arrived() + [add]

        def store():
            result[...] = own[...]

        return [], actions + [store], flow.sent


class Scatter:
    def __init__(self, sizes):
        self.sizes, self.units, self.round = sizes, [], 0

    def add(self, arrays, units):
        for i, order, split, columns, start, stride in units:
            assert start >= self.round
            self.units.append(
                ScatterUnit(self.sizes, arrays[i], order, split, columns, start, stride)
            )
        return self.units[len(self.units) - len(units) :]

    def add_small(self, row):
        self.units.append(SmallUnit(self, row, self.all() - 4))
        return self.units[-1]

    def all(self):
        return max(unit.start + (unit.count - 1) * unit.stride + 1 for unit in self.units)

    def until(self, end, collective_id):
        begin, self.round = self.round, max(end, self.round)
        part = ScatterPart(self, begin, end, collective_id)
        return part if part.units else None


class ScatterPart:
    aliases = {}

    def __init__(self, plan, begin, end, collective_id):
        self.sizes, self.begin, self.end, self.collective_id = plan.sizes, begin, end, collective_id
        self.units = []
        buffers, pairs = [], 0
        self.arrays, self.out_shape, self.out_specs = [], [], []
        for unit in plan.units:
            first, stop = [
                min(max(-((unit.start - to) // unit.stride), 0), unit.count) for to in (begin, end)
            ]
            if first >= stop:
                continue
            self.units.append((unit, first, stop))
            self.arrays.append(unit.state if first else unit.grad)
            if stop == unit.count:
                shape = (unit.rows, unit.width)
                self.out_shape.append(jax.ShapeDtypeStruct(shape, F32))
                self.out_specs.append(
                    pl.BlockSpec(shape, lambda *_: (0, 0), pipeline_mode=pl.Buffered(1))
                )
            else:
                shape = unit.left(unit.order[: stop - 1])
                self.out_shape.append(jax.ShapeDtypeStruct(shape, unit.grad.dtype))
                self.out_specs.append(pl.BlockSpec(memory_space=pl.ANY))
            buffers += [pltpu.VMEM(shape, unit.grad.dtype) for shape in unit.shapes(first, stop)]
            pairs += sum(self.sizes.values()) - 4 + self.sizes["m"] - 1
        self.specs = [unit.spec for unit, _, _ in self.units]
        self.scratch = buffers + [
            pltpu.SemaphoreType.DMA((pairs,)),
            pltpu.SemaphoreType.DMA((pairs,)),
            pltpu.SemaphoreType.DMA((len(self.units),)),
        ]

    def times(self, busy):
        rounds = [[] for _ in range(self.end - self.begin)]
        for n, (unit, first, stop) in enumerate(self.units):
            for i in range(first, stop):
                done = unit.order[:i]
                axis = ("c" + unit.order + "m")[i]
                shape = unit.left(done) if i <= len(unit.order) else (unit.rows, unit.share)
                size = functools.reduce(lambda a, b: a * b, shape, unit.grad.dtype.itemsize)
                rounds[unit.start + i * unit.stride - self.begin].append((n, i, axis, size))
        times, length = round_times(self.sizes, rounds)
        return times, busy if length > 2.0 * busy else length

    def rounds(self, ins, outs, scratch):
        place = Place(self.sizes)
        send, recv, local = scratch[-3:]
        buffers = list(scratch[:-3])
        taken = [0]
        rounds = [[] for _ in range(self.end - self.begin)]
        start_up, ends, waits = [], [], []
        for i, (unit, first, stop) in enumerate(self.units):
            flow = Flow(place, send, recv, taken)
            count = 1 + stop - first
            mine, buffers = buffers[:count], buffers[count:]
            done = stop == unit.count
            ahead, end, wait = unit.steps(
                flow, ins[i], ins[i], None if done else outs[i], outs[i] if done else None,
                mine, local.at[i], first, stop,
            )
            if first:
                start_up += ahead
            else:
                flow.steps[0][:0] = ahead
            for step, actions in enumerate(flow.steps):
                rounds[unit.start + (first + step) * unit.stride - self.begin].append(actions)
            after = unit.start + stop * unit.stride - self.begin
            if done and after < len(rounds):
                rounds[after].append(end)
            else:
                ends += end
            waits += wait
        rounds = [[action for actions in there for action in actions] for there in rounds]
        rounds[0][:0] = start_up + [place.greet]
        return rounds, ends + waits

    def received(self, outs):
        for (unit, first, stop), out in zip(self.units, outs):
            if stop == unit.count:
                unit.result = out
            else:
                unit.state = out


def run_all(actions):
    for action in actions:
        action()


def run_kernel(
    body, args, *, grid, in_specs, out_specs, out_shape, name, scratch_shapes=(), exchange=None, polls=1,
    busy=0.0,
):
    if exchange is None:
        return pl.pallas_call(
            functools.partial(body, lambda: None),
            grid=grid,
            in_specs=in_specs,
            out_specs=out_specs,
            out_shape=out_shape,
            scratch_shapes=scratch_shapes,
            compiler_params=pltpu.CompilerParams(vmem_limit_bytes=VMEM_LIMIT),
            name=name,
        )(*args)
    counts = (len(args), len(exchange.arrays), len(out_shape), len(exchange.out_shape))
    total = functools.reduce(lambda a, b: a * b, grid, 1)
    times, pace = exchange.times(busy)

    def kernel(*refs):
        refs = list(refs)
        ins, sent, outs, received = [[refs.pop(0) for _ in range(n)] for n in counts]
        own = [refs.pop(0) for _ in range(len(scratch_shapes))]
        step = 0
        for i, size in enumerate(grid):
            step = step * size + pl.program_id(i)
        rounds, last = exchange.rounds(sent, received, refs)
        slots, after = {}, []
        for i, (actions, time) in enumerate(zip(rounds, times)):
            slot = int(total * polls * time / pace + 0.5) if busy and i else 0
            if slot >= total * polls or i and not busy:
                after += actions
            else:
                slots.setdefault((slot % polls, slot // polls), []).extend(actions)
        called = [0]

        def poll():
            for at_step in range(total):
                actions = slots.get((called[0], at_step))
                if actions:
                    pl.when(step == at_step)(functools.partial(run_all, actions))
            called[0] += 1

        body(poll, *ins, *outs, *own)
        assert called[0] == polls
        pl.when(step == total - 1)(functools.partial(run_all, after + last))

    outs = pl.pallas_call(
        kernel,
        grid=grid,
        in_specs=list(in_specs) + exchange.specs,
        out_specs=list(out_specs) + exchange.out_specs,
        out_shape=list(out_shape) + exchange.out_shape,
        scratch_shapes=list(scratch_shapes) + exchange.scratch,
        input_output_aliases={counts[0] + i: counts[2] + o for i, o in exchange.aliases.items()},
        compiler_params=pltpu.CompilerParams(
            vmem_limit_bytes=VMEM_LIMIT,
            collective_id=exchange.collective_id,
            has_side_effects=True,
        ),
        name=name,
    )(*args, *exchange.arrays)
    exchange.received(outs[counts[2] :])
    return outs[: counts[2]]


def exchange_alone(exchange, name):
    run_kernel(
        lambda poll: poll(), [], grid=(1,), in_specs=[], out_specs=[], out_shape=[], name=name,
        exchange=exchange,
    )


HEAD = 128
BLOCK = 512
EPS = 1e-06
NEGATIVE = -1e30
GELU_C = 0.7978845608
GELU_K = 0.044715
SCALE = HEAD**-0.5
LOG2E = 1.4426950408889634
PAIR = 2 * HEAD
TILE = 256


def matmul(left, right):
    return jnp.dot(left, right, preferred_element_type=F32)


def matmul_nt(left, right):
    return lax.dot_general(left, right, (((1,), (1,)), ((), ())), preferred_element_type=F32)


def inverse_rms(values):
    return lax.rsqrt(jnp.mean(values * values, axis=-1, keepdims=True) + EPS)


def rms_backward(values, gain, grad):
    inverse = inverse_rms(values)
    unit = values * inverse
    weighted = grad * gain
    inner = jnp.mean(weighted * unit, axis=-1, keepdims=True)
    return inverse * (weighted - unit * inner), grad * unit


def row_of(gains, i):
    return gains[pl.ds(i, 1), :]


def whole(shape):
    return pl.BlockSpec(shape, lambda *_: (0,) * len(shape))


def project_kernel(
    poll, valid, x_ref, gains, cot, wq, wk, wv, normed_t, masked, masked_t, q, k, v, normed
):
    @pl.when(pl.program_id(0) == 0)
    def _():
        x = x_ref[...].astype(F32)
        rows = (x * inverse_rms(x) * row_of(gains, 0)).astype(BF16)
        normed[...] = rows
        normed_t[...] = rows.T
        keep = position(cot.shape, 0) < valid[0]
        grad = jnp.where(keep, cot[...], jnp.zeros_like(cot))
        masked[...] = grad
        masked_t[...] = grad.T

    rows = normed[...]
    for weight, out in ((wq, q), (wk, k), (wv, v)):
        poll()
        out[...] = matmul(rows, weight[...]).astype(BF16)


def project(valid, x, gains, cot, weights, exchange):
    rows, width = x.shape
    tile = pl.BlockSpec((width, TILE), lambda j: (0, j))
    out = pl.BlockSpec((rows, TILE), lambda j: (0, j))
    full = whole((rows, width))
    turned = whole((width, rows))
    return run_kernel(
        project_kernel,
        (valid, x, gains, cot, *weights),
        grid=(width // TILE,),
        in_specs=[pl.BlockSpec(memory_space=pltpu.SMEM), full, whole(gains.shape), full]
        + [tile] * 3,
        out_specs=[turned, full, turned, out, out, out],
        out_shape=[
            jax.ShapeDtypeStruct((width, rows), BF16),
            jax.ShapeDtypeStruct((rows, width), BF16),
            jax.ShapeDtypeStruct((width, rows), BF16),
        ]
        + [jax.ShapeDtypeStruct((rows, width), BF16)] * 3,
        scratch_shapes=[pltpu.VMEM((rows, width), BF16)],
        name="project_tokens",
        exchange=exchange,
        busy=14.0,
        polls=3,
    )


def attend(query, pieces):
    scores = []
    for keys, _, mask in pieces:
        score = matmul_nt(keys, query) * (SCALE * LOG2E)
        scores.append(score if mask is None else jnp.where(mask, score, NEGATIVE))
    top = functools.reduce(jnp.maximum, [jnp.max(s, axis=0, keepdims=True) for s in scores])
    total, mixed = 0.0, 0.0
    for score, (_, values, _) in zip(scores, pieces):
        weights = jnp.exp2(score - top)
        total = total + jnp.sum(weights, axis=0, keepdims=True)
        mixed = mixed + matmul(values.T, weights.astype(BF16))
    return (mixed / total).T.astype(BF16), top + jnp.log2(total)


def attend_backward(query, log_total, grad, centre, pieces):
    grad_query = 0.0
    for keys, values, mask, add_keys, add_values in pieces:
        score = matmul_nt(keys, query) * (SCALE * LOG2E)
        if mask is not None:
            score = jnp.where(mask, score, NEGATIVE)
        probs = jnp.exp2(score - log_total)
        add_values(matmul(probs.astype(BF16), grad))
        grad_probs = matmul_nt(values, grad)
        grad_scores = (probs * (grad_probs - centre)).astype(BF16)
        add_keys(matmul(grad_scores, query) * SCALE)
        grad_query = grad_query + matmul(keys.T, grad_scores)
    return (grad_query * SCALE).T


def centre_of(grad, mixed):
    return jnp.sum((grad.astype(F32) * mixed.astype(F32)).T, axis=0, keepdims=True)


def position(shape, axis):
    return lax.broadcasted_iota(jnp.int32, shape, axis)


def token_pieces(block, half, valid):
    key = position((TILE, TILE), 0)
    query = position((TILE, TILE), 1)
    causal, recent = key <= query, key > query
    pieces = []
    if block:
        start = (block - 1) * BLOCK
        pieces.append(("near", start + half * TILE, TILE, recent))
        if half == 0:
            pieces.append(("near", start + TILE, TILE, None))
    start = block * BLOCK
    for piece in range(half + 1):
        first = start + piece * TILE
        seen = first + key < valid
        mask = causal if piece == half else None
        if block:
            mask = seen if mask is None else mask & seen
        pieces.append(("near", first, TILE, mask))
    pieces.append(("state", block * BLOCK, BLOCK, None))
    return pieces


def state_forward_kernel(
    poll, valid, s0, gains, wq, wk, wv, wu, k, v,
    normed_t, sq, sk, sv, read, log_out, update_out, states, last,
    state, normed, total,
):
    block, pair = pl.program_id(0), pl.program_id(1)

    @pl.when((block == 0) & (pair == 0))
    def _():
        state[...] = s0[...].astype(F32)

    @pl.when(pair == 0)
    def _():
        now = state[...]
        rows = (now * inverse_rms(now) * row_of(gains, 1)).astype(BF16)
        normed[...] = rows
        normed_t[...] = rows.T
        states[...] = now
        total[...] = jnp.zeros_like(total)

    poll()
    rows = normed[...]
    for weight, out in ((wq, sq), (wk, sk), (wv, sv)):
        out[...] = matmul(rows, weight[...]).astype(BF16)
    poll()
    seen = block * BLOCK + position((BLOCK, BLOCK), 0) < valid[0]
    for head in range(2):
        lanes = pl.ds(head * HEAD, HEAD)
        read[:, lanes], log_out[0, 0, pl.ds(head, 1), :] = attend(
            sq[:, lanes], [(k[:, lanes], v[:, lanes], seen)]
        )
    total[...] += matmul(read[...], wu[...])

    @pl.when(pair == pl.num_programs(1) - 1)
    def _():
        update = total[...]
        gate = 1.0 / (1.0 + jnp.exp(-row_of(gains, 3)))
        later = gate * state[...] + (1.0 - gate) * update
        update_out[...] = update
        state[...] = later
        last[...] = later.astype(BF16)


def state_forward(valid, s0, gains, weights, update_weight, k, v, exchange):
    rows, width = s0.shape
    blocks, pairs = k.shape[0] // BLOCK, width // PAIR
    columns = pl.BlockSpec((width, PAIR), lambda b, p: (0, p))
    tile = pl.BlockSpec((rows, PAIR), lambda b, p: (b, p))
    band = pl.BlockSpec((rows, width), lambda b, p: (b, 0))

    def stack(kind):
        return jax.ShapeDtypeStruct((blocks * rows, width), kind)

    return run_kernel(
        state_forward_kernel,
        (valid, s0, gains, *weights, update_weight, k, v),
        grid=(blocks, pairs),
        in_specs=[
            pl.BlockSpec(memory_space=pltpu.SMEM), whole((rows, width)), whole(gains.shape),
            columns, columns, columns, pl.BlockSpec((PAIR, width), lambda b, p: (p, 0)),
            pl.BlockSpec((BLOCK, PAIR), lambda b, p: (b, p)),
            pl.BlockSpec((BLOCK, PAIR), lambda b, p: (b, p)),
        ],
        out_specs=[
            pl.BlockSpec((width, rows), lambda b, p: (0, b)), tile, tile, tile, tile,
            pl.BlockSpec((1, 1, 2, rows), lambda b, p: (b, p, 0, 0)),
            band, band, whole((rows, width)),
        ],
        out_shape=[
            jax.ShapeDtypeStruct((width, blocks * rows), BF16),
            stack(BF16), stack(BF16), stack(BF16), stack(BF16),
            jax.ShapeDtypeStruct((blocks, pairs, 2, rows), F32),
            stack(F32), stack(F32), jax.ShapeDtypeStruct((rows, width), BF16),
        ],
        scratch_shapes=[
            pltpu.VMEM((rows, width), F32), pltpu.VMEM((rows, width), BF16),
            pltpu.VMEM((rows, width), F32),
        ],
        name="state_forward",
        exchange=exchange,
        busy=27.7,
        polls=2,
    )


def token_forward_kernel(
    poll, valid, x, gains, q, k, v, sk, sv, wo, mixed, log_out, resid, ynorm, ynorm_t
):
    pair = pl.program_id(0)

    @pl.when(pair == 0)
    def _():
        resid[...] = x[...].astype(F32)

    count = valid[0]
    for head in range(2):
        lanes = pl.ds(head * HEAD, HEAD)
        poll()
        for block in range(q.shape[0] // BLOCK):
            for half in range(BLOCK // TILE):
                rows = pl.ds(block * BLOCK + half * TILE, TILE)
                pieces = []
                for kind, first, size, mask in token_pieces(block, half, count):
                    keys, values = (k, v) if kind == "near" else (sk, sv)
                    there = pl.ds(first, size)
                    pieces.append((keys[there, lanes], values[there, lanes], mask))
                mixed[rows, lanes], log_out[0, pl.ds(head, 1), rows] = attend(
                    q[rows, lanes], pieces
                )
    resid[...] += matmul(mixed[...], wo[...])

    @pl.when(pair == pl.num_programs(0) - 1)
    def _():
        rows = resid[...]
        rounded = (rows * inverse_rms(rows) * row_of(gains, 2)).astype(BF16)
        ynorm[...] = rounded
        ynorm_t[...] = rounded.T


def token_forward(valid, x, gains, q, k, v, sk, sv, wo, exchange):
    rows, width = x.shape
    pairs = width // PAIR
    tile = pl.BlockSpec((rows, PAIR), lambda p: (0, p))
    states = pl.BlockSpec((sk.shape[0], PAIR), lambda p: (0, p))
    return run_kernel(
        token_forward_kernel,
        (valid, x, gains, q, k, v, sk, sv, wo),
        grid=(pairs,),
        in_specs=[
            pl.BlockSpec(memory_space=pltpu.SMEM), whole((rows, width)), whole(gains.shape),
            tile, tile, tile, states, states, pl.BlockSpec((PAIR, width), lambda p: (p, 0)),
        ],
        out_specs=[
            tile, pl.BlockSpec((1, 2, rows), lambda p: (p, 0, 0)),
            whole((rows, width)), whole((rows, width)), whole((width, rows)),
        ],
        out_shape=[
            jax.ShapeDtypeStruct((rows, width), BF16),
            jax.ShapeDtypeStruct((pairs, 2, rows), F32),
            jax.ShapeDtypeStruct((rows, width), F32),
            jax.ShapeDtypeStruct((rows, width), BF16),
            jax.ShapeDtypeStruct((width, rows), BF16),
        ],
        name="token_forward",
        exchange=exchange,
        busy=28.4,
        polls=2,
    )


def feed_forward_kernel(
    first, final, poll, ynorm, ynorm_t, masked, masked_t, total_in, grad_in, up_w, down_w,
    out, grad_out, up_grad, down_grad,
    total, grad_total, sems,
):
    step, last = pl.program_id(0), pl.num_programs(0) - 1
    loads = [pltpu.make_async_copy(total_in, total, sems.at[0])]
    stores = [pltpu.make_async_copy(grad_total, grad_out, sems.at[1])]
    if not first:
        loads.append(pltpu.make_async_copy(grad_in, grad_total, sems.at[1]))
    if not final:
        stores.append(pltpu.make_async_copy(total, out, sems.at[0]))

    poll()

    @pl.when(step == 0)
    def _():
        for copy in loads:
            copy.start()
        if first:
            grad_total[...] = jnp.zeros_like(grad_total)

    up_part, down_part = up_w[0], down_w[0]
    up = matmul(ynorm[...], up_part)
    grad_hidden = matmul(masked[...], down_part)
    square = up * up
    bent = jnp.tanh(GELU_C * (up + GELU_K * square * up))
    hidden = (0.5 * up * (1.0 + bent)).astype(BF16)
    slope = 0.5 * (1.0 + bent) + 0.5 * up * (1.0 - bent * bent) * (
        GELU_C * (1.0 + 3.0 * GELU_K * square)
    )
    grad_up = (grad_hidden * slope).astype(BF16)
    poll()
    down_grad[0] = matmul(masked_t[...], hidden).astype(BF16)
    poll()
    up_grad[0] = matmul(ynorm_t[...], grad_up).astype(BF16)

    @pl.when(step == 0)
    def _():
        for copy in loads:
            copy.wait()

    poll()
    total[...] += matmul_nt(hidden, down_part)
    grad_total[...] += matmul_nt(grad_up, up_part)

    @pl.when(step == last)
    def _():
        for copy in stores:
            copy.start()
        if final:
            out[...] = total[...].astype(BF16)
        for copy in stores:
            copy.wait()


def feed_forward(first, final, rows_in, total, grad, up_w, down_w, exchange, chunk=512):
    rows, width = total.shape
    parts, _, part = up_w.shape
    chunk = min(chunk, part)
    each = part // chunk
    weight = pl.BlockSpec((1, width, chunk), lambda j: (j // each, 0, j % each))
    once = pl.BlockSpec((rows, width), lambda j: (0, 0), pipeline_mode=pl.Buffered(1))
    turned = pl.BlockSpec((width, rows), lambda j: (0, 0), pipeline_mode=pl.Buffered(1))
    anywhere = pl.BlockSpec(memory_space=pl.ANY)
    return run_kernel(
        functools.partial(feed_forward_kernel, first, final),
        (*rows_in, total, grad, up_w, down_w),
        grid=(parts * each,),
        in_specs=[once, turned, once, turned, anywhere, anywhere, weight, weight],
        out_specs=[once if final else anywhere, anywhere, weight, weight],
        out_shape=[
            jax.ShapeDtypeStruct((rows, width), BF16 if final else F32),
            jax.ShapeDtypeStruct((rows, width), F32),
            jax.ShapeDtypeStruct(up_w.shape, BF16),
            jax.ShapeDtypeStruct(down_w.shape, BF16),
        ],
        scratch_shapes=[
            pltpu.VMEM((rows, width), F32), pltpu.VMEM((rows, width), F32),
            pltpu.SemaphoreType.DMA((2,)),
        ],
        name="feed_forward_final" if final else "feed_forward_first",
        exchange=exchange,
        busy=38.0,
        polls=4,
    )


def token_backward_kernel(
    poll, valid, resid, gains, masked, grad_ynorm, normed_t, snormed_t,
    q, k, v, sk, sv, wo, mixed, log_total,
    grad_resid, gain_grad, dq, dk, dv, dsk, dsv, wo_grad, wq_grad, skw_grad, svw_grad,
    rounded, work, other, sems, grad_mixed, near_k, near_v, state_k, state_v,
):
    loads = [
        pltpu.make_async_copy(source, target, sems.at[i])
        for i, (source, target) in enumerate(((resid, work), (grad_ynorm, other), (masked, rounded)))
    ]
    store = pltpu.make_async_copy(work, grad_resid, sems.at[3])

    @pl.when(pl.program_id(0) == 0)
    def _():
        for copy in loads:
            copy.start()

    poll()

    @pl.when(pl.program_id(0) == 0)
    def _():
        for copy in loads:
            copy.wait()
        grad, gain_rows = rms_backward(work[...], row_of(gains, 2), other[...])
        grad = rounded[...].astype(F32) + grad
        work[...] = grad
        rounded[...] = grad.astype(BF16)
        gain_grad[...] = jnp.sum(gain_rows, axis=0, keepdims=True)
        store.start()

    @pl.when(pl.program_id(0) == pl.num_programs(0) - 1)
    def _():
        store.wait()

    grad_rows = rounded[...]
    grad_mixed[...] = matmul_nt(grad_rows, wo[...]).astype(BF16)
    wo_grad[...] = matmul(mixed[...].T, grad_rows).astype(BF16)
    for ref in (near_k, near_v, state_k, state_v):
        ref[...] = jnp.zeros_like(ref)
    count = valid[0]
    for head in range(2):
        lanes = pl.ds(head * HEAD, HEAD)

        def adder(ref, there):
            def add(term):
                ref[there, lanes] += term

            return add

        poll()
        for block in range(q.shape[0] // BLOCK):
            for half in range(BLOCK // TILE):
                rows = pl.ds(block * BLOCK + half * TILE, TILE)
                pieces = []
                for kind, first, size, mask in token_pieces(block, half, count):
                    keys, values = (k, v) if kind == "near" else (sk, sv)
                    sums = (near_k, near_v) if kind == "near" else (state_k, state_v)
                    there = pl.ds(first, size)
                    pieces.append(
                        (keys[there, lanes], values[there, lanes], mask)
                        + tuple(adder(ref, there) for ref in sums)
                    )
                out_grad = grad_mixed[rows, lanes]
                dq[rows, lanes] = attend_backward(
                    q[rows, lanes],
                    log_total[0, pl.ds(head, 1), rows],
                    out_grad,
                    centre_of(out_grad, mixed[rows, lanes]),
                    pieces,
                ).astype(BF16)
    dk[...] = near_k[...]
    dv[...] = near_v[...]
    dsk[...] = state_k[...].astype(BF16)
    dsv[...] = state_v[...].astype(BF16)
    wq_grad[...] = matmul(normed_t[...], dq[...]).astype(BF16)
    skw_grad[...] = matmul(snormed_t[...], dsk[...]).astype(BF16)
    svw_grad[...] = matmul(snormed_t[...], dsv[...]).astype(BF16)


def token_backward(
    valid, resid, gains, masked, grad_ynorm, normed_t, snormed_t,
    q, k, v, sk, sv, wo, mixed, log_total, exchange,
):
    rows, width = resid.shape
    anywhere = pl.BlockSpec(memory_space=pl.ANY)
    turned = pl.BlockSpec((width, rows), lambda p: (0, 0), pipeline_mode=pl.Buffered(1))
    turned_state = pl.BlockSpec(snormed_t.shape, lambda p: (0, 0), pipeline_mode=pl.Buffered(1))
    columns = pl.BlockSpec((width, PAIR), lambda p: (0, p))
    once = pl.BlockSpec((rows, width), lambda p: (0, 0), pipeline_mode=pl.Buffered(1))
    pairs = width // PAIR
    tile = pl.BlockSpec((rows, PAIR), lambda p: (0, p))
    states = pl.BlockSpec((sk.shape[0], PAIR), lambda p: (0, p))
    band = pl.BlockSpec((PAIR, width), lambda p: (p, 0))
    return run_kernel(
        token_backward_kernel,
        (
            valid, resid, gains, masked, grad_ynorm, normed_t, snormed_t,
            q, k, v, sk, sv, wo, mixed, log_total,
        ),
        grid=(pairs,),
        in_specs=[
            pl.BlockSpec(memory_space=pltpu.SMEM), anywhere, whole(gains.shape), anywhere, anywhere,
            turned, turned_state, tile, tile, tile, states, states, band, tile,
            pl.BlockSpec((1, 2, rows), lambda p: (p, 0, 0)),
        ],
        out_specs=[anywhere, whole((1, width)), tile, tile, tile, states, states, band]
        + [columns] * 3,
        out_shape=[
            jax.ShapeDtypeStruct((rows, width), F32),
            jax.ShapeDtypeStruct((1, width), F32),
            jax.ShapeDtypeStruct((rows, width), BF16),
            jax.ShapeDtypeStruct((rows, width), F32),
            jax.ShapeDtypeStruct((rows, width), F32),
            jax.ShapeDtypeStruct(sk.shape, BF16),
            jax.ShapeDtypeStruct(sk.shape, BF16),
        ]
        + [jax.ShapeDtypeStruct((width, width), BF16)] * 4,
        scratch_shapes=[
            pltpu.VMEM((rows, width), BF16), pltpu.VMEM((rows, width), F32),
            pltpu.VMEM((rows, width), F32), pltpu.SemaphoreType.DMA((4,)),
            pltpu.VMEM((rows, PAIR), BF16), pltpu.VMEM((rows, PAIR), F32),
            pltpu.VMEM((rows, PAIR), F32), pltpu.VMEM((sk.shape[0], PAIR), F32),
            pltpu.VMEM((sk.shape[0], PAIR), F32),
        ],
        name="token_backward",
        exchange=exchange,
        busy=55.0,
        polls=3,
    )


def state_backward_kernel(
    poll, valid, cot, gains, wq, wk, wv, wu, states, updates,
    sq, k, v, read, log_total, near_k, near_v, dsk, dsv, read_last, normed_t, snormed_t,
    dk, dv, grad_state, gain_grad, bias_grad, wk_grad, wv_grad, sqw_grad, wu_grad,
    later, dz, total, grad_read, sum_k, sum_v, dsq, kept_dz, kept,
):
    step, pair = pl.program_id(0), pl.program_id(1)
    block = pl.num_programs(0) - 1 - step
    gate = 1.0 / (1.0 + jnp.exp(-row_of(gains, 3)))

    @pl.when((step == 0) & (pair == 0))
    def _():
        later[...] = cot[...].astype(F32)
        gain_grad[...] = jnp.zeros_like(gain_grad)
        bias_grad[...] = jnp.zeros_like(bias_grad)

    @pl.when(pair == 0)
    def _():
        grad = later[...]
        rounded = (grad * (1.0 - gate)).astype(BF16)
        dz[...] = rounded

        @pl.when(step == 0)
        def _():
            kept_dz[...] = rounded

        bias_grad[...] += (
            jnp.sum(grad * (states[...] - updates[...]), axis=0, keepdims=True) * gate * (1.0 - gate)
        )
        total[...] = jnp.zeros_like(total)

    poll()
    grad_read[...] = matmul_nt(dz[...], wu[...]).astype(BF16)
    seen = block * BLOCK + position((BLOCK, BLOCK), 0) < valid[0]
    sum_k[...] = near_k[...]
    sum_v[...] = near_v[...]
    for head in range(2):
        lanes = pl.ds(head * HEAD, HEAD)

        def adder(ref):
            def add(term):
                ref[:, lanes] += term

            return add

        out_grad = grad_read[:, lanes]
        dsq[:, lanes] = attend_backward(
            sq[:, lanes],
            log_total[0, 0, pl.ds(head, 1), :],
            out_grad,
            centre_of(out_grad, read[:, lanes]),
            [(k[:, lanes], v[:, lanes], seen, adder(sum_k), adder(sum_v))],
        ).astype(BF16)
    poll()
    dk[...] = sum_k[...].astype(BF16)
    dv[...] = sum_v[...].astype(BF16)
    total[...] += (
        matmul_nt(dsq[...], wq[...]) + matmul_nt(dsk[...], wk[...]) + matmul_nt(dsv[...], wv[...])
    )

    @pl.when(step == 0)
    def _():
        for i, ref in enumerate((dk, dv, dsq)):
            kept[i, pair] = ref[...]

    @pl.when(step == 1)
    def _():
        for i, (left, ref, out) in enumerate(
            ((normed_t, dk, wk_grad), (normed_t, dv, wv_grad), (snormed_t, dsq, sqw_grad))
        ):
            half = left.shape[1] // 2
            out[...] = (
                matmul(left[:, :half], ref[...]) + matmul(left[:, half:], kept[i, pair])
            ).astype(BF16)
        wu_grad[...] = (
            matmul(read[...].T, dz[...]) + matmul(read_last[...].T, kept_dz[...])
        ).astype(BF16)

    @pl.when(pair == pl.num_programs(1) - 1)
    def _():
        grad, gain_rows = rms_backward(states[...], row_of(gains, 1), total[...])
        grad = later[...] * gate + grad
        later[...] = grad
        grad_state[...] = grad
        gain_grad[...] += jnp.sum(gain_rows, axis=0, keepdims=True)


def state_backward(
    valid, cot, gains, weights, update_weight, states, updates,
    sq, k, v, read, log_total, near_k, near_v, dsk, dsv, normed_t, snormed_t, exchange,
):
    rows, width = cot.shape
    blocks, pairs = k.shape[0] // BLOCK, width // PAIR
    columns = pl.BlockSpec((width, PAIR), lambda s, p: (0, p))
    tile = pl.BlockSpec((rows, PAIR), lambda s, p: (blocks - 1 - s, p))
    token = pl.BlockSpec((BLOCK, PAIR), lambda s, p: (blocks - 1 - s, p))
    band = pl.BlockSpec((rows, width), lambda s, p: (blocks - 1 - s, 0))
    small = whole((1, width))
    return run_kernel(
        state_backward_kernel,
        (
            valid, cot, gains, *weights, update_weight, states, updates,
            sq, k, v, read, log_total, near_k, near_v, dsk, dsv, read, normed_t, snormed_t,
        ),
        grid=(blocks, pairs),
        in_specs=[
            pl.BlockSpec(memory_space=pltpu.SMEM), whole((rows, width)), whole(gains.shape),
            columns, columns, columns, pl.BlockSpec((PAIR, width), lambda s, p: (p, 0)),
            band, band, tile, token, token, tile,
            pl.BlockSpec((1, 1, 2, rows), lambda s, p: (blocks - 1 - s, p, 0, 0)),
            token, token, tile, tile,
            pl.BlockSpec((rows, PAIR), lambda s, p: (blocks - 1, p)),
            pl.BlockSpec(normed_t.shape, lambda s, p: (0, 0), pipeline_mode=pl.Buffered(1)),
            pl.BlockSpec(snormed_t.shape, lambda s, p: (0, 0), pipeline_mode=pl.Buffered(1)),
        ],
        out_specs=[token, token, whole((rows, width)), small, small]
        + [pl.BlockSpec((width, PAIR), lambda s, p: (0, p * s))] * 3
        + [pl.BlockSpec((PAIR, width), lambda s, p: (p * s, 0))],
        out_shape=[
            jax.ShapeDtypeStruct(k.shape, BF16),
            jax.ShapeDtypeStruct(k.shape, BF16),
            jax.ShapeDtypeStruct((rows, width), F32),
            jax.ShapeDtypeStruct((1, width), F32),
            jax.ShapeDtypeStruct((1, width), F32),
        ]
        + [jax.ShapeDtypeStruct((width, width), BF16)] * 4,
        scratch_shapes=[
            pltpu.VMEM((rows, width), F32), pltpu.VMEM((rows, width), BF16),
            pltpu.VMEM((rows, width), F32), pltpu.VMEM((rows, PAIR), BF16),
            pltpu.VMEM((BLOCK, PAIR), F32), pltpu.VMEM((BLOCK, PAIR), F32),
            pltpu.VMEM((rows, PAIR), BF16), pltpu.VMEM((rows, width), BF16),
            pltpu.VMEM((3, pairs, BLOCK, PAIR), BF16),
        ],
        name="state_backward",
        exchange=exchange,
        busy=51.0,
        polls=2,
    )


def token_grad_kernel(
    plan, poll, x, gains, grad_resid, dq, dk, dv, wq, wk, wv, *refs
):
    *others, grad_x, gain_grad = refs
    plan.rows = [gain_grad] + others
    poll()

    @pl.when(pl.program_id(0) == 0)
    def _():
        gain_grad[...] = jnp.zeros_like(gain_grad)

    grad_normed = matmul_nt(dq[...], wq[...]) + matmul_nt(dk[...], wk[...])
    poll()
    grad_normed = grad_normed + matmul_nt(dv[...], wv[...])
    grad, gain_rows = rms_backward(x[...].astype(F32), row_of(gains, 0), grad_normed)
    grad_x[...] = grad_resid[...] + grad
    gain_grad[...] += jnp.sum(gain_rows, axis=0, keepdims=True)


def token_grad(x, gains, grad_resid, grads, weights, other_rows, plan, exchange):
    rows, width = x.shape
    band = pl.BlockSpec((TILE, width), lambda i: (i, 0))
    weight = pl.BlockSpec((width, width), lambda i: (0, 0), pipeline_mode=pl.Buffered(1))
    return run_kernel(
        functools.partial(token_grad_kernel, plan),
        (x, gains, grad_resid, *grads, *weights, *other_rows),
        grid=(rows // TILE,),
        in_specs=[band, whole(gains.shape), band, band, band, band, weight, weight, weight]
        + [whole((1, width))] * len(other_rows),
        out_specs=[band, whole((1, width))],
        out_shape=[
            jax.ShapeDtypeStruct((rows, width), F32), jax.ShapeDtypeStruct((1, width), F32)
        ],
        name="token_grad",
        exchange=exchange,
        busy=13.8,
        polls=2,
    )


def cut(width, pieces):
    return [(i * width // pieces, width // pieces) for i in range(pieces)]


def plan_gather(sizes, small, square, forward):
    width, half = square[0].shape[1], forward[0].shape[1]
    units = [(0, "zx", False, (0, small.shape[1]), 0, 1)]
    for group, (starts, routes, stride) in zip(((1, 2, 3), (4, 5, 6), (7,), (8,)), GATHER_SQUARE):
        pieces = cut(width, len(starts))
        can_share = pieces[0][1] // sizes["m"] % 128 == 0
        for n, (columns, start) in enumerate(zip(pieces, starts)):
            for j, i in enumerate(group):
                order = routes[(n * len(group) + j) % len(routes)]
                shared = can_share and "m" in order
                units.append((i, order if shared else "zx", shared, columns, start, stride))
    for i, (starts, stride) in enumerate(GATHER_FORWARD):
        for n, columns in enumerate(cut(half, min(len(starts), half // 128))):
            order = ("zxm", "zmx")[n % 2]
            units.append((9 + i, order, False, columns, starts[n], stride))
    arrays = [small] + square + forward
    return Gather(sizes, arrays, [(0, array.shape[1]) for array in arrays], units)


def forward_units(arrays, start, table):
    units = []
    for i, (array, pieces) in enumerate(zip(arrays, table)):
        columns = cut(array.shape[-1], min(len(pieces), array.shape[-1] // 128))
        units += [
            (i, order, False, there, start + offset, stride)
            for there, (order, offset, stride) in zip(columns, pieces)
        ]
    return units


def square_units(sizes, arrays, start, table):
    units = []
    for columns, pieces in zip(cut(arrays[0].shape[-1], len(table)), table):
        can_share = columns[1] // sizes["m"] % 128 == 0
        for i, (order, offset, stride) in enumerate(pieces):
            shared = can_share and "m" in order
            units.append(
                (i, order if shared else "xz", shared, columns, start + offset, stride)
            )
    return units


def finish_kernel(kept, counts, *refs):
    refs = list(refs)
    sources = [refs.pop(0) for _ in range(kept)]
    parts = [[refs.pop(0) for _ in range(n)] for n in counts]
    targets = [refs.pop(0) for _ in range(kept)]
    stages, sems = refs[-1 - kept : -1], refs[-1]
    loads, stores = [], []
    for i, (source, stage, target) in enumerate(zip(sources, stages, targets)):
        loads.append(pltpu.make_async_copy(source, stage, sems.at[i]))
        stores.append(pltpu.make_async_copy(stage, target, sems.at[kept + i]))
    for load in loads:
        load.start()
    for load, store in zip(loads, stores):
        load.wait()
        store.start()
    for group, out in zip(parts, refs):
        first = 0
        for part in group:
            out[:, pl.ds(first, part.shape[1])] = part[...]
            first += part.shape[1]
    for store in stores:
        store.wait()


def finish(arrays, groups):
    anywhere, inside = pl.BlockSpec(memory_space=pl.ANY), pl.BlockSpec(memory_space=pltpu.VMEM)
    shapes = [
        jax.ShapeDtypeStruct((g[0].shape[0], sum(p.shape[1] for p in g)), F32) for g in groups
    ]
    parts = [part for g in groups for part in g]
    outs = pl.pallas_call(
        functools.partial(finish_kernel, len(arrays), [len(g) for g in groups]),
        in_specs=[anywhere] * len(arrays) + [inside] * len(parts),
        out_specs=[anywhere] * len(arrays) + [inside] * len(groups),
        out_shape=[jax.ShapeDtypeStruct(a.shape, a.dtype) for a in arrays] + shapes,
        scratch_shapes=[pltpu.VMEM(a.shape, a.dtype) for a in arrays]
        + [pltpu.SemaphoreType.DMA((2 * len(arrays),))],
        compiler_params=pltpu.CompilerParams(vmem_limit_bytes=VMEM_LIMIT),
        name="finish",
    )(*arrays, *parts)
    return outs[: len(arrays)], outs[len(arrays) :]


def shards(
    mlp_size,
    tokens,
    initial_state,
    valid,
    token_query_weight,
    token_key_weight,
    token_value_weight,
    token_output_weight,
    state_query_weight,
    state_key_weight,
    state_value_weight,
    state_update_weight,
    up_projection_weight,
    down_projection_weight,
    token_norm_gain,
    state_norm_gain,
    feedforward_norm_gain,
    state_gate_bias,
    output_cotangent,
    final_state_cotangent,
):
    rows = token_query_weight.shape[0]
    width = tokens.shape[2]
    seg_size = width // rows
    sizes = {"z": seg_size // 4, "x": 2, "c": 2, "m": mlp_size}
    half = up_projection_weight.shape[1] // 2
    small = jnp.concatenate(
        [token_norm_gain, state_norm_gain, feedforward_norm_gain, state_gate_bias]
    ).reshape(-1, 128)
    small = jnp.pad(small, ((0, 16 - small.shape[0]), (0, 0)))
    square = [
        token_query_weight,
        token_key_weight,
        token_value_weight,
        state_query_weight,
        state_key_weight,
        state_value_weight,
        state_update_weight,
        token_output_weight,
    ]
    forward = [
        weight[:, first : first + half]
        for first in (0, half)
        for weight in (up_projection_weight, down_projection_weight)
    ]
    plan = plan_gather(sizes, small, square, forward)
    x, s0, cot = tokens[0], initial_state[0], output_cotangent[0]

    def full(*names):
        return [plan.targets[n].reshape(width, width) for n in names]

    def forward_full(*names):
        return [plan.targets[n].reshape(mlp_size, width, half) for n in names]

    exchange_alone(plan.until(plan.ready((0, 1, 2, 3)), 1), "gather_first")
    gains = plan.targets[0].reshape(seg_size, -1)[:, : 4 * rows].reshape(seg_size, 4, rows)
    gains = gains.transpose(1, 0, 2).reshape(4, width).astype(F32)
    token_weights = full(1, 2, 3)
    normed_t, masked, masked_t, q, k, v = project(
        valid, x, gains, cot, token_weights, plan.until(plan.ready((4, 5, 6, 7)), 2)
    )
    state_weights, (wu,) = full(4, 5, 6), full(7)
    ready = plan.ready((9, 10))
    middle = max(plan.ready((8,)), GATHER_MIDDLE)
    snormed_t, sq, sk, sv, read, read_log, updates, states, last = state_forward(
        valid, s0, gains, state_weights, wu, k, v, plan.until(middle, 3)
    )
    (wo,) = full(8)
    mixed, token_log, resid, *ynorms = token_forward(
        valid, x, gains, q, k, v, sk, sv, wo, plan.until(ready, 4)
    )
    total, grad_total, *first_grads = feed_forward(
        True, False, (*ynorms, masked, masked_t), resid, resid, *forward_full(9, 10),
        plan.until(plan.ready((11, 12)), 5),
    )

    def parted(grads):
        shape = (seg_size // 4, 2, 2, rows)
        return [
            g.reshape((mlp_size,) + shape + (half,)) if g.ndim == 3 else g.reshape(shape + (width,))
            for g in grads
        ]

    sums = Scatter(sizes)
    rounds = iter(SCATTER_ROUNDS)

    def next_rounds(collective_id):
        return sums.until(sums.round + next(rounds), collective_id)

    units_first = sums.add(parted(first_grads), forward_units(first_grads, 0, SCATTER_FIRST))
    out, grad_total, *last_grads = feed_forward(
        False, True, (*ynorms, masked, masked_t), total, grad_total, *forward_full(11, 12),
        next_rounds(6),
    )
    units_last = sums.add(parted(last_grads), forward_units(last_grads, sums.round, SCATTER_LAST))
    grad_resid, mlp_gain_grad, dq, near_k, near_v, dsk, dsv, *early_grads = token_backward(
        valid, resid, gains, masked, grad_total, normed_t, snormed_t,
        q, k, v, sk, sv, wo, mixed, token_log, next_rounds(7),
    )
    units_early = sums.add(
        parted(early_grads), square_units(sizes, early_grads, sums.round, SCATTER_EARLY)
    )
    dk, dv, grad_state, state_gain_grad, bias_grad, *late_grads = state_backward(
        valid, final_state_cotangent[0], gains, state_weights, wu,
        states, updates, sq, k, v, read, read_log, near_k, near_v, dsk, dsv, normed_t, snormed_t,
        next_rounds(8),
    )
    units_late = sums.add(
        parted(late_grads), square_units(sizes, late_grads, sums.round, SCATTER_LATE)
    )
    small_unit = sums.add_small(mlp_gain_grad)
    grad_tokens, _ = token_grad(
        x, gains, grad_resid, [dq, dk, dv], token_weights,
        [state_gain_grad, mlp_gain_grad, bias_grad], sums, sums.until(sums.all(), 9),
    )
    small_sum = small_unit.result[:4].reshape(4, seg_size, rows)
    small_sum = lax.dynamic_index_in_dim(small_sum, lax.axis_index("seg"), 1, keepdims=False)

    def group(units, i, count):
        return [unit.result for unit in units[i::count]]

    def forward_group(i):
        return [
            unit.result
            for units in (units_first, units_last)
            for unit in units[i * len(units) // 2 : (i + 1) * len(units) // 2]
        ]

    own_results, weight_sums = finish(
        [last, out, grad_state, grad_tokens],
        [
            group(units_early, 1, 4),
            group(units_late, 0, 4),
            group(units_late, 1, 4),
            group(units_early, 0, 4),
            group(units_late, 2, 4),
            group(units_early, 2, 4),
            group(units_early, 3, 4),
            group(units_late, 3, 4),
            forward_group(0),
            forward_group(1),
        ],
    )
    return (
        *[own_results[i][None] for i in (1, 0, 3, 2)],
        *weight_sums,
        *[small_sum[i] for i in range(4)],
    )


def solution(mesh):
    own = P(("seg", "mlp"), None, None)
    square, forward, small = P("seg", None), P("seg", "mlp"), P("seg")
    return jax.shard_map(
        functools.partial(shards, mesh.shape["mlp"]),
        mesh=mesh,
        in_specs=(own, own, P(("seg", "mlp")))
        + (square,) * 8
        + (forward,) * 2
        + (small,) * 4
        + (own, own),
        out_specs=(own,) * 4 + (square,) * 8 + (forward,) * 2 + (small,) * 4,
        check_vma=False,
    )
```

```python
import functools
import jax
import jax.numpy as jnp
from jax import lax
from jax.experimental import pallas as pl
from jax.experimental.pallas import tpu as pltpu
from jax.sharding import PartitionSpec as P

BF16 = jnp.bfloat16
F32 = jnp.float32
VMEM_LIMIT = 60 << 20
GATHER_SQUARE = (
    ((0, 1), ("zx", "zxm", "zxm"), 1),
    ((2, 3), ("zx", "zxm", "zxm"), 1),
    ((4, 4), ("zx", "zxm"), 1),
    ((5, 5), ("zx", "zxm"), 1),
)
GATHER_FORWARD = (((6, 6), 1), ((7, 7), 1), ((9, 9), 1), ((10, 10), 1))
GATHER_MIDDLE = 9
SCATTER_FIRST = ((("mxz", 0, 1), ("xmz", 0, 1)), (("mxz", 1, 1), ("xmz", 1, 1)))
SCATTER_LAST = SCATTER_FIRST
SCATTER_EARLY = (
    (("xz", 0, 1), ("mxz", 0, 1), ("mxz", 0, 1), ("xz", 0, 1)),
    (("mxz", 1, 1), ("mxz", 1, 1), ("xz", 1, 1), ("mxz", 1, 1)),
)
SCATTER_LATE = (
    (("xz", 0, 1), ("mxz", 0, 1), ("mxz", 0, 1), ("zx", 0, 1)),
    (("mxz", 1, 1), ("mxz", 1, 1), ("xz", 1, 1), ("mxz", 1, 1)),
)
SCATTER_ROUNDS = (3, 3, 2)
LINK_RATE = 85e3
CORE_RATE = 560e3
START_COST = 2.5
STEP_COST = 0.3
LATENCY = 2.0


class Place:
    def __init__(self, sizes):
        seg = lax.axis_index("seg")
        self.sizes = sizes
        self.at = {
            "z": lax.div(seg, 4),
            "x": lax.rem(lax.div(seg, 2), 2),
            "c": lax.rem(seg, 2),
            "m": lax.axis_index("mlp"),
        }

    def device(self, moved):
        at = {**self.at, **moved}
        return (at["z"] * 4 + at["x"] * 2 + at["c"], at["m"])

    def ahead(self, axis, step):
        return lax.rem(self.at[axis] + step, self.sizes[axis])

    def behind(self, axis, step):
        return lax.rem(self.at[axis] + self.sizes[axis] - step, self.sizes[axis])

    def greet(self):
        barrier = pltpu.get_barrier_semaphore()
        count = 0
        for axis in "zxcm":
            for step in range(1, self.sizes[axis]):
                pl.semaphore_signal(
                    barrier,
                    inc=1,
                    device_id=self.device({axis: self.ahead(axis, step)}),
                    device_id_type=pl.DeviceIdType.MESH,
                )
                count += 1
        pl.semaphore_wait(barrier, count)


class Flow:
    def __init__(self, place, send, recv, taken):
        self.place, self.send, self.recv, self.taken = place, send, recv, taken
        self.steps, self.arriving, self.sent = [], [], []

    def move(self, actions, make):
        pair = self.taken[0]
        self.taken[0] += 1

        def copy(source, target, moved):
            return pltpu.make_async_remote_copy(
                src_ref=source,
                dst_ref=target,
                send_sem=self.send.at[pair],
                recv_sem=self.recv.at[pair],
                device_id=self.place.device(moved),
                device_id_type=pl.DeviceIdType.MESH,
            )

        def outgoing():
            source, target, moved, _ = make()
            return copy(source, target, moved)

        def incoming():
            _, _, moved, landing = make()
            return copy(landing, landing, moved)

        actions.append(lambda: outgoing().start())
        self.sent.append(lambda: outgoing().wait_send())
        self.arriving.append(lambda: incoming().wait_recv())

    def arrived(self):
        waits, self.arriving = self.arriving, []
        return waits


def gather_steps(flow, source, target, order, split, columns, skipped, local_sem, begin, end):
    place = flow.place
    at, sizes = place.at, place.sizes
    lead = ("m" if len(target.shape) == 6 else "") + "zxc"
    first_column, width = columns
    share = width // sizes["m"] if split else width

    def block(done, moved, skip=0):
        first = first_column + skip
        if not split or "m" in done:
            lanes = pl.ds(first, width)
        else:
            lanes = pl.ds(pl.multiple_of(first + moved.get("m", at["m"]) * share, 128), share)
        return (pl.ds(0, source.shape[0]), lanes)

    def view(done, **moved):
        index = tuple(
            moved[a] if a in moved else pl.ds(0, sizes[a]) if a in done else at[a] for a in lead
        )
        return target.at[index + block(done, moved)]

    def own_source():
        return source.at[block("", {}, skipped)]

    def own():
        return pltpu.make_async_copy(own_source(), view(""), local_sem)

    waits = []
    for i, axis in enumerate(order + "c"):
        done = order[:i]
        if not begin <= i < end:
            continue
        actions = flow.arrived() + waits
        waits = []
        if i == 0:
            actions.append(lambda: own().start())
            waits.append(lambda: own().wait())
        for step in range(1, sizes[axis]):

            def make(axis=axis, step=step, done=done):
                return (
                    view(done) if done else own_source(),
                    view(done),
                    {axis: place.ahead(axis, step)},
                    view(done, **{axis: place.behind(axis, step)}),
                )

            flow.move(actions, make)
        flow.steps.append(actions)
    flow.last = flow.arrived() + waits + flow.sent


def add_into(total, term):
    lead = total.shape[:-2]

    def body(i, carry):
        index, rest = [], i
        for size in reversed(lead):
            index.append(lax.rem(rest, size))
            rest = lax.div(rest, size)
        there = tuple(reversed(index)) + (Ellipsis,)
        total[there] = total[there] + term[there]
        return carry

    lax.fori_loop(0, functools.reduce(lambda a, b: a * b, lead, 1), body, 0)


class ScatterUnit:
    def __init__(self, sizes, grad, order, split, columns, start, stride):
        self.sizes, self.grad, self.order, self.split = sizes, grad, order, split
        self.columns, self.start, self.stride = columns, start, stride
        self.whole_m = grad.ndim == 6
        self.lead = ("m" if self.whole_m else "") + "zx"
        self.rows, self.width = grad.shape[-2], columns[1]
        self.share = self.width // sizes["m"] if split else self.width
        self.count = 1 + len(order) + (not self.whole_m)
        self.spec = pl.BlockSpec(memory_space=pl.ANY)
        self.state = self.result = None

    def left(self, done):
        width = self.share if "m" in done else self.width
        return tuple(self.sizes[a] for a in self.lead if a not in done) + (self.rows, width)

    def shapes(self, begin, end):
        shapes = [self.left(self.order[: max(begin - 1, 0)])]
        for i in range(begin, end):
            if i == 0:
                shapes.append(self.left(""))
            elif i <= len(self.order):
                axis = self.order[i - 1]
                shapes.append((self.sizes[axis] - 1,) + self.left(self.order[:i]))
            elif self.split:
                shapes.append((self.rows, self.width))
            else:
                shapes.append((self.sizes["m"], self.rows, self.width))
        return shapes

    def steps(self, flow, grad, state, saved, result, buffers, local_sem, begin, end):
        place, at, sizes, order = flow.place, flow.place.at, self.sizes, self.order
        own, landings = buffers[0], dict(zip(range(begin, end), buffers[1:]))
        gone = order[: max(begin - 1, 0)]
        lead = [a for a in self.lead if a not in gone]
        narrow = self.split and "m" in gone

        def lanes_of(place_m):
            return pl.ds(pl.multiple_of(place_m * self.share, 128), self.share)

        def grad_half(core):
            index = tuple(pl.ds(0, sizes[a]) for a in self.lead)
            return grad.at[index + (core, pl.ds(0, self.rows), pl.ds(*self.columns))]

        def view(done, **moved):
            index = tuple(
                moved[a] if a in moved else at[a] if a in done else pl.ds(0, sizes[a]) for a in lead
            )
            lanes = pl.ds(0, self.share if narrow else self.width)
            if self.split and not narrow and ("m" in done or "m" in moved):
                lanes = lanes_of(moved.get("m", at["m"]))
            return own.at[index + (pl.ds(0, self.rows), lanes)]

        def load():
            return pltpu.make_async_copy(grad_half(at["c"]) if begin == 0 else state, own, local_sem)

        def added(axis, done, landing):
            return [
                lambda step=step: add_into(view(done), landing.at[step - 1])
                for step in range(1, sizes[axis])
            ]

        ahead = [lambda: load().start()]
        actions = []
        if begin > 0:
            actions.append(lambda: load().wait())
        for i in range(begin, end):
            landing = landings[i]
            if i == 0:
                flow.move(
                    actions,
                    lambda landing=landing: (
                        grad_half(1 - at["c"]), landing, {"c": 1 - at["c"]}, landing
                    ),
                )
                flow.steps.append(actions)
                actions = [lambda: load().wait()] + flow.arrived()
                actions.append(lambda landing=landing: add_into(own, landing))
            elif i <= len(order):
                axis, done = order[i - 1], order[: i - 1]
                for step in range(1, sizes[axis]):

                    def make(axis=axis, step=step, done=done, landing=landing):
                        there = place.ahead(axis, step)
                        slot = landing.at[step - 1]
                        return (view(done, **{axis: there}), slot, {axis: there}, slot)

                    flow.move(actions, make)
                flow.steps.append(actions)
                actions = flow.arrived() + added(axis, order[:i], landing)
            else:

                def part(place_m, landing=landing):
                    if self.split:
                        return landing.at[pl.ds(0, self.rows), lanes_of(place_m)]
                    return landing.at[place_m]

                def keep():
                    part(at["m"])[...] = view(order)[...]

                actions.append(keep)
                for step in range(1, sizes["m"]):
                    flow.move(
                        actions,
                        lambda step=step: (
                            part(at["m"]),
                            part(at["m"]),
                            {"m": place.ahead("m", step)},
                            part(place.behind("m", step)),
                        ),
                    )
                flow.steps.append(actions)
                actions = flow.arrived()
        if end == self.count:

            def store():
                if self.whole_m:
                    total = view(order)[...].astype(F32)
                elif self.split:
                    total = landing[...].astype(F32)
                else:
                    total = landing[0].astype(F32)
                    for i in range(1, sizes["m"]):
                        total = total + landing[i].astype(F32)
                result[...] = total

            return ahead, actions + [store], flow.sent

        def save():
            return pltpu.make_async_copy(view(order[: end - 1]), saved, local_sem)

        return ahead, actions + [lambda: save().start()], flow.sent + [lambda: save().wait()]


def step_time(sizes, axis, size):
    if axis == "c":
        return size / CORE_RATE
    return 2 * size * ((sizes["z"] // 2) ** 2 if axis == "z" else sizes[axis] - 1) / LINK_RATE


def round_times(sizes, rounds):
    now, free, ended, times = START_COST, {axis: 0.0 for axis in "zxcm"}, {}, []
    for there in rounds:
        for unit, step, axis, size in there:
            now = max(now, ended.get((unit, step - 1), 0.0)) + STEP_COST
            free[axis] = max(free[axis], now) + step_time(sizes, axis, size)
            ended[unit, step] = free[axis] + LATENCY
        times.append(now)
    return times, max(ended.values())


class Gather:
    def __init__(self, sizes, arrays, spans, units):
        self.sizes, self.arrays, self.spans, self.round = sizes, arrays, spans, 0
        self.units = [unit[:-2] for unit in units]
        self.starts = [unit[-2:] for unit in units]
        self.targets = [None] * len(arrays)

    def ready(self, names):
        return max(
            self.stop(start, unit) for start, unit in zip(self.starts, self.units) if unit[0] in names
        )

    def stop(self, start, unit):
        return start[0] + len(unit[1]) * start[1] + 1

    def until(self, end, collective_id):
        begin, self.round = self.round, max(end, self.round)
        return GatherPart(self, begin, end, collective_id) if begin < end else None


class GatherPart:
    def __init__(self, plan, begin, end, collective_id):
        self.plan, self.begin, self.end, self.collective_id = plan, begin, end, collective_id
        self.units = [
            (start, unit)
            for start, unit in zip(plan.starts, plan.units)
            if start[0] < end and plan.stop(start, unit) > begin
        ]
        self.names = sorted({unit[0] for _, unit in self.units})
        split = {unit[0]: unit[2] for _, unit in self.units}
        order = {unit[0]: unit[1] for _, unit in self.units}
        sizes = plan.sizes
        anywhere = pl.BlockSpec(memory_space=pl.ANY)
        old = [n for n in self.names if plan.targets[n] is not None]
        self.arrays = [plan.arrays[n] for n in self.names] + [plan.targets[n] for n in old]
        self.specs = [anywhere] * len(self.arrays)
        self.out_shape = [
            jax.ShapeDtypeStruct(
                ((sizes["m"],) if "m" in order[n] and not split[n] else ())
                + (sizes["z"], 2, 2)
                + (plan.arrays[n].shape[0], plan.spans[n][1]),
                plan.arrays[n].dtype,
            )
            for n in self.names
        ]
        self.out_specs = [anywhere] * len(self.names)
        self.aliases = {len(self.names) + i: self.names.index(n) for i, n in enumerate(old)}
        pairs = len(self.units) * (sum(sizes.values()) - 4)
        self.scratch = [
            pltpu.SemaphoreType.DMA((pairs,)),
            pltpu.SemaphoreType.DMA((pairs,)),
            pltpu.SemaphoreType.DMA((len(self.units),)),
        ]

    def times(self, busy):
        sizes = self.plan.sizes
        loads = [{axis: 0.0 for axis in "zxcm"} for _ in range(self.end - self.begin)]
        for (start, stride), (n, order, split, columns) in self.units:
            size = self.plan.arrays[n].shape[0] * columns[1] * self.plan.arrays[n].dtype.itemsize
            if split:
                size //= sizes["m"]
            for i, axis in enumerate(order + "c"):
                if self.begin <= start + i * stride < self.end:
                    loads[start + i * stride - self.begin][axis] += step_time(sizes, axis, size)
                size *= sizes[axis]
        times = [0.0]
        for load in loads:
            times.append(times[-1] + max(load.values()) + LATENCY)
        return times[:-1], busy

    def rounds(self, ins, outs, scratch):
        place = Place(self.plan.sizes)
        send, recv, local = scratch
        taken = [0]
        rounds = [[] for _ in range(self.end - self.begin)]
        last = []
        for i, ((start, stride), (n, order, split, columns)) in enumerate(self.units):
            flow = Flow(place, send, recv, taken)
            begin, end = [max(-((start - to) // stride), 0) for to in (self.begin, self.end)]
            slot = self.names.index(n)
            gather_steps(
                flow, ins[slot], outs[slot], order, split, columns, self.plan.spans[n][0],
                local.at[i], begin, end,
            )
            for step, actions in enumerate(flow.steps):
                there = rounds[start + (begin + step) * stride - self.begin]
                there.insert(0 if begin + step == 0 else len(there), actions)
            last += flow.last
        rounds = [[action for actions in there for action in actions] for there in rounds]
        rounds[0].insert(0, place.greet)
        return rounds, last

    def received(self, outs):
        for n, out in zip(self.names, outs):
            self.plan.targets[n] = out


class SmallUnit:
    def __init__(self, plan, row, start):
        self.plan, self.grad, self.start, self.stride = plan, row, start, 1
        self.order, self.count = "xzm", 4
        self.rows, self.width = 8, row.shape[1]
        self.share = self.width
        self.spec = pl.BlockSpec(memory_space=pl.ANY)
        self.state = self.result = None

    def left(self, done):
        return (self.rows, self.width)

    def shapes(self, begin, end):
        sizes = self.plan.sizes
        return [self.left("")] + [(sizes[axis],) + self.left("") for axis in "c" + self.order]

    def steps(self, flow, row, state, saved, result, buffers, local_sem, begin, end):
        place, at = flow.place, flow.place.at
        own, landings = buffers[0], buffers[1:]
        actions = []

        def fill():
            own[...] = jnp.zeros_like(own)
            for i, row in enumerate(self.plan.rows):
                own[pl.ds(i, 1), :] = row[...]

        actions.append(fill)
        for axis, landing in zip("c" + self.order, landings):

            def keep(axis=axis, landing=landing):
                landing[at[axis]] = own[...]

            actions.append(keep)
            for step in range(1, place.sizes[axis]):

                def make(axis=axis, landing=landing, step=step):
                    slot = landing.at[at[axis]]
                    return (slot, slot, {axis: place.ahead(axis, step)}, landing.at[place.behind(axis, step)])

                flow.move(actions, make)
            flow.steps.append(actions)

            def add(axis=axis, landing=landing):
                total = landing[0]
                for i in range(1, place.sizes[axis]):
                    total = total + landing[i]
                own[...] = total

            actions = flow.arrived() + [add]

        def store():
            result[...] = own[...]

        return [], actions + [store], flow.sent


class Scatter:
    def __init__(self, sizes):
        self.sizes, self.units, self.round = sizes, [], 0

    def add(self, arrays, units):
        for i, order, split, columns, start, stride in units:
            assert start >= self.round
            self.units.append(
                ScatterUnit(self.sizes, arrays[i], order, split, columns, start, stride)
            )
        return self.units[len(self.units) - len(units) :]

    def add_small(self, row):
        self.units.append(SmallUnit(self, row, self.all() - 4))
        return self.units[-1]

    def all(self):
        return max(unit.start + (unit.count - 1) * unit.stride + 1 for unit in self.units)

    def until(self, end, collective_id):
        begin, self.round = self.round, max(end, self.round)
        part = ScatterPart(self, begin, end, collective_id)
        return part if part.units else None


class ScatterPart:
    aliases = {}

    def __init__(self, plan, begin, end, collective_id):
        self.sizes, self.begin, self.end, self.collective_id = plan.sizes, begin, end, collective_id
        self.units = []
        buffers, pairs = [], 0
        self.arrays, self.out_shape, self.out_specs = [], [], []
        for unit in plan.units:
            first, stop = [
                min(max(-((unit.start - to) // unit.stride), 0), unit.count) for to in (begin, end)
            ]
            if first >= stop:
                continue
            self.units.append((unit, first, stop))
            self.arrays.append(unit.state if first else unit.grad)
            if stop == unit.count:
                shape = (unit.rows, unit.width)
                self.out_shape.append(jax.ShapeDtypeStruct(shape, F32))
                self.out_specs.append(
                    pl.BlockSpec(shape, lambda *_: (0, 0), pipeline_mode=pl.Buffered(1))
                )
            else:
                shape = unit.left(unit.order[: stop - 1])
                self.out_shape.append(jax.ShapeDtypeStruct(shape, unit.grad.dtype))
                self.out_specs.append(pl.BlockSpec(memory_space=pl.ANY))
            buffers += [pltpu.VMEM(shape, unit.grad.dtype) for shape in unit.shapes(first, stop)]
            pairs += sum(self.sizes.values()) - 4 + self.sizes["m"] - 1
        self.specs = [unit.spec for unit, _, _ in self.units]
        self.scratch = buffers + [
            pltpu.SemaphoreType.DMA((pairs,)),
            pltpu.SemaphoreType.DMA((pairs,)),
            pltpu.SemaphoreType.DMA((len(self.units),)),
        ]

    def times(self, busy):
        rounds = [[] for _ in range(self.end - self.begin)]
        for n, (unit, first, stop) in enumerate(self.units):
            for i in range(first, stop):
                done = unit.order[:i]
                axis = ("c" + unit.order + "m")[i]
                shape = unit.left(done) if i <= len(unit.order) else (unit.rows, unit.share)
                size = functools.reduce(lambda a, b: a * b, shape, unit.grad.dtype.itemsize)
                rounds[unit.start + i * unit.stride - self.begin].append((n, i, axis, size))
        times, length = round_times(self.sizes, rounds)
        return times, busy if length > 2.0 * busy else length

    def rounds(self, ins, outs, scratch):
        place = Place(self.sizes)
        send, recv, local = scratch[-3:]
        buffers = list(scratch[:-3])
        taken = [0]
        rounds = [[] for _ in range(self.end - self.begin)]
        start_up, ends, waits = [], [], []
        for i, (unit, first, stop) in enumerate(self.units):
            flow = Flow(place, send, recv, taken)
            count = 1 + stop - first
            mine, buffers = buffers[:count], buffers[count:]
            done = stop == unit.count
            ahead, end, wait = unit.steps(
                flow, ins[i], ins[i], None if done else outs[i], outs[i] if done else None,
                mine, local.at[i], first, stop,
            )
            if first:
                start_up += ahead
            else:
                flow.steps[0][:0] = ahead
            for step, actions in enumerate(flow.steps):
                rounds[unit.start + (first + step) * unit.stride - self.begin].append(actions)
            after = unit.start + stop * unit.stride - self.begin
            if done and after < len(rounds):
                rounds[after].append(end)
            else:
                ends += end
            waits += wait
        rounds = [[action for actions in there for action in actions] for there in rounds]
        rounds[0][:0] = start_up + [place.greet]
        return rounds, ends + waits

    def received(self, outs):
        for (unit, first, stop), out in zip(self.units, outs):
            if stop == unit.count:
                unit.result = out
            else:
                unit.state = out


def run_all(actions):
    for action in actions:
        action()


def run_kernel(
    body, args, *, grid, in_specs, out_specs, out_shape, name, scratch_shapes=(), exchange=None, polls=1,
    busy=0.0,
):
    if exchange is None:
        return pl.pallas_call(
            functools.partial(body, lambda: None),
            grid=grid,
            in_specs=in_specs,
            out_specs=out_specs,
            out_shape=out_shape,
            scratch_shapes=scratch_shapes,
            compiler_params=pltpu.CompilerParams(vmem_limit_bytes=VMEM_LIMIT),
            name=name,
        )(*args)
    counts = (len(args), len(exchange.arrays), len(out_shape), len(exchange.out_shape))
    total = functools.reduce(lambda a, b: a * b, grid, 1)
    times, pace = exchange.times(busy)

    def kernel(*refs):
        refs = list(refs)
        ins, sent, outs, received = [[refs.pop(0) for _ in range(n)] for n in counts]
        own = [refs.pop(0) for _ in range(len(scratch_shapes))]
        step = 0
        for i, size in enumerate(grid):
            step = step * size + pl.program_id(i)
        rounds, last = exchange.rounds(sent, received, refs)
        slots, after = {}, []
        for i, (actions, time) in enumerate(zip(rounds, times)):
            slot = int(total * polls * time / pace + 0.5) if busy and i else 0
            if slot >= total * polls or i and not busy:
                after += actions
            else:
                slots.setdefault((slot % polls, slot // polls), []).extend(actions)
        called = [0]

        def poll():
            for at_step in range(total):
                actions = slots.get((called[0], at_step))
                if actions:
                    pl.when(step == at_step)(functools.partial(run_all, actions))
            called[0] += 1

        body(poll, *ins, *outs, *own)
        assert called[0] == polls
        pl.when(step == total - 1)(functools.partial(run_all, after + last))

    outs = pl.pallas_call(
        kernel,
        grid=grid,
        in_specs=list(in_specs) + exchange.specs,
        out_specs=list(out_specs) + exchange.out_specs,
        out_shape=list(out_shape) + exchange.out_shape,
        scratch_shapes=list(scratch_shapes) + exchange.scratch,
        input_output_aliases={counts[0] + i: counts[2] + o for i, o in exchange.aliases.items()},
        compiler_params=pltpu.CompilerParams(
            vmem_limit_bytes=VMEM_LIMIT,
            collective_id=exchange.collective_id,
            has_side_effects=True,
        ),
        name=name,
    )(*args, *exchange.arrays)
    exchange.received(outs[counts[2] :])
    return outs[: counts[2]]


def exchange_alone(exchange, name):
    run_kernel(
        lambda poll: poll(), [], grid=(1,), in_specs=[], out_specs=[], out_shape=[], name=name,
        exchange=exchange,
    )


HEAD = 128
BLOCK = 512
EPS = 1e-06
NEGATIVE = -1e30
GELU_C = 0.7978845608
GELU_K = 0.044715
SCALE = HEAD**-0.5
LOG2E = 1.4426950408889634
PAIR = 2 * HEAD
TILE = 256


def matmul(left, right):
    return jnp.dot(left, right, preferred_element_type=F32)


def matmul_nt(left, right):
    return lax.dot_general(left, right, (((1,), (1,)), ((), ())), preferred_element_type=F32)


def inverse_rms(values):
    return lax.rsqrt(jnp.mean(values * values, axis=-1, keepdims=True) + EPS)


def rms_backward(values, gain, grad):
    inverse = inverse_rms(values)
    unit = values * inverse
    weighted = grad * gain
    inner = jnp.mean(weighted * unit, axis=-1, keepdims=True)
    return inverse * (weighted - unit * inner), grad * unit


def row_of(gains, i):
    return gains[pl.ds(i, 1), :]


def whole(shape):
    return pl.BlockSpec(shape, lambda *_: (0,) * len(shape))


def project_kernel(
    poll, valid, x_ref, gains, cot, wq, wk, wv, normed_t, masked, masked_t, q, k, v, normed
):
    @pl.when(pl.program_id(0) == 0)
    def _():
        x = x_ref[...].astype(F32)
        rows = (x * inverse_rms(x) * row_of(gains, 0)).astype(BF16)
        normed[...] = rows
        normed_t[...] = rows.T
        keep = position(cot.shape, 0) < valid[0]
        grad = jnp.where(keep, cot[...], jnp.zeros_like(cot))
        masked[...] = grad
        masked_t[...] = grad.T

    rows = normed[...]
    for weight, out in ((wq, q), (wk, k), (wv, v)):
        poll()
        out[...] = matmul(rows, weight[...]).astype(BF16)


def project(valid, x, gains, cot, weights, exchange):
    rows, width = x.shape
    tile = pl.BlockSpec((width, TILE), lambda j: (0, j))
    out = pl.BlockSpec((rows, TILE), lambda j: (0, j))
    full = whole((rows, width))
    turned = whole((width, rows))
    return run_kernel(
        project_kernel,
        (valid, x, gains, cot, *weights),
        grid=(width // TILE,),
        in_specs=[pl.BlockSpec(memory_space=pltpu.SMEM), full, whole(gains.shape), full]
        + [tile] * 3,
        out_specs=[turned, full, turned, out, out, out],
        out_shape=[
            jax.ShapeDtypeStruct((width, rows), BF16),
            jax.ShapeDtypeStruct((rows, width), BF16),
            jax.ShapeDtypeStruct((width, rows), BF16),
        ]
        + [jax.ShapeDtypeStruct((rows, width), BF16)] * 3,
        scratch_shapes=[pltpu.VMEM((rows, width), BF16)],
        name="project_tokens",
        exchange=exchange,
        busy=14.0,
        polls=3,
    )


def attend(query, pieces):
    scores = []
    for keys, _, mask in pieces:
        score = matmul_nt(keys, query) * (SCALE * LOG2E)
        scores.append(score if mask is None else jnp.where(mask, score, NEGATIVE))
    top = functools.reduce(jnp.maximum, [jnp.max(s, axis=0, keepdims=True) for s in scores])
    total, mixed = 0.0, 0.0
    for score, (_, values, _) in zip(scores, pieces):
        weights = jnp.exp2(score - top)
        total = total + jnp.sum(weights, axis=0, keepdims=True)
        mixed = mixed + matmul(values.T, weights.astype(BF16))
    return (mixed / total).T.astype(BF16), top + jnp.log2(total)


def attend_backward(query, log_total, grad, centre, pieces):
    grad_query = 0.0
    for keys, values, mask, add_keys, add_values in pieces:
        score = matmul_nt(keys, query) * (SCALE * LOG2E)
        if mask is not None:
            score = jnp.where(mask, score, NEGATIVE)
        probs = jnp.exp2(score - log_total)
        add_values(matmul(probs.astype(BF16), grad))
        grad_probs = matmul_nt(values, grad)
        grad_scores = (probs * (grad_probs - centre)).astype(BF16)
        add_keys(matmul(grad_scores, query) * SCALE)
        grad_query = grad_query + matmul(keys.T, grad_scores)
    return (grad_query * SCALE).T


def centre_of(grad, mixed):
    return jnp.sum((grad.astype(F32) * mixed.astype(F32)).T, axis=0, keepdims=True)


def position(shape, axis):
    return lax.broadcasted_iota(jnp.int32, shape, axis)


def token_pieces(block, half, valid):
    key = position((TILE, TILE), 0)
    query = position((TILE, TILE), 1)
    causal, recent = key <= query, key > query
    pieces = []
    if block:
        start = (block - 1) * BLOCK
        pieces.append(("near", start + half * TILE, TILE, recent))
        if half == 0:
            pieces.append(("near", start + TILE, TILE, None))
    start = block * BLOCK
    for piece in range(half + 1):
        first = start + piece * TILE
        seen = first + key < valid
        mask = causal if piece == half else None
        if block:
            mask = seen if mask is None else mask & seen
        pieces.append(("near", first, TILE, mask))
    pieces.append(("state", block * BLOCK, BLOCK, None))
    return pieces


def state_forward_kernel(
    poll, valid, s0, gains, wq, wk, wv, wu, k, v,
    normed_t, sq, sk, sv, read, log_out, update_out, states, last,
    state, normed, total,
):
    block, pair = pl.program_id(0), pl.program_id(1)

    @pl.when((block == 0) & (pair == 0))
    def _():
        state[...] = s0[...].astype(F32)

    @pl.when(pair == 0)
    def _():
        now = state[...]
        rows = (now * inverse_rms(now) * row_of(gains, 1)).astype(BF16)
        normed[...] = rows
        normed_t[...] = rows.T
        states[...] = now
        total[...] = jnp.zeros_like(total)

    poll()
    rows = normed[...]
    for weight, out in ((wq, sq), (wk, sk), (wv, sv)):
        out[...] = matmul(rows, weight[...]).astype(BF16)
    poll()
    seen = block * BLOCK + position((BLOCK, BLOCK), 0) < valid[0]
    for head in range(2):
        lanes = pl.ds(head * HEAD, HEAD)
        read[:, lanes], log_out[0, 0, pl.ds(head, 1), :] = attend(
            sq[:, lanes], [(k[:, lanes], v[:, lanes], seen)]
        )
    total[...] += matmul(read[...], wu[...])

    @pl.when(pair == pl.num_programs(1) - 1)
    def _():
        update = total[...]
        gate = 1.0 / (1.0 + jnp.exp(-row_of(gains, 3)))
        later = gate * state[...] + (1.0 - gate) * update
        update_out[...] = update
        state[...] = later
        last[...] = later.astype(BF16)


def state_forward(valid, s0, gains, weights, update_weight, k, v, exchange):
    rows, width = s0.shape
    blocks, pairs = k.shape[0] // BLOCK, width // PAIR
    columns = pl.BlockSpec((width, PAIR), lambda b, p: (0, p))
    tile = pl.BlockSpec((rows, PAIR), lambda b, p: (b, p))
    band = pl.BlockSpec((rows, width), lambda b, p: (b, 0))

    def stack(kind):
        return jax.ShapeDtypeStruct((blocks * rows, width), kind)

    return run_kernel(
        state_forward_kernel,
        (valid, s0, gains, *weights, update_weight, k, v),
        grid=(blocks, pairs),
        in_specs=[
            pl.BlockSpec(memory_space=pltpu.SMEM), whole((rows, width)), whole(gains.shape),
            columns, columns, columns, pl.BlockSpec((PAIR, width), lambda b, p: (p, 0)),
            pl.BlockSpec((BLOCK, PAIR), lambda b, p: (b, p)),
            pl.BlockSpec((BLOCK, PAIR), lambda b, p: (b, p)),
        ],
        out_specs=[
            pl.BlockSpec((width, rows), lambda b, p: (0, b)), tile, tile, tile, tile,
            pl.BlockSpec((1, 1, 2, rows), lambda b, p: (b, p, 0, 0)),
            band, band, whole((rows, width)),
        ],
        out_shape=[
            jax.ShapeDtypeStruct((width, blocks * rows), BF16),
            stack(BF16), stack(BF16), stack(BF16), stack(BF16),
            jax.ShapeDtypeStruct((blocks, pairs, 2, rows), F32),
            stack(F32), stack(F32), jax.ShapeDtypeStruct((rows, width), BF16),
        ],
        scratch_shapes=[
            pltpu.VMEM((rows, width), F32), pltpu.VMEM((rows, width), BF16),
            pltpu.VMEM((rows, width), F32),
        ],
        name="state_forward",
        exchange=exchange,
        busy=27.7,
        polls=2,
    )


def token_forward_kernel(
    poll, valid, x, gains, q, k, v, sk, sv, wo, mixed, log_out, resid, ynorm, ynorm_t
):
    pair = pl.program_id(0)

    @pl.when(pair == 0)
    def _():
        resid[...] = x[...].astype(F32)

    count = valid[0]
    for head in range(2):
        lanes = pl.ds(head * HEAD, HEAD)
        poll()
        for block in range(q.shape[0] // BLOCK):
            for half in range(BLOCK // TILE):
                rows = pl.ds(block * BLOCK + half * TILE, TILE)
                pieces = []
                for kind, first, size, mask in token_pieces(block, half, count):
                    keys, values = (k, v) if kind == "near" else (sk, sv)
                    there = pl.ds(first, size)
                    pieces.append((keys[there, lanes], values[there, lanes], mask))
                mixed[rows, lanes], log_out[0, pl.ds(head, 1), rows] = attend(
                    q[rows, lanes], pieces
                )
    resid[...] += matmul(mixed[...], wo[...])

    @pl.when(pair == pl.num_programs(0) - 1)
    def _():
        rows = resid[...]
        rounded = (rows * inverse_rms(rows) * row_of(gains, 2)).astype(BF16)
        ynorm[...] = rounded
        ynorm_t[...] = rounded.T


def token_forward(valid, x, gains, q, k, v, sk, sv, wo, exchange):
    rows, width = x.shape
    pairs = width // PAIR
    tile = pl.BlockSpec((rows, PAIR), lambda p: (0, p))
    states = pl.BlockSpec((sk.shape[0], PAIR), lambda p: (0, p))
    return run_kernel(
        token_forward_kernel,
        (valid, x, gains, q, k, v, sk, sv, wo),
        grid=(pairs,),
        in_specs=[
            pl.BlockSpec(memory_space=pltpu.SMEM), whole((rows, width)), whole(gains.shape),
            tile, tile, tile, states, states, pl.BlockSpec((PAIR, width), lambda p: (p, 0)),
        ],
        out_specs=[
            tile, pl.BlockSpec((1, 2, rows), lambda p: (p, 0, 0)),
            whole((rows, width)), whole((rows, width)), whole((width, rows)),
        ],
        out_shape=[
            jax.ShapeDtypeStruct((rows, width), BF16),
            jax.ShapeDtypeStruct((pairs, 2, rows), F32),
            jax.ShapeDtypeStruct((rows, width), F32),
            jax.ShapeDtypeStruct((rows, width), BF16),
            jax.ShapeDtypeStruct((width, rows), BF16),
        ],
        name="token_forward",
        exchange=exchange,
        busy=28.4,
        polls=2,
    )


def feed_forward_kernel(
    first, final, poll, ynorm, ynorm_t, masked, masked_t, total_in, grad_in, up_w, down_w,
    out, grad_out, up_grad, down_grad,
    total, grad_total, sems,
):
    step, last = pl.program_id(0), pl.num_programs(0) - 1
    loads = [pltpu.make_async_copy(total_in, total, sems.at[0])]
    stores = [pltpu.make_async_copy(grad_total, grad_out, sems.at[1])]
    if not first:
        loads.append(pltpu.make_async_copy(grad_in, grad_total, sems.at[1]))
    if not final:
        stores.append(pltpu.make_async_copy(total, out, sems.at[0]))

    poll()

    @pl.when(step == 0)
    def _():
        for copy in loads:
            copy.start()
        if first:
            grad_total[...] = jnp.zeros_like(grad_total)

    up_part, down_part = up_w[0], down_w[0]
    up = matmul(ynorm[...], up_part)
    grad_hidden = matmul(masked[...], down_part)
    square = up * up
    bent = jnp.tanh(GELU_C * (up + GELU_K * square * up))
    hidden = (0.5 * up * (1.0 + bent)).astype(BF16)
    slope = 0.5 * (1.0 + bent) + 0.5 * up * (1.0 - bent * bent) * (
        GELU_C * (1.0 + 3.0 * GELU_K * square)
    )
    grad_up = (grad_hidden * slope).astype(BF16)
    poll()
    down_grad[0] = matmul(masked_t[...], hidden).astype(BF16)
    poll()
    up_grad[0] = matmul(ynorm_t[...], grad_up).astype(BF16)

    @pl.when(step == 0)
    def _():
        for copy in loads:
            copy.wait()

    poll()
    total[...] += matmul_nt(hidden, down_part)
    grad_total[...] += matmul_nt(grad_up, up_part)

    @pl.when(step == last)
    def _():
        for copy in stores:
            copy.start()
        if final:
            out[...] = total[...].astype(BF16)
        for copy in stores:
            copy.wait()


def feed_forward(first, final, rows_in, total, grad, up_w, down_w, exchange, chunk=512):
    rows, width = total.shape
    parts, _, part = up_w.shape
    chunk = min(chunk, part)
    each = part // chunk
    weight = pl.BlockSpec((1, width, chunk), lambda j: (j // each, 0, j % each))
    once = pl.BlockSpec((rows, width), lambda j: (0, 0), pipeline_mode=pl.Buffered(1))
    turned = pl.BlockSpec((width, rows), lambda j: (0, 0), pipeline_mode=pl.Buffered(1))
    anywhere = pl.BlockSpec(memory_space=pl.ANY)
    return run_kernel(
        functools.partial(feed_forward_kernel, first, final),
        (*rows_in, total, grad, up_w, down_w),
        grid=(parts * each,),
        in_specs=[once, turned, once, turned, anywhere, anywhere, weight, weight],
        out_specs=[once if final else anywhere, anywhere, weight, weight],
        out_shape=[
            jax.ShapeDtypeStruct((rows, width), BF16 if final else F32),
            jax.ShapeDtypeStruct((rows, width), F32),
            jax.ShapeDtypeStruct(up_w.shape, BF16),
            jax.ShapeDtypeStruct(down_w.shape, BF16),
        ],
        scratch_shapes=[
            pltpu.VMEM((rows, width), F32), pltpu.VMEM((rows, width), F32),
            pltpu.SemaphoreType.DMA((2,)),
        ],
        name="feed_forward_final" if final else "feed_forward_first",
        exchange=exchange,
        busy=38.0,
        polls=4,
    )


def token_backward_kernel(
    poll, valid, resid, gains, masked, grad_ynorm, normed_t, snormed_t,
    q, k, v, sk, sv, wo, mixed, log_total,
    grad_resid, gain_grad, dq, dk, dv, dsk, dsv, wo_grad, wq_grad, skw_grad, svw_grad,
    rounded, work, other, sems, grad_mixed, near_k, near_v, state_k, state_v,
):
    loads = [
        pltpu.make_async_copy(source, target, sems.at[i])
        for i, (source, target) in enumerate(((resid, work), (grad_ynorm, other), (masked, rounded)))
    ]
    store = pltpu.make_async_copy(work, grad_resid, sems.at[3])

    @pl.when(pl.program_id(0) == 0)
    def _():
        for copy in loads:
            copy.start()

    poll()

    @pl.when(pl.program_id(0) == 0)
    def _():
        for copy in loads:
            copy.wait()
        grad, gain_rows = rms_backward(work[...], row_of(gains, 2), other[...])
        grad = rounded[...].astype(F32) + grad
        work[...] = grad
        rounded[...] = grad.astype(BF16)
        gain_grad[...] = jnp.sum(gain_rows, axis=0, keepdims=True)
        store.start()

    @pl.when(pl.program_id(0) == pl.num_programs(0) - 1)
    def _():
        store.wait()

    grad_rows = rounded[...]
    grad_mixed[...] = matmul_nt(grad_rows, wo[...]).astype(BF16)
    wo_grad[...] = matmul(mixed[...].T, grad_rows).astype(BF16)
    for ref in (near_k, near_v, state_k, state_v):
        ref[...] = jnp.zeros_like(ref)
    count = valid[0]
    for head in range(2):
        lanes = pl.ds(head * HEAD, HEAD)

        def adder(ref, there):
            def add(term):
                ref[there, lanes] += term

            return add

        poll()
        for block in range(q.shape[0] // BLOCK):
            for half in range(BLOCK // TILE):
                rows = pl.ds(block * BLOCK + half * TILE, TILE)
                pieces = []
                for kind, first, size, mask in token_pieces(block, half, count):
                    keys, values = (k, v) if kind == "near" else (sk, sv)
                    sums = (near_k, near_v) if kind == "near" else (state_k, state_v)
                    there = pl.ds(first, size)
                    pieces.append(
                        (keys[there, lanes], values[there, lanes], mask)
                        + tuple(adder(ref, there) for ref in sums)
                    )
                out_grad = grad_mixed[rows, lanes]
                dq[rows, lanes] = attend_backward(
                    q[rows, lanes],
                    log_total[0, pl.ds(head, 1), rows],
                    out_grad,
                    centre_of(out_grad, mixed[rows, lanes]),
                    pieces,
                ).astype(BF16)
    dk[...] = near_k[...]
    dv[...] = near_v[...]
    dsk[...] = state_k[...].astype(BF16)
    dsv[...] = state_v[...].astype(BF16)
    wq_grad[...] = matmul(normed_t[...], dq[...]).astype(BF16)
    skw_grad[...] = matmul(snormed_t[...], dsk[...]).astype(BF16)
    svw_grad[...] = matmul(snormed_t[...], dsv[...]).astype(BF16)


def token_backward(
    valid, resid, gains, masked, grad_ynorm, normed_t, snormed_t,
    q, k, v, sk, sv, wo, mixed, log_total, exchange,
):
    rows, width = resid.shape
    anywhere = pl.BlockSpec(memory_space=pl.ANY)
    turned = pl.BlockSpec((width, rows), lambda p: (0, 0), pipeline_mode=pl.Buffered(1))
    turned_state = pl.BlockSpec(snormed_t.shape, lambda p: (0, 0), pipeline_mode=pl.Buffered(1))
    columns = pl.BlockSpec((width, PAIR), lambda p: (0, p))
    once = pl.BlockSpec((rows, width), lambda p: (0, 0), pipeline_mode=pl.Buffered(1))
    pairs = width // PAIR
    tile = pl.BlockSpec((rows, PAIR), lambda p: (0, p))
    states = pl.BlockSpec((sk.shape[0], PAIR), lambda p: (0, p))
    band = pl.BlockSpec((PAIR, width), lambda p: (p, 0))
    return run_kernel(
        token_backward_kernel,
        (
            valid, resid, gains, masked, grad_ynorm, normed_t, snormed_t,
            q, k, v, sk, sv, wo, mixed, log_total,
        ),
        grid=(pairs,),
        in_specs=[
            pl.BlockSpec(memory_space=pltpu.SMEM), anywhere, whole(gains.shape), anywhere, anywhere,
            turned, turned_state, tile, tile, tile, states, states, band, tile,
            pl.BlockSpec((1, 2, rows), lambda p: (p, 0, 0)),
        ],
        out_specs=[anywhere, whole((1, width)), tile, tile, tile, states, states, band]
        + [columns] * 3,
        out_shape=[
            jax.ShapeDtypeStruct((rows, width), F32),
            jax.ShapeDtypeStruct((1, width), F32),
            jax.ShapeDtypeStruct((rows, width), BF16),
            jax.ShapeDtypeStruct((rows, width), F32),
            jax.ShapeDtypeStruct((rows, width), F32),
            jax.ShapeDtypeStruct(sk.shape, BF16),
            jax.ShapeDtypeStruct(sk.shape, BF16),
        ]
        + [jax.ShapeDtypeStruct((width, width), BF16)] * 4,
        scratch_shapes=[
            pltpu.VMEM((rows, width), BF16), pltpu.VMEM((rows, width), F32),
            pltpu.VMEM((rows, width), F32), pltpu.SemaphoreType.DMA((4,)),
            pltpu.VMEM((rows, PAIR), BF16), pltpu.VMEM((rows, PAIR), F32),
            pltpu.VMEM((rows, PAIR), F32), pltpu.VMEM((sk.shape[0], PAIR), F32),
            pltpu.VMEM((sk.shape[0], PAIR), F32),
        ],
        name="token_backward",
        exchange=exchange,
        busy=55.0,
        polls=3,
    )


def state_backward_kernel(
    poll, valid, cot, gains, wq, wk, wv, wu, states, updates,
    sq, k, v, read, log_total, near_k, near_v, dsk, dsv, read_last, normed_t, snormed_t,
    dk, dv, grad_state, gain_grad, bias_grad, wk_grad, wv_grad, sqw_grad, wu_grad,
    later, dz, total, grad_read, sum_k, sum_v, dsq, kept_dz, kept,
):
    step, pair = pl.program_id(0), pl.program_id(1)
    block = pl.num_programs(0) - 1 - step
    gate = 1.0 / (1.0 + jnp.exp(-row_of(gains, 3)))

    @pl.when((step == 0) & (pair == 0))
    def _():
        later[...] = cot[...].astype(F32)
        gain_grad[...] = jnp.zeros_like(gain_grad)
        bias_grad[...] = jnp.zeros_like(bias_grad)

    @pl.when(pair == 0)
    def _():
        grad = later[...]
        rounded = (grad * (1.0 - gate)).astype(BF16)
        dz[...] = rounded

        @pl.when(step == 0)
        def _():
            kept_dz[...] = rounded

        bias_grad[...] += (
            jnp.sum(grad * (states[...] - updates[...]), axis=0, keepdims=True) * gate * (1.0 - gate)
        )
        total[...] = jnp.zeros_like(total)

    poll()
    grad_read[...] = matmul_nt(dz[...], wu[...]).astype(BF16)
    seen = block * BLOCK + position((BLOCK, BLOCK), 0) < valid[0]
    sum_k[...] = near_k[...]
    sum_v[...] = near_v[...]
    for head in range(2):
        lanes = pl.ds(head * HEAD, HEAD)

        def adder(ref):
            def add(term):
                ref[:, lanes] += term

            return add

        out_grad = grad_read[:, lanes]
        dsq[:, lanes] = attend_backward(
            sq[:, lanes],
            log_total[0, 0, pl.ds(head, 1), :],
            out_grad,
            centre_of(out_grad, read[:, lanes]),
            [(k[:, lanes], v[:, lanes], seen, adder(sum_k), adder(sum_v))],
        ).astype(BF16)
    poll()
    dk[...] = sum_k[...].astype(BF16)
    dv[...] = sum_v[...].astype(BF16)
    total[...] += (
        matmul_nt(dsq[...], wq[...]) + matmul_nt(dsk[...], wk[...]) + matmul_nt(dsv[...], wv[...])
    )

    @pl.when(step == 0)
    def _():
        for i, ref in enumerate((dk, dv, dsq)):
            kept[i, pair] = ref[...]

    @pl.when(step == 1)
    def _():
        for i, (left, ref, out) in enumerate(
            ((normed_t, dk, wk_grad), (normed_t, dv, wv_grad), (snormed_t, dsq, sqw_grad))
        ):
            half = left.shape[1] // 2
            out[...] = (
                matmul(left[:, :half], ref[...]) + matmul(left[:, half:], kept[i, pair])
            ).astype(BF16)
        wu_grad[...] = (
            matmul(read[...].T, dz[...]) + matmul(read_last[...].T, kept_dz[...])
        ).astype(BF16)

    @pl.when(pair == pl.num_programs(1) - 1)
    def _():
        grad, gain_rows = rms_backward(states[...], row_of(gains, 1), total[...])
        grad = later[...] * gate + grad
        later[...] = grad
        grad_state[...] = grad
        gain_grad[...] += jnp.sum(gain_rows, axis=0, keepdims=True)


def state_backward(
    valid, cot, gains, weights, update_weight, states, updates,
    sq, k, v, read, log_total, near_k, near_v, dsk, dsv, normed_t, snormed_t, exchange,
):
    rows, width = cot.shape
    blocks, pairs = k.shape[0] // BLOCK, width // PAIR
    columns = pl.BlockSpec((width, PAIR), lambda s, p: (0, p))
    tile = pl.BlockSpec((rows, PAIR), lambda s, p: (blocks - 1 - s, p))
    token = pl.BlockSpec((BLOCK, PAIR), lambda s, p: (blocks - 1 - s, p))
    band = pl.BlockSpec((rows, width), lambda s, p: (blocks - 1 - s, 0))
    small = whole((1, width))
    return run_kernel(
        state_backward_kernel,
        (
            valid, cot, gains, *weights, update_weight, states, updates,
            sq, k, v, read, log_total, near_k, near_v, dsk, dsv, read, normed_t, snormed_t,
        ),
        grid=(blocks, pairs),
        in_specs=[
            pl.BlockSpec(memory_space=pltpu.SMEM), whole((rows, width)), whole(gains.shape),
            columns, columns, columns, pl.BlockSpec((PAIR, width), lambda s, p: (p, 0)),
            band, band, tile, token, token, tile,
            pl.BlockSpec((1, 1, 2, rows), lambda s, p: (blocks - 1 - s, p, 0, 0)),
            token, token, tile, tile,
            pl.BlockSpec((rows, PAIR), lambda s, p: (blocks - 1, p)),
            pl.BlockSpec(normed_t.shape, lambda s, p: (0, 0), pipeline_mode=pl.Buffered(1)),
            pl.BlockSpec(snormed_t.shape, lambda s, p: (0, 0), pipeline_mode=pl.Buffered(1)),
        ],
        out_specs=[token, token, whole((rows, width)), small, small]
        + [pl.BlockSpec((width, PAIR), lambda s, p: (0, p * s))] * 3
        + [pl.BlockSpec((PAIR, width), lambda s, p: (p * s, 0))],
        out_shape=[
            jax.ShapeDtypeStruct(k.shape, BF16),
            jax.ShapeDtypeStruct(k.shape, BF16),
            jax.ShapeDtypeStruct((rows, width), F32),
            jax.ShapeDtypeStruct((1, width), F32),
            jax.ShapeDtypeStruct((1, width), F32),
        ]
        + [jax.ShapeDtypeStruct((width, width), BF16)] * 4,
        scratch_shapes=[
            pltpu.VMEM((rows, width), F32), pltpu.VMEM((rows, width), BF16),
            pltpu.VMEM((rows, width), F32), pltpu.VMEM((rows, PAIR), BF16),
            pltpu.VMEM((BLOCK, PAIR), F32), pltpu.VMEM((BLOCK, PAIR), F32),
            pltpu.VMEM((rows, PAIR), BF16), pltpu.VMEM((rows, width), BF16),
            pltpu.VMEM((3, pairs, BLOCK, PAIR), BF16),
        ],
        name="state_backward",
        exchange=exchange,
        busy=51.0,
        polls=2,
    )


def token_grad_kernel(
    plan, poll, x, gains, grad_resid, dq, dk, dv, wq, wk, wv, *refs
):
    *others, grad_x, gain_grad = refs
    plan.rows = [gain_grad] + others
    poll()

    @pl.when(pl.program_id(0) == 0)
    def _():
        gain_grad[...] = jnp.zeros_like(gain_grad)

    grad_normed = matmul_nt(dq[...], wq[...]) + matmul_nt(dk[...], wk[...])
    poll()
    grad_normed = grad_normed + matmul_nt(dv[...], wv[...])
    grad, gain_rows = rms_backward(x[...].astype(F32), row_of(gains, 0), grad_normed)
    grad_x[...] = grad_resid[...] + grad
    gain_grad[...] += jnp.sum(gain_rows, axis=0, keepdims=True)


def token_grad(x, gains, grad_resid, grads, weights, other_rows, plan, exchange):
    rows, width = x.shape
    band = pl.BlockSpec((TILE, width), lambda i: (i, 0))
    weight = pl.BlockSpec((width, width), lambda i: (0, 0), pipeline_mode=pl.Buffered(1))
    return run_kernel(
        functools.partial(token_grad_kernel, plan),
        (x, gains, grad_resid, *grads, *weights, *other_rows),
        grid=(rows // TILE,),
        in_specs=[band, whole(gains.shape), band, band, band, band, weight, weight, weight]
        + [whole((1, width))] * len(other_rows),
        out_specs=[band, whole((1, width))],
        out_shape=[
            jax.ShapeDtypeStruct((rows, width), F32), jax.ShapeDtypeStruct((1, width), F32)
        ],
        name="token_grad",
        exchange=exchange,
        busy=13.8,
        polls=2,
    )


def cut(width, pieces):
    return [(i * width // pieces, width // pieces) for i in range(pieces)]


def plan_gather(sizes, small, square, forward):
    width, half = square[0].shape[1], forward[0].shape[1] // 2
    units = [(0, "zx", False, (0, small.shape[1]), 0, 1)]
    for group, (starts, routes, stride) in zip(((1, 2, 3), (4, 5, 6), (7,), (8,)), GATHER_SQUARE):
        pieces = cut(width, len(starts))
        can_share = pieces[0][1] // sizes["m"] % 128 == 0
        for n, (columns, start) in enumerate(zip(pieces, starts)):
            for j, i in enumerate(group):
                order = routes[(n * len(group) + j) % len(routes)]
                shared = can_share and "m" in order
                units.append((i, order if shared else "zx", shared, columns, start, stride))
    for i, (starts, stride) in enumerate(GATHER_FORWARD):
        for n, columns in enumerate(cut(half, min(len(starts), half // 128))):
            order = ("zxm", "zmx")[n % 2]
            units.append((9 + i, order, False, columns, starts[n], stride))
    spans = [(0, array.shape[1]) for array in [small] + square]
    spans += [(first, half) for first in (0, half) for _ in forward]
    return Gather(sizes, [small] + square + forward * 2, spans, units)


def forward_units(arrays, start, table):
    units = []
    for i, (array, pieces) in enumerate(zip(arrays, table)):
        columns = cut(array.shape[-1], min(len(pieces), array.shape[-1] // 128))
        units += [
            (i, order, False, there, start + offset, stride)
            for there, (order, offset, stride) in zip(columns, pieces)
        ]
    return units


def square_units(sizes, arrays, start, table):
    units = []
    for columns, pieces in zip(cut(arrays[0].shape[-1], len(table)), table):
        can_share = columns[1] // sizes["m"] % 128 == 0
        for i, (order, offset, stride) in enumerate(pieces):
            shared = can_share and "m" in order
            units.append(
                (i, order if shared else "xz", shared, columns, start + offset, stride)
            )
    return units


def finish_kernel(kept, counts, *refs):
    refs = list(refs)
    sources = [refs.pop(0) for _ in range(kept)]
    parts = [[refs.pop(0) for _ in range(n)] for n in counts]
    targets = [refs.pop(0) for _ in range(kept)]
    stages, sems = refs[-1 - kept : -1], refs[-1]
    loads, stores = [], []
    for i, (source, stage, target) in enumerate(zip(sources, stages, targets)):
        loads.append(pltpu.make_async_copy(source, stage, sems.at[i]))
        stores.append(pltpu.make_async_copy(stage, target, sems.at[kept + i]))
    for load in loads:
        load.start()
    for load, store in zip(loads, stores):
        load.wait()
        store.start()
    for group, out in zip(parts, refs):
        first = 0
        for part in group:
            out[:, pl.ds(first, part.shape[1])] = part[...]
            first += part.shape[1]
    for store in stores:
        store.wait()


def finish(arrays, groups):
    anywhere, inside = pl.BlockSpec(memory_space=pl.ANY), pl.BlockSpec(memory_space=pltpu.VMEM)
    shapes = [
        jax.ShapeDtypeStruct((g[0].shape[0], sum(p.shape[1] for p in g)), F32) for g in groups
    ]
    parts = [part for g in groups for part in g]
    outs = pl.pallas_call(
        functools.partial(finish_kernel, len(arrays), [len(g) for g in groups]),
        in_specs=[anywhere] * len(arrays) + [inside] * len(parts),
        out_specs=[anywhere] * len(arrays) + [inside] * len(groups),
        out_shape=[jax.ShapeDtypeStruct(a.shape, a.dtype) for a in arrays] + shapes,
        scratch_shapes=[pltpu.VMEM(a.shape, a.dtype) for a in arrays]
        + [pltpu.SemaphoreType.DMA((2 * len(arrays),))],
        compiler_params=pltpu.CompilerParams(vmem_limit_bytes=VMEM_LIMIT),
        name="finish",
    )(*arrays, *parts)
    return outs[: len(arrays)], outs[len(arrays) :]


def shards(
    mlp_size,
    tokens,
    initial_state,
    valid,
    token_query_weight,
    token_key_weight,
    token_value_weight,
    token_output_weight,
    state_query_weight,
    state_key_weight,
    state_value_weight,
    state_update_weight,
    up_projection_weight,
    down_projection_weight,
    token_norm_gain,
    state_norm_gain,
    feedforward_norm_gain,
    state_gate_bias,
    output_cotangent,
    final_state_cotangent,
):
    rows = token_query_weight.shape[0]
    width = tokens.shape[2]
    seg_size = width // rows
    sizes = {"z": seg_size // 4, "x": 2, "c": 2, "m": mlp_size}
    half = up_projection_weight.shape[1] // 2
    small = jnp.concatenate(
        [token_norm_gain, state_norm_gain, feedforward_norm_gain, state_gate_bias]
    ).reshape(-1, 128)
    small = jnp.pad(small, ((0, 16 - small.shape[0]), (0, 0)))
    square = [
        token_query_weight,
        token_key_weight,
        token_value_weight,
        state_query_weight,
        state_key_weight,
        state_value_weight,
        state_update_weight,
        token_output_weight,
    ]
    forward = [up_projection_weight, down_projection_weight]
    plan = plan_gather(sizes, small, square, forward)
    x, s0, cot = tokens[0], initial_state[0], output_cotangent[0]

    def full(*names):
        return [plan.targets[n].reshape(width, width) for n in names]

    def forward_full(*names):
        return [plan.targets[n].reshape(mlp_size, width, half) for n in names]

    exchange_alone(plan.until(plan.ready((0, 1, 2, 3)), 1), "gather_first")
    gains = plan.targets[0].reshape(seg_size, -1)[:, : 4 * rows].reshape(seg_size, 4, rows)
    gains = gains.transpose(1, 0, 2).reshape(4, width).astype(F32)
    token_weights = full(1, 2, 3)
    normed_t, masked, masked_t, q, k, v = project(
        valid, x, gains, cot, token_weights, plan.until(plan.ready((4, 5, 6, 7)), 2)
    )
    state_weights, (wu,) = full(4, 5, 6), full(7)
    ready = plan.ready((9, 10))
    middle = max(plan.ready((8,)), GATHER_MIDDLE)
    snormed_t, sq, sk, sv, read, read_log, updates, states, last = state_forward(
        valid, s0, gains, state_weights, wu, k, v, plan.until(middle, 3)
    )
    (wo,) = full(8)
    mixed, token_log, resid, *ynorms = token_forward(
        valid, x, gains, q, k, v, sk, sv, wo, plan.until(ready, 4)
    )
    total, grad_total, *first_grads = feed_forward(
        True, False, (*ynorms, masked, masked_t), resid, resid, *forward_full(9, 10),
        plan.until(plan.ready((11, 12)), 5),
    )

    def parted(grads):
        shape = (seg_size // 4, 2, 2, rows)
        return [
            g.reshape((mlp_size,) + shape + (half,)) if g.ndim == 3 else g.reshape(shape + (width,))
            for g in grads
        ]

    sums = Scatter(sizes)
    rounds = iter(SCATTER_ROUNDS)

    def next_rounds(collective_id):
        return sums.until(sums.round + next(rounds), collective_id)

    units_first = sums.add(parted(first_grads), forward_units(first_grads, 0, SCATTER_FIRST))
    out, grad_total, *last_grads = feed_forward(
        False, True, (*ynorms, masked, masked_t), total, grad_total, *forward_full(11, 12),
        next_rounds(6),
    )
    units_last = sums.add(parted(last_grads), forward_units(last_grads, sums.round, SCATTER_LAST))
    grad_resid, mlp_gain_grad, dq, near_k, near_v, dsk, dsv, *early_grads = token_backward(
        valid, resid, gains, masked, grad_total, normed_t, snormed_t,
        q, k, v, sk, sv, wo, mixed, token_log, next_rounds(7),
    )
    units_early = sums.add(
        parted(early_grads), square_units(sizes, early_grads, sums.round, SCATTER_EARLY)
    )
    dk, dv, grad_state, state_gain_grad, bias_grad, *late_grads = state_backward(
        valid, final_state_cotangent[0], gains, state_weights, wu,
        states, updates, sq, k, v, read, read_log, near_k, near_v, dsk, dsv, normed_t, snormed_t,
        next_rounds(8),
    )
    units_late = sums.add(
        parted(late_grads), square_units(sizes, late_grads, sums.round, SCATTER_LATE)
    )
    small_unit = sums.add_small(mlp_gain_grad)
    grad_tokens, _ = token_grad(
        x, gains, grad_resid, [dq, dk, dv], token_weights,
        [state_gain_grad, mlp_gain_grad, bias_grad], sums, sums.until(sums.all(), 9),
    )
    small_sum = small_unit.result[:4].reshape(4, seg_size, rows)
    small_sum = lax.dynamic_index_in_dim(small_sum, lax.axis_index("seg"), 1, keepdims=False)

    def group(units, i, count):
        return [unit.result for unit in units[i::count]]

    def forward_group(i):
        return [
            unit.result
            for units in (units_first, units_last)
            for unit in units[i * len(units) // 2 : (i + 1) * len(units) // 2]
        ]

    own_results, weight_sums = finish(
        [last, out, grad_state, grad_tokens],
        [
            group(units_early, 1, 4),
            group(units_late, 0, 4),
            group(units_late, 1, 4),
            group(units_early, 0, 4),
            group(units_late, 2, 4),
            group(units_early, 2, 4),
            group(units_early, 3, 4),
            group(units_late, 3, 4),
            forward_group(0),
            forward_group(1),
        ],
    )
    return (
        *[own_results[i][None] for i in (1, 0, 3, 2)],
        *weight_sums,
        *[small_sum[i] for i in range(4)],
    )


def solution(mesh):
    own = P(("seg", "mlp"), None, None)
    square, forward, small = P("seg", None), P("seg", "mlp"), P("seg")
    return jax.shard_map(
        functools.partial(shards, mesh.shape["mlp"]),
        mesh=mesh,
        in_specs=(own, own, P(("seg", "mlp")))
        + (square,) * 8
        + (forward,) * 2
        + (small,) * 4
        + (own, own),
        out_specs=(own,) * 4 + (square,) * 8 + (forward,) * 2 + (small,) * 4,
        check_vma=False,
    )
```
